128 devices in a mesh: rows: 4 (over y_lo, core), img: 32 (over x, z, y_hi).
Axes of the slice: x: 4, y: 4 (y_hi: 2, y_lo: 2; y = y_hi * 2 + y_lo), z: 4, core: 2. Of those that a mesh axis runs over, the one named last changes fastest.
Arguments:
- features: bfloat16 [32, 8, 72, 2048], P('img', 'rows')
- image_size: int32 [32, 2], replicated, may hold values from 4 to 72, as said below
- reduce_weight: bfloat16 [2048, 512], P('img'), may hold values from -0.125 to 0.125
- dilated_weight: bfloat16 [512, 4608], P('img'), may hold values from -0.09375 to 0.09375
- expand_weight: bfloat16 [512, 2048], P('img'), may hold values from -0.25 to 0.25
- head_weight: bfloat16 [4, 2048, 4608], P(None, 'img'), may hold values from -0.046875 to 0.046875
- message_weight: bfloat16 [4, 512, 4608], P(None, 'img'), may hold values from -0.09375 to 0.09375
- gate_weight: bfloat16 [4, 512, 512], P(None, 'img'), may hold values from -0.25 to 0.25
- bottleneck_gain: float32 [2, 512], replicated, may hold values from 0.25 to 1.75
- bottleneck_bias: float32 [2, 512], replicated, may hold values from -2.5 to 2.5
- expand_gain: float32 [2048], replicated, may hold values from 0.25 to 1.75
- expand_bias: float32 [2048], replicated, may hold values from -2.5 to 2.5
- head_gain: float32 [4, 512], replicated, may hold values from 0.25 to 1.75
- head_bias: float32 [4, 512], replicated, may hold values from -2.5 to 2.5
- depth_cotangent: bfloat16 [32, 8, 72, 512], P('img', 'rows'), may hold values from -6 to 6
- seg_cotangent: bfloat16 [32, 8, 72, 512], P('img', 'rows'), may hold values from -6 to 6
Outputs:
- depth_stream: float32 [32, 8, 72, 512], P('img', 'rows')
- seg_stream: float32 [32, 8, 72, 512], P('img', 'rows')
- input_grad: float32 [32, 8, 72, 2048], P('img', 'rows')
- reduce_grad: float32 [2048, 512], P('img')
- dilated_grad: float32 [512, 4608], P('img')
- expand_grad: float32 [512, 2048], P('img')
- head_grad: float32 [4, 2048, 4608], P(None, 'img')
- message_grad: float32 [4, 512, 4608], P(None, 'img')
- gate_grad: float32 [4, 512, 512], P(None, 'img')
- bottleneck_gain_grad: float32 [2, 512], replicated
- bottleneck_bias_grad: float32 [2, 512], replicated
- expand_gain_grad: float32 [2048], replicated
- expand_bias_grad: float32 [2048], replicated
- head_gain_grad: float32 [4, 512], replicated
- head_bias_grad: float32 [4, 512], replicated
The draws below stay inside these ranges and needn't reach their ends.
Inputs may be any that keep to these rules, and one draw needn't show every extreme that they name: `image_size`: each image's map is either full-size, 8 rows by 72 columns, or half-size, 4 rows by 36 columns; image 0 is full-size and image 1 half-size.
All inputs are finite; a program needn't handle non-finite values.
Results may differ from the reference program's by a relative error of at most 0.028.
Values may be sent and summed in bfloat16 or wider, within the bound.
No kernel may reach another device: no remote copies, remote signals or barrier semaphores. Data moves between devices by JAX's collectives and lax.ppermute only.
A program may use at most 384 MiB of HBM per device.

```python
import jax
import jax.numpy as jnp
from jax import lax

D = 2048
MID = 512
HMAX = 8
WMAX = 72
IMAGES = 32


def draw_features(key, part):
    key = jax.random.fold_in(key, 11)
    first_key, second_key = jax.random.split(key)
    shape_all = (IMAGES, HMAX, WMAX, D)
    spread = 1.0 + 2.0 * jnp.arange(IMAGES, dtype=jnp.float32)[:, None, None, None] / max(IMAGES - 1, 1)
    offset = 0.5 * jax.random.normal(second_key, (D,), jnp.float32)
    base_draw = jax.random.normal(first_key, shape_all, jnp.float32)
    return (base_draw * spread + offset).astype(jnp.bfloat16)


def draw_image_size(key, part):
    key = jax.random.fold_in(key, 23)
    halves = jax.random.randint(key, (IMAGES,), 1, 3)
    halves = halves.at[0].set(2).at[1].set(1)
    return jnp.stack([HMAX * halves // 2, WMAX * halves // 2], axis=1).astype(jnp.int32)


def steps_of(rng, extent, cuts, least, largest):
    gain, own = 1.0, jax.random.fold_in(rng, 6)
    for axis_at, shards_of in cuts:
        steps = jnp.exp(jax.random.uniform(jax.random.fold_in(own, axis_at), (shards_of,), jnp.float32, least / len(cuts), largest / len(cuts)))
        gain = gain * jnp.repeat(steps, extent[axis_at] // shards_of).reshape([-1 if axis == axis_at else 1 for axis in range(len(extent))])
    return gain


def gaussian(rng, extent, width, limit, shards=(), kind=jnp.bfloat16):
    level = steps_of(rng, extent, shards, -0.22, 0.18) if shards else 1.0
    entries = jax.random.normal(rng, extent, jnp.float32) * width * level
    return jnp.minimum(jnp.maximum(entries, -limit), limit).astype(kind)


def setup_inputs(seed: int = 0) -> dict:
    key_list = jax.random.split(jax.random.key(seed), 17)
    return {
        "features": draw_features(jax.random.fold_in(key_list[16], 71), 0),
        "image_size": draw_image_size(jax.random.fold_in(key_list[16], 71), 0),
        "reduce_weight": gaussian(key_list[2], (D, MID), D ** -0.5, 0.125, ((0, 32),)),
        "dilated_weight": gaussian(key_list[3], (MID, 9 * MID), (9 * MID) ** -0.5, 0.09375, ((0, 32),)),
        "expand_weight": gaussian(key_list[4], (MID, D), MID ** -0.5, 0.25, ((0, 32),)),
        "head_weight": gaussian(key_list[5], (4, D, 9 * MID), (9 * D) ** -0.5, 0.046875, ((1, 32),)),
        "message_weight": gaussian(key_list[6], (4, MID, 9 * MID), (9 * MID) ** -0.5, 0.09375, ((1, 32),)),
        "gate_weight": gaussian(key_list[7], (4, MID, MID), MID ** -0.5, 0.25, ((1, 32),)),
        "bottleneck_gain": jnp.clip(1.0 + 0.15 * jax.random.normal(key_list[8], (2, MID), jnp.float32), 0.25, 1.75),
        "bottleneck_bias": gaussian(key_list[9], (2, MID), 0.5, 2.5, (), jnp.float32),
        "expand_gain": jnp.clip(1.0 + 0.15 * jax.random.normal(key_list[10], (D,), jnp.float32), 0.25, 1.75),
        "expand_bias": gaussian(key_list[11], (D,), 0.5, 2.5, (), jnp.float32),
        "head_gain": jnp.clip(1.0 + 0.15 * jax.random.normal(key_list[12], (4, MID), jnp.float32), 0.25, 1.75),
        "head_bias": gaussian(key_list[13], (4, MID), 0.5, 2.5, (), jnp.float32),
        "depth_cotangent": gaussian(key_list[14], (IMAGES, HMAX, WMAX, MID), 1.0, 6.0, ((0, 32), (1, 4))),
        "seg_cotangent": gaussian(key_list[15], (IMAGES, HMAX, WMAX, MID), 1.0, 6.0, ((0, 32), (1, 4))),
    }


EPS = 1e-05
HIGH = lax.Precision.HIGHEST

@jax.custom_vjp
def low(v):
    return lax.optimization_barrier(v.astype(jnp.bfloat16)).astype(jnp.float32)

@jax.custom_vjp
def low_back(v):
    return v

def low_keep(v):
    return (low(v), None)

def low_pass(kept, grad):
    return (grad,)

def back_keep(v):
    return (v, None)

def back_low(kept, grad):
    return (low(grad),)
low.defvjp(low_keep, low_pass)
low_back.defvjp(back_keep, back_low)

def pad_both(tensor, dilation):
    margins = [(0, 0)] * (tensor.ndim - 3) + [(dilation, dilation), (dilation, dilation), (0, 0)]
    return jnp.pad(tensor, margins)

def conv_taps(tensor, weight, dilation, pattern):
    padded = pad_both(tensor, dilation)
    height = tensor.shape[-3]
    across = tensor.shape[-2]
    out_width = weight.shape[-1] // 9
    summed = None
    for tap_row in range(3):
        for tap_col in range(3):
            tap_index = tap_row * 3 + tap_col
            window = padded[..., tap_row * dilation:tap_row * dilation + height, tap_col * dilation:tap_col * dilation + across, :]
            product = jnp.einsum(pattern, window, weight[..., tap_index * out_width:(tap_index + 1) * out_width], precision=HIGH)
            summed = product if summed is None else summed + product
    return summed

def normalize(tensor, inside, gains_in, shift_bias, pixel_count):
    pixel_axes = (-4, -3, -2)
    average = lax.optimization_barrier(jnp.sum(tensor * inside, axis=pixel_axes, keepdims=True)) / pixel_count
    seconds = lax.optimization_barrier(jnp.sum(tensor * tensor * inside, axis=pixel_axes, keepdims=True)) / pixel_count
    inverse = lax.rsqrt(seconds - average * average + EPS)
    return gains_in * ((tensor - average) * inverse) + shift_bias

def reference(features, image_size, reduce_weight, dilated_weight, expand_weight, head_weight, message_weight, gate_weight, bottleneck_gain, bottleneck_bias, expand_gain, expand_bias, head_gain, head_bias, depth_cotangent, seg_cotangent):
    heights = image_size[:, 0]
    widths_in = image_size[:, 1]
    row_ids = jnp.arange(HMAX, dtype=jnp.int32)
    col_ids = jnp.arange(WMAX, dtype=jnp.int32)
    valid = (row_ids[None, :, None] < heights[:, None, None]) & (col_ids[None, None, :] < widths_in[:, None, None])
    inside = valid.astype(jnp.float32)[..., None]
    pixel_count = jnp.sum(heights.astype(jnp.float32) * widths_in.astype(jnp.float32))

    def forward(base, whole_reduce, whole_dilated, whole_expand, whole_head, whole_message, whole_gate, bottle_gain, bottle_bias, wide_gain, wide_bias, task_gain, task_bias):
        base_in = base * inside
        pre_one = low_back(jnp.einsum('irwc,cm->irwm', base_in, whole_reduce, precision=HIGH))
        act_one = low(jax.nn.gelu(normalize(pre_one, inside, bottle_gain[0], bottle_bias[0], pixel_count)) * inside)
        pre_two = low_back(conv_taps(act_one, whole_dilated, 2, 'irwc,co->irwo'))
        act_two = low(jax.nn.gelu(normalize(pre_two, inside, bottle_gain[1], bottle_bias[1], pixel_count)) * inside)
        pre_three = low_back(jnp.einsum('irwm,mc->irwc', act_two, whole_expand, precision=HIGH))
        joined = normalize(pre_three, inside, wide_gain, wide_bias, pixel_count) + base_in
        trunk = low(jax.nn.gelu(joined) * inside)
        pre_head = low_back(conv_taps(trunk, whole_head, 1, 'irwc,kco->kirwo'))
        task = low(jax.nn.gelu(normalize(pre_head, inside, task_gain[:, None, None, None, :], task_bias[:, None, None, None, :], pixel_count)) * inside)
        message = low_back(conv_taps(task, whole_message, 1, 'kirwc,kco->kirwo'))
        gate = jax.nn.sigmoid(low_back(jnp.einsum('kirwc,kcd->kirwd', task, whole_gate, precision=HIGH)))
        gated_msg = gate * message
        depth_out = (task[0] + gated_msg[1] + gated_msg[2] + gated_msg[3]) * inside
        seg_out = (task[1] + gated_msg[0] + gated_msg[2] + gated_msg[3]) * inside
        return (depth_out, seg_out)
    outputs, pullback = jax.vjp(forward, features.astype(jnp.float32), reduce_weight.astype(jnp.float32), dilated_weight.astype(jnp.float32), expand_weight.astype(jnp.float32), head_weight.astype(jnp.float32), message_weight.astype(jnp.float32), gate_weight.astype(jnp.float32), bottleneck_gain, bottleneck_bias, expand_gain, expand_bias, head_gain, head_bias)
    grads = pullback((depth_cotangent.astype(jnp.float32), seg_cotangent.astype(jnp.float32)))
    return (outputs[0], outputs[1], grads[0], grads[1], grads[2], grads[3], grads[4], grads[5], grads[6], grads[7], grads[8], grads[9], grads[10], grads[11], grads[12])
```

```python
import functools

import jax
import jax.numpy as jnp
from jax import lax
from jax.experimental import pallas as pl
from jax.experimental.pallas import tpu as pltpu
from jax.sharding import Mesh, PartitionSpec as P

EPS = 1e-05
PITCH = 80
F32 = jnp.float32
BF16 = jnp.bfloat16

FINE = ("ylo", "core", "x", "z", "yhi")
ROWS = ("ylo", "core")
IMG = ("x", "z", "yhi")
RING = ("ylo", "yhi")
GROUP = ("ylo", "core", "yhi")
POOL = ("x", "z", "core")


def swap(value, axis, flip):
    count = lax.axis_size(axis)
    return lax.ppermute(value, axis, [(i, i ^ flip) for i in range(count)])


def over_core(value):
    return swap(value, "core", 1)


def over_y(value, flip):
    return swap(value, RING, {1: 2, 2: 1, 3: 3}[flip])


def total(value, everywhere):
    value = value + over_core(value)
    if everywhere:
        for flip in (1, 3):
            value = value + over_y(value, flip)
    for axis in ("x", "z"):
        for flip in (1, 3):
            value = value + swap(value, axis, flip)
    return value


def in_order(mine, other, bit):
    first = bit == 0
    return jnp.where(first, mine, other), jnp.where(first, other, mine)


def gather_rows(value, ylo, core):
    pair = jnp.concatenate(in_order(value, over_core(value), core))
    return jnp.concatenate(in_order(pair, over_y(pair, 1), ylo))


def at_flip(pieces, flip):
    return jnp.where(
        flip < 2,
        jnp.where(flip == 0, pieces[0], pieces[1]),
        jnp.where(flip == 2, pieces[2], pieces[3]),
    )


def to_heads(value, y, core):
    half = value.shape[0] // 2
    near, far = over_y(value, 1), over_y(value, 3)
    across = jnp.concatenate([over_y(far[:half], 1), over_y(near[half:], 3)])
    pieces = (value, near, across, far)
    keep = [at_flip(pieces, y ^ (2 * core + low)) for low in (0, 1)]
    give = [at_flip(pieces, y ^ (2 * (1 - core) + low)) for low in (0, 1)]
    got = over_core(jnp.concatenate(give))
    got = (got[: value.shape[0]], got[value.shape[0] :])
    strips = []
    for low in (0, 1):
        strips += in_order(keep[low], got[low], core)
    return jnp.concatenate(strips)


def from_heads(value, y, core):
    rows = value.shape[0] // 4
    strip = [value[i * rows : (i + 1) * rows] for i in range(4)]
    own = [jnp.where(core == 0, strip[2 * low], strip[2 * low + 1]) for low in (0, 1)]
    other = [jnp.where(core == 0, strip[2 * low + 1], strip[2 * low]) for low in (0, 1)]
    got = over_core(jnp.concatenate(other).astype(BF16))
    got = [got[:rows], got[rows:]]
    first = [jnp.where(core == 0, own[low].astype(BF16), got[low]) for low in (0, 1)]
    second = [jnp.where(core == 0, got[low], own[low].astype(BF16)) for low in (0, 1)]
    pieces = first + second
    mine, near, across, far = (at_flip(pieces, y ^ flip) for flip in range(4))
    half = rows // 2
    from_near = over_y(across[:half], 1)
    from_far = over_y(across[half:], 3)
    near = jnp.concatenate(
        [near[:half], (near[half:].astype(F32) + from_far.astype(F32)).astype(BF16)]
    )
    far = jnp.concatenate(
        [(far[:half].astype(F32) + from_near.astype(F32)).astype(BF16), far[half:]]
    )
    return mine.astype(F32) + over_y(near, 1).astype(F32) + over_y(far, 3).astype(F32)


def shifted(value, dilation, rows_above, rows_below):
    padded = jnp.pad(
        value,
        ((rows_above * PITCH + dilation, rows_below * PITCH + dilation), (0, 0)),
    )
    length = value.shape[0] + (rows_above + rows_below) * PITCH
    return jnp.stack(
        [padded[k * dilation : k * dilation + length] for k in range(3)]
    )


def conv_body(step, rows, x_ref, w_ref, out_ref):
    tap = pl.program_id(0)
    start = pl.multiple_of((tap // 3) * step, 16)
    part = jnp.dot(
        x_ref[tap % 3, pl.ds(start, rows), :], w_ref[...], preferred_element_type=F32
    )

    @pl.when(tap == 0)
    def _():
        out_ref[...] = part

    @pl.when(tap > 0)
    def _():
        out_ref[...] += part


def conv(stack, weight, step, rows):
    _, length, deep = stack.shape
    wide = 512
    return pl.pallas_call(
        functools.partial(conv_body, step, rows),
        grid=(9,),
        in_specs=[
            pl.BlockSpec((3, length, deep), lambda t: (0, 0, 0)),
            pl.BlockSpec((deep, wide), lambda t: (0, t)),
        ],
        out_specs=pl.BlockSpec((rows, wide), lambda t: (0, 0)),
        out_shape=jax.ShapeDtypeStruct((rows, wide), F32),
        compiler_params=pltpu.CompilerParams(vmem_limit_bytes=48 << 20),
        cost_estimate=pl.CostEstimate(
            flops=2 * 9 * rows * deep * wide,
            bytes_accessed=2 * 9 * deep * wide + 6 * length * deep + 4 * rows * wide,
            transcendentals=0,
        ),
    )(stack, weight)


def conv_t_body(step, rows, g_ref, w_ref, out_ref):
    tap = pl.program_id(1)
    start = pl.multiple_of((2 - tap // 3) * step, 16)
    part = lax.dot_general(
        g_ref[2 - tap % 3, pl.ds(start, rows), :],
        w_ref[...],
        (((1,), (1,)), ((), ())),
        preferred_element_type=F32,
    )

    @pl.when(tap == 0)
    def _():
        out_ref[...] = part

    @pl.when(tap > 0)
    def _():
        out_ref[...] += part


def conv_t(stack, weight, step, rows):
    _, length, wide = stack.shape
    deep = weight.shape[0]
    return pl.pallas_call(
        functools.partial(conv_t_body, step, rows),
        grid=(deep // 512, 9),
        in_specs=[
            pl.BlockSpec((3, length, wide), lambda c, t: (0, 0, 0)),
            pl.BlockSpec((512, wide), lambda c, t: (c, t)),
        ],
        out_specs=pl.BlockSpec((rows, 512), lambda c, t: (0, c)),
        out_shape=jax.ShapeDtypeStruct((rows, deep), F32),
        compiler_params=pltpu.CompilerParams(vmem_limit_bytes=48 << 20),
        cost_estimate=pl.CostEstimate(
            flops=2 * 9 * rows * deep * wide,
            bytes_accessed=2 * 9 * deep * wide + 6 * length * wide + 4 * rows * deep,
            transcendentals=0,
        ),
    )(stack, weight)


def conv_w_body(step, rows, x_ref, g_ref, out_ref):
    tap = pl.program_id(0)
    start = pl.multiple_of((2 - tap // 3) * step, 16)
    out_ref[...] = jnp.dot(
        x_ref[...], g_ref[2 - tap % 3, pl.ds(start, rows), :], preferred_element_type=F32
    ).astype(out_ref.dtype)


def conv_w(turned, stack, step):
    deep, rows = turned.shape
    _, length, wide = stack.shape
    return pl.pallas_call(
        functools.partial(conv_w_body, step, rows),
        grid=(9,),
        in_specs=[
            pl.BlockSpec((deep, rows), lambda t: (0, 0)),
            pl.BlockSpec((3, length, wide), lambda t: (0, 0, 0)),
        ],
        out_specs=pl.BlockSpec((deep, wide), lambda t: (0, t)),
        out_shape=jax.ShapeDtypeStruct((deep, 9 * wide), BF16),
        compiler_params=pltpu.CompilerParams(vmem_limit_bytes=48 << 20),
        cost_estimate=pl.CostEstimate(
            flops=2 * 9 * rows * deep * wide,
            bytes_accessed=2 * 9 * deep * wide + 6 * length * wide + 2 * rows * deep,
            transcendentals=0,
        ),
    )(turned, stack)


def sums_of(value, inside):
    return jnp.stack(
        [jnp.sum(value * inside, axis=0), jnp.sum(value * value * inside, axis=0)]
    )


def norm_of(value, sums, gain, bias, count):
    mean = sums[0] / count
    inverse = lax.rsqrt(sums[1] / count - mean * mean + EPS)
    centred = (value - mean) * inverse
    return gain * centred + bias, centred, inverse


def back_sums(upstream, centred):
    return jnp.stack([jnp.sum(upstream * centred, axis=0), jnp.sum(upstream, axis=0)])


def norm_back(upstream, centred, inverse, gain, inside, sums, count):
    return inside * gain * inverse * (upstream - (sums[1] + centred * sums[0]) / count)


def gelu_back(before, upstream):
    unused, pullback = jax.vjp(jax.nn.gelu, before)
    return pullback(upstream)[0]


def strips_of(value):
    _, rows, across, deep = value.shape
    padded = jnp.pad(value[0], ((0, 0), (0, PITCH - across), (0, 0)))
    return padded.reshape(rows * PITCH, deep)


def maps_of(value, across):
    rows = value.shape[0] // PITCH
    return value.reshape(1, rows, PITCH, -1)[:, :, :across]


def shares_summed(value):
    count = lax.axis_size(IMG)
    parts = lax.all_to_all(
        value.reshape(count, value.shape[0] // count, value.shape[1]), IMG, 0, 0
    )
    return jnp.sum(parts.astype(F32), axis=0)


def shards(
    features,
    image_size,
    reduce_weight,
    dilated_weight,
    expand_weight,
    head_weight,
    message_weight,
    gate_weight,
    bottleneck_gain,
    bottleneck_bias,
    expand_gain,
    expand_bias,
    head_gain,
    head_bias,
    depth_cotangent,
    seg_cotangent,
):
    ylo, core, yhi = (lax.axis_index(a) for a in ("ylo", "core", "yhi"))
    plane = lax.axis_index("x") * 4 + lax.axis_index("z")
    y = yhi * 2 + ylo
    strip = ylo * 2 + core
    across = features.shape[2]
    local = core == yhi

    count = jnp.sum(image_size[:, 0].astype(F32) * image_size[:, 1].astype(F32))

    def inside_of(image, first, rows):
        size = lax.dynamic_index_in_dim(image_size, image, 0, keepdims=False)
        at = jnp.arange(rows * PITCH, dtype=jnp.int32)
        valid = (first + at // PITCH < size[0]) & (at % PITCH < size[1])
        return valid.astype(F32)[:, None]

    inside = inside_of(plane * 2 + yhi, strip * 2, 2)
    inside_whole = inside_of(plane * 2 + core, 0, 8)

    group = [
        (i, i ^ 5) for i in range(8) if (i >> 1) & 1 == i & 1
    ]

    def brought(mine, sent):
        return jnp.where(local, mine, lax.ppermute(sent, GROUP, group))

    def of_head(stacked, head):
        return lax.dynamic_index_in_dim(stacked, head, 0, keepdims=False)

    trunk_weights = jnp.concatenate([dilated_weight, expand_weight], axis=1)
    reduce_part = brought(reduce_weight, reduce_weight)
    pool = lax.all_to_all(
        jnp.broadcast_to(reduce_part[None], (16,) + reduce_part.shape), ("x", "z"), 0, 0
    )
    whole_reduce = jnp.stack(in_order(pool, over_core(pool), core), axis=1).reshape(
        -1, reduce_weight.shape[1]
    )
    trunk_part = brought(trunk_weights, trunk_weights)
    whole_trunk = lax.all_gather(trunk_part, POOL, axis=0, tiled=True)
    wide = dilated_weight.shape[1]
    whole_dilated, whole_expand = whole_trunk[:, :wide], whole_trunk[:, wide:]
    task_weights = jnp.concatenate([message_weight, gate_weight], axis=2)
    head_part = brought(of_head(head_weight, y), of_head(head_weight, y ^ 3))
    task_part = brought(of_head(task_weights, y), of_head(task_weights, y ^ 3))
    whole_head = lax.all_gather(head_part, POOL, axis=0, tiled=True)
    whole_task = lax.all_gather(task_part, POOL, axis=0, tiled=True)
    whole_message, whole_gate = whole_task[:, :wide], whole_task[:, wide:]

    base = strips_of(features) * inside.astype(BF16)
    cotangents = to_heads(
        jnp.concatenate([strips_of(depth_cotangent), strips_of(seg_cotangent)], axis=1),
        y,
        core,
    ).astype(F32)
    base_image = gather_rows(base, ylo, core)

    pre_one = jnp.dot(base, whole_reduce, preferred_element_type=F32)
    norm_one, centred_one, inverse_one = norm_of(
        pre_one, total(sums_of(pre_one, inside), True), bottleneck_gain[0], bottleneck_bias[0], count
    )
    act_one = gather_rows((jax.nn.gelu(norm_one) * inside).astype(BF16), ylo, core)

    def strip_stack(image):
        padded = jnp.pad(image, ((2 * PITCH + 2, 2 * PITCH + 2), (0, 0)))
        return jnp.stack(
            [
                lax.dynamic_slice_in_dim(padded, strip * (2 * PITCH) + 2 * k, 6 * PITCH, 0)
                for k in range(3)
            ]
        )

    pre_two = conv(strip_stack(act_one), whole_dilated, 2 * PITCH, 2 * PITCH)
    norm_two, centred_two, inverse_two = norm_of(
        pre_two, total(sums_of(pre_two, inside), True), bottleneck_gain[1], bottleneck_bias[1], count
    )
    act_two = (jax.nn.gelu(norm_two) * inside).astype(BF16)
    act_two_image = gather_rows(act_two, ylo, core)
    pre_three = jnp.dot(act_two, whole_expand, preferred_element_type=F32)
    norm_three, centred_three, inverse_three = norm_of(
        pre_three, total(sums_of(pre_three, inside), True), expand_gain, expand_bias, count
    )
    joined = norm_three + base.astype(F32)
    trunk = to_heads((jax.nn.gelu(joined) * inside).astype(BF16), y, core)

    pre_head = conv(shifted(trunk, 1, 1, 1), whole_head, PITCH, 8 * PITCH)
    gain_here, bias_here = of_head(head_gain, y), of_head(head_bias, y)
    norm_head, centred_head, inverse_head = norm_of(
        pre_head, total(sums_of(pre_head, inside_whole), False), gain_here, bias_here, count
    )
    task = (jax.nn.gelu(norm_head) * inside_whole).astype(BF16)
    message = conv(shifted(task, 1, 1, 1), whole_message, PITCH, 8 * PITCH)
    gate = jax.nn.sigmoid(jnp.dot(task, whole_gate, preferred_element_type=F32))
    gated = (gate * message).astype(BF16)
    streams = from_heads(
        jnp.concatenate(
            [jnp.where(y == 0, task, gated), jnp.where(y == 1, task, gated)], axis=1
        ),
        y,
        core,
    )
    streams = maps_of(streams * inside, across)
    depth_out, seg_out = jnp.split(streams, 2, axis=3)

    cot_depth, cot_seg = jnp.split(cotangents * inside_whole, 2, axis=1)
    receive = jnp.where(y == 0, cot_seg, jnp.where(y == 1, cot_depth, cot_depth + cot_seg))
    direct = jnp.where(y == 0, cot_depth, jnp.where(y == 1, cot_seg, jnp.zeros_like(cot_seg)))
    d_logit = (receive * message * gate * (1.0 - gate)).astype(BF16)
    d_message = (receive * gate).astype(BF16)
    d_message_stack = shifted(d_message, 1, 1, 1)
    d_task = (
        direct
        + lax.dot_general(
            d_logit, whole_gate, (((1,), (1,)), ((), ())), preferred_element_type=F32
        )
        + conv_t(d_message_stack, whole_message, PITCH, 8 * PITCH)
    )
    d_norm_head = gelu_back(norm_head, d_task * inside_whole)
    head_sums_here = back_sums(d_norm_head, centred_head)
    head_sums = total(head_sums_here, False)
    d_pre_head = norm_back(
        d_norm_head, centred_head, inverse_head, gain_here, inside_whole, head_sums, count
    ).astype(BF16)
    d_head_stack = shifted(d_pre_head, 1, 1, 1)

    head_share = lax.psum_scatter(
        conv_w(trunk.T, d_head_stack, PITCH), POOL, scatter_dimension=0, tiled=True
    )
    task_turned = task.T
    task_share = lax.psum_scatter(
        jnp.concatenate(
            [
                conv_w(task_turned, d_message_stack, PITCH),
                jnp.dot(task_turned, d_logit, preferred_element_type=F32).astype(BF16),
            ],
            axis=1,
        ),
        POOL,
        scatter_dimension=0,
        tiled=True,
    )

    d_trunk = from_heads(conv_t(d_head_stack, whole_head, PITCH, 8 * PITCH), y, core)
    d_joined = gelu_back(joined, d_trunk * inside)
    placed_sums = jnp.where(
        jnp.arange(4)[None, :, None] == y, head_sums_here[:, None], jnp.zeros((1, 1, 1), F32)
    ).reshape(2, -1)
    wide_sums = total(
        jnp.concatenate([back_sums(d_joined, centred_three), placed_sums], axis=1), True
    )
    deep = expand_gain.shape[0]
    expand_sums, all_head_sums = wide_sums[:, :deep], wide_sums[:, deep:]
    d_pre_three = norm_back(
        d_joined, centred_three, inverse_three, expand_gain, inside, expand_sums, count
    ).astype(BF16)
    d_act_two = lax.dot_general(
        d_pre_three, whole_expand, (((1,), (1,)), ((), ())), preferred_element_type=F32
    )
    d_norm_two = gelu_back(norm_two, d_act_two * inside)
    second_sums = total(back_sums(d_norm_two, centred_two), True)
    d_pre_two = gather_rows(
        norm_back(
            d_norm_two, centred_two, inverse_two, bottleneck_gain[1], inside, second_sums, count
        ).astype(BF16),
        ylo,
        core,
    )
    d_act_one = conv_t(strip_stack(d_pre_two), whole_dilated, 2 * PITCH, 2 * PITCH)
    d_norm_one = gelu_back(norm_one, d_act_one * inside)
    first_sums = total(back_sums(d_norm_one, centred_one), True)
    d_pre_one = norm_back(
        d_norm_one, centred_one, inverse_one, bottleneck_gain[0], inside, first_sums, count
    ).astype(BF16)
    d_base = d_joined + lax.dot_general(
        d_pre_one, whole_reduce, (((1,), (1,)), ((), ())), preferred_element_type=F32
    )
    input_grad = maps_of(d_base * inside, across)

    d_three_part = lax.all_to_all(
        jnp.stack(jnp.split(d_pre_three, 4, axis=1)), ROWS, 0, 0
    ).reshape(8 * PITCH, -1)
    d_two_part = lax.dynamic_slice_in_dim(d_pre_two, strip * 128, 128, 1)
    d_one_part = lax.dynamic_slice_in_dim(
        gather_rows(d_pre_one, ylo, core), strip * 128, 128, 1
    )
    grad_expand = jnp.dot(act_two_image.T, d_three_part, preferred_element_type=F32)
    grad_dilated = conv_w(act_one.T, shifted(d_two_part, 2, 2, 2), 2 * PITCH)
    grad_reduce = jnp.dot(base_image.T, d_one_part, preferred_element_type=F32)
    trunk_share = shares_summed(
        jnp.concatenate([grad_expand.astype(BF16), grad_dilated], axis=1)
    ).astype(BF16)
    reduce_share = shares_summed(grad_reduce.astype(BF16)).astype(BF16)
    all_reduce = gather_rows(reduce_share, ylo, core).reshape(4, -1, 128)
    all_trunk = gather_rows(trunk_share, ylo, core).reshape(4, 16, -1)
    sum_reduce = jnp.moveaxis(all_reduce, 0, 1).reshape(-1, 512).astype(F32)
    sum_expand = jnp.moveaxis(all_trunk[:, :, :512], 0, 1).reshape(16, -1).astype(F32)
    sum_dilated = (
        jnp.moveaxis(all_trunk[:, :, 512:].reshape(4, 16, 9, 128), 0, 2)
        .reshape(16, -1)
        .astype(F32)
    )

    def all_heads(share):
        pieces = [share]
        for flip in (1, 2, 3):
            pairs = []
            for i in range(8):
                low, c, high = i >> 2, (i >> 1) & 1, i & 1
                to = (high * 2 + low) ^ flip
                if to >> 1 == c:
                    pairs.append((i, ((to & 1) << 2) | (c << 1) | (to >> 1)))
            pieces.append(lax.ppermute(share, GROUP, pairs))
        low = [jnp.stack(in_order(pieces[0], pieces[1], ylo)), jnp.stack(in_order(pieces[2], pieces[3], ylo))]
        stacked = jnp.concatenate(in_order(low[0], low[1], yhi))
        pairs = [(i, i ^ 2) for i in range(8) if (i >> 1) & 1 == i & 1]
        return jnp.where(local, stacked, lax.ppermute(stacked, GROUP, pairs)).astype(F32)

    sum_head = all_heads(head_share)
    sum_task = all_heads(task_share)
    sum_message, sum_gate = sum_task[:, :, :wide], sum_task[:, :, wide:]

    return (
        depth_out,
        seg_out,
        input_grad,
        sum_reduce,
        sum_dilated,
        sum_expand,
        sum_head,
        sum_message,
        sum_gate,
        jnp.stack([first_sums[0], second_sums[0]]),
        jnp.stack([first_sums[1], second_sums[1]]),
        expand_sums[0],
        expand_sums[1],
        all_head_sums[0].reshape(4, -1),
        all_head_sums[1].reshape(4, -1),
    )


def solution(mesh):
    fine = Mesh(mesh.devices.reshape(2, 2, 4, 4, 2), FINE)
    maps = P(IMG, ROWS, None, None)
    placed = (
        maps,
        P(),
        P(IMG, None),
        P(IMG, None),
        P(IMG, None),
        P(None, IMG, None),
        P(None, IMG, None),
        P(None, IMG, None),
        P(),
        P(),
        P(),
        P(),
        P(),
        P(),
        maps,
        maps,
    )
    return jax.shard_map(
        shards,
        mesh=fine,
        in_specs=placed,
        out_specs=(
            maps,
            maps,
            maps,
            P(IMG, None),
            P(IMG, None),
            P(IMG, None),
            P(None, IMG, None),
            P(None, IMG, None),
            P(None, IMG, None),
            P(),
            P(),
            P(),
            P(),
            P(),
            P(),
        ),
        check_vma=False,
    )
```

```python
import functools

import jax
import jax.numpy as jnp
from jax import lax
from jax.experimental import pallas as pl
from jax.experimental.pallas import tpu as pltpu
from jax.sharding import Mesh, PartitionSpec as P

EPS = 1e-05
PITCH = 80
ROOT = 0.7978845608028654
CUBE = 0.044715
F32 = jnp.float32
BF16 = jnp.bfloat16

FINE = ("ylo", "core", "x", "z", "yhi")
ROWS = ("ylo", "core")
IMG = ("x", "z", "yhi")
RING = ("ylo", "yhi")
GROUP = ("ylo", "core", "yhi")
POOL = ("x", "z", "core")


def swap(value, axis, flip):
    count = lax.axis_size(axis)
    return lax.ppermute(value, axis, [(i, i ^ flip) for i in range(count)])


def over_core(value):
    return swap(value, "core", 1)


def over_y(value, flip):
    return swap(value, RING, {1: 2, 2: 1, 3: 3}[flip])


def fold(value, *partners):
    for axis, flip in partners:
        value = value + (over_y(value, flip) if axis == "y" else swap(value, axis, flip))
    return value


CORE, LINE, PLANE, RIDGE = ("core", 1), (("x", 1), ("x", 3)), (("z", 1), ("z", 3)), (("y", 1), ("y", 3))


def hold(*arrays):
    return lax.optimization_barrier(arrays)


def in_order(mine, other, bit):
    first = bit == 0
    return jnp.where(first, mine, other), jnp.where(first, other, mine)


def beside_rows(value):
    return (
        value,
        over_y(value, 1),
        over_core(value),
        lax.ppermute(value, GROUP, [(i, i ^ 6) for i in range(8)]),
    )


def from_rows(parts):
    own, low, other, both = parts
    return (
        own,
        over_y(low, 1),
        over_core(other),
        lax.ppermute(both, GROUP, [(i, i ^ 6) for i in range(8)]),
    )


def beside_y(value):
    return over_y(value, 1), over_y(value, 3)


def across_y(near, far):
    half = near.shape[0] // 2
    return over_y(far[:half], 1), over_y(near[half:], 3)


def sent_home(kept_here, got, same):
    return jnp.where(same, kept_here, got), jnp.where(same, got, kept_here)


def half_way(other):
    half = other.shape[1] // 2
    return over_y(other[0, :half], 1), over_y(other[0, half:], 3)


def last_way(own, other, from_near, from_far):
    half = own.shape[1] // 2
    near = jnp.concatenate(
        [own[1, :half], (own[1, half:].astype(F32) + from_far.astype(F32)).astype(BF16)]
    )
    far = jnp.concatenate(
        [(other[1, :half].astype(F32) + from_near.astype(F32)).astype(BF16), other[1, half:]]
    )
    return own[0], over_y(near, 1), over_y(far, 3)


def gelu_parts(value):
    squared = value * value
    bend = jnp.tanh(ROOT * value * (1.0 + CUBE * squared))
    return 0.5 * (1.0 + bend), bend, squared


def gelu(value):
    return value * gelu_parts(value)[0]


def gelu_slope(value):
    level, bend, squared = gelu_parts(value)
    return level + 0.5 * value * (1.0 - bend * bend) * ROOT * (1.0 + 3.0 * CUBE * squared)


def moments(sums_ref, count):
    mean = sums_ref[0:1, :] / count
    return mean, lax.rsqrt(sums_ref[1:2, :] / count - mean * mean + EPS)


def store_sums(sums_ref, first, second):
    sums_ref[0:1, :] = jnp.sum(first, axis=0, keepdims=True)
    sums_ref[1:2, :] = jnp.sum(second, axis=0, keepdims=True)


def add_sums(sums_ref, first, second, columns=slice(None)):
    sums_ref[0:1, columns] += jnp.sum(first, axis=0, keepdims=True)
    sums_ref[1:2, columns] += jnp.sum(second, axis=0, keepdims=True)


def store_moved(stack_ref, start, value, dilation, columns=slice(None)):
    rows = pl.ds(start, PITCH)
    stack_ref[0, rows, columns] = pltpu.roll(value, dilation, 0).astype(BF16)
    stack_ref[1, rows, columns] = value.astype(BF16)
    stack_ref[2, rows, columns] = pltpu.roll(value, PITCH - dilation, 0).astype(BF16)


def clear_ends(stack_ref, rows):
    length = stack_ref.shape[1]
    empty = jnp.zeros((3, rows, stack_ref.shape[2]), BF16)
    stack_ref[:, 0:rows, :] = empty
    stack_ref[:, length - rows : length, :] = empty


def move_map(stack_ref, map_ref, dilation):
    clear_ends(stack_ref, dilation * PITCH)

    @pl.loop(0, 8)
    def _(r):
        at = pl.multiple_of(r * PITCH, 16)
        store_moved(
            stack_ref,
            pl.multiple_of(at + dilation * PITCH, 16),
            map_ref[pl.ds(at, PITCH), :].astype(F32),
            dilation,
        )


def times_turned(first, second):
    return lax.dot_general(first, second, (((1,), (1,)), ((), ())), preferred_element_type=F32)


def whole(shape):
    return pl.BlockSpec(shape, lambda *at: (0,) * len(shape), pipeline_mode=pl.Buffered(1))


def kept(shape):
    return pl.BlockSpec(shape, lambda *at: (0,) * len(shape))


SCALARS = pl.BlockSpec(memory_space=pltpu.SMEM)


def call(kernel, grid, in_specs, out_specs, outs, scratch, flops, *operands):
    moved = sum(a.size * a.dtype.itemsize for a in operands)
    return pl.pallas_call(
        kernel,
        grid=grid,
        in_specs=in_specs,
        out_specs=out_specs,
        out_shape=[jax.ShapeDtypeStruct(*o) for o in outs],
        scratch_shapes=scratch,
        compiler_params=pltpu.CompilerParams(vmem_limit_bytes=56 << 20),
        cost_estimate=pl.CostEstimate(flops=flops, bytes_accessed=moved, transcendentals=0),
    )(*operands)


def clear_image(image_ref):
    strip = 2 * PITCH
    empty = jnp.zeros((strip, image_ref.shape[1]), BF16)
    image_ref[0:strip, :] = empty
    image_ref[5 * strip : 6 * strip, :] = empty


def window_moved(stack_ref, image_ref, start):
    @pl.loop(0, 6)
    def _(r):
        at = pl.multiple_of(r * PITCH, 16)
        value = image_ref[pl.ds(pl.multiple_of(start + at, 16), PITCH), :]
        store_moved(stack_ref, at, value.astype(F32), 2)


def dilated_kernel(
    count_ref, at_ref, p0, p1, p2, p3, sums_ref, gain_ref, bias_ref, inside_ref, mine_ref, w_ref,
    out_ref, out_sums, image_out, image_ref, stack_ref, total_ref,
):
    tap = pl.program_id(0)
    strip = 2 * PITCH

    @pl.when(tap == 0)
    def _():
        clear_image(image_ref)
        mean, inverse = moments(sums_ref, count_ref[0])
        for k, piece in enumerate((p0, p1, p2, p3)):
            start = pl.multiple_of(at_ref[k], 16)
            normed = gain_ref[...] * ((piece[...].astype(F32) - mean) * inverse) + bias_ref[...]
            act = gelu(normed) * inside_ref[pl.ds(start, strip), :]
            image_ref[pl.ds(pl.multiple_of(start + strip, 16), strip), :] = act.astype(BF16)
        window_moved(stack_ref, image_ref, at_ref[0])
        image_out[...] = image_ref[strip : 5 * strip, :]
        total_ref[...] = jnp.zeros_like(total_ref)

    start = pl.multiple_of((tap // 3) * strip, 16)
    total_ref[...] += jnp.dot(
        stack_ref[tap % 3, pl.ds(start, strip), :], w_ref[...], preferred_element_type=F32
    )

    @pl.when(tap == 8)
    def _():
        out = total_ref[...].astype(BF16)
        out_ref[...] = out
        out = out.astype(F32)
        value = out * mine_ref[...]
        store_sums(out_sums, value, value * out)


def dilated_forward(count, at, pieces, sums, gain, bias, inside, mine, weights, first_block):
    strip, deep = pieces[0].shape
    operands = (*pieces, sums, gain, bias, inside, mine)
    return call(
        dilated_kernel,
        (9,),
        [SCALARS, SCALARS]
        + [whole(a.shape) for a in operands]
        + [pl.BlockSpec((deep, 512), lambda t: (0, first_block + t))],
        [kept((strip, 512)), kept((2, 512)), kept((4 * strip, deep))],
        [((strip, 512), BF16), ((2, 512), F32), ((4 * strip, deep), BF16)],
        [
            pltpu.VMEM((6 * strip, deep), BF16),
            pltpu.VMEM((3, 3 * strip, deep), BF16),
            pltpu.VMEM((strip, 512), F32),
        ],
        18 * strip * deep * 512,
        count,
        at,
        *operands,
        weights,
    )


def expand_kernel(count_ref, value_ref, sums_ref, gain_ref, bias_ref, inside_ref, w_ref, act_ref, out_ref, out_sums):
    mean, inverse = moments(sums_ref, count_ref[0])
    normed = gain_ref[...] * ((value_ref[...].astype(F32) - mean) * inverse) + bias_ref[...]
    act = (gelu(normed) * inside_ref[...]).astype(BF16)
    act_ref[...] = act
    for c in range(4):
        columns = slice(c * 512, (c + 1) * 512)
        part = jnp.dot(act, w_ref[:, columns], preferred_element_type=F32).astype(BF16)
        out_ref[:, columns] = part
        part = part.astype(F32)
        out_sums[0:1, columns] = jnp.sum(part, axis=0, keepdims=True)
        out_sums[1:2, columns] = jnp.sum(part * part, axis=0, keepdims=True)


def expand_forward(count, value, sums, gain, bias, inside, weights):
    rows, deep = value.shape
    return call(
        expand_kernel,
        (1,),
        [SCALARS]
        + [whole(a.shape) for a in (value, sums, gain, bias, inside)]
        + [whole((deep, 2048))],
        [kept((rows, deep)), kept((rows, 2048)), kept((2, 2048))],
        [((rows, deep), BF16), ((rows, 2048), BF16), ((2, 2048), F32)],
        [],
        2 * rows * deep * 2048,
        count,
        value,
        sums,
        gain,
        bias,
        inside,
        weights,
    )


def head_kernel(
    count_ref, at_ref, keep_ref, got_ref, base_keep, base_got, sums_ref, gain_ref, bias_ref, inside_ref, w_ref,
    out_ref, out_sums, trunk_ref, slope_ref, steep_ref, stack_ref,
):
    tap = pl.program_id(0)
    strip = 2 * PITCH

    @pl.when(tap == 0)
    def _():
        clear_ends(stack_ref, PITCH)
        mean, inverse = moments(sums_ref, count_ref[0])
        for k, (values, bases) in enumerate(((keep_ref, base_keep), (got_ref, base_got))):

            @pl.loop(0, 4)
            def _(r):
                source = pl.ds(pl.multiple_of(r * PITCH, 16), PITCH)
                first = at_ref[2 * k + r // 2] + (r % 2) * PITCH
                first = pl.multiple_of(first, 16)
                rows = pl.ds(first, PITCH)
                inside = inside_ref[rows, :]
                for c in range(4):
                    columns = slice(c * 512, (c + 1) * 512)
                    centred = (values[source, columns].astype(F32) - mean[:, columns]) * inverse[:, columns]
                    joined = (
                        gain_ref[:, columns] * centred
                        + bias_ref[:, columns]
                        + bases[source, columns].astype(F32)
                    )
                    level, bend, squared = gelu_parts(joined)
                    trunk = joined * level * inside
                    slope = (
                        level + 0.5 * joined * (1.0 - bend * bend) * ROOT * (1.0 + 3.0 * CUBE * squared)
                    ) * inside
                    trunk_ref[rows, columns] = trunk.astype(BF16)
                    slope_ref[rows, columns] = slope.astype(BF16)
                    steep_ref[rows, columns] = (slope * centred).astype(BF16)
                    store_moved(stack_ref, pl.multiple_of(first + PITCH, 16), trunk, 1, columns)

        out_ref[...] = jnp.zeros_like(out_ref)

    start = pl.multiple_of((tap // 3) * PITCH, 16)
    out_ref[...] += jnp.dot(
        stack_ref[tap % 3, pl.ds(start, 4 * strip), :], w_ref[...], preferred_element_type=F32
    )

    @pl.when(tap == 8)
    def _():
        value = out_ref[...] * inside_ref[...]
        store_sums(out_sums, value, value * out_ref[...])


def head_forward(count, at, keep, got, base_keep, base_got, sums, gain, bias, inside, weights):
    rows = inside.shape[0]
    deep = keep.shape[1]
    return call(
        head_kernel,
        (9,),
        [SCALARS, SCALARS]
        + [whole(keep.shape)] * 4
        + [whole(a.shape) for a in (sums, gain, bias, inside)]
        + [pl.BlockSpec((deep, 512), lambda t: (0, t))],
        [whole((rows, 512)), kept((2, 512))] + [whole((rows, deep))] * 3,
        [((rows, 512), F32), ((2, 512), F32)] + [((rows, deep), BF16)] * 3,
        [pltpu.VMEM((3, rows + 2 * PITCH, deep), BF16)],
        18 * rows * deep * 512,
        count,
        at,
        keep,
        got,
        base_keep,
        base_got,
        sums,
        gain,
        bias,
        inside,
        weights,
    )


def message_kernel(
    count_ref, at_ref, y_ref, value_ref, sums_ref, gain_ref, bias_ref, inside_ref, w_ref, cot_keep, cot_got,
    task_ref, streams_keep, streams_give, d_message_ref, d_logit_ref, d_norm_ref, out_sums,
    stack_ref, total_ref, gate_ref,
):
    rows_all, deep = value_ref.shape
    mean, inverse = moments(sums_ref, count_ref[0])
    gain, bias = gain_ref[...], bias_ref[...]
    number = y_ref[0]
    clear_ends(stack_ref, PITCH)

    def centred_at(rows):
        return (value_ref[rows, :] - mean) * inverse

    @pl.loop(0, 8)
    def _(r):
        at = pl.multiple_of(r * PITCH, 16)
        rows = pl.ds(at, PITCH)
        task = gelu(gain * centred_at(rows) + bias) * inside_ref[rows, :]
        task_ref[rows, :] = task.astype(BF16)
        store_moved(stack_ref, pl.multiple_of(at + PITCH, 16), task, 1)

    gate_ref[...] = jnp.dot(
        task_ref[...], w_ref[:, 9 * 512 : 10 * 512], preferred_element_type=F32
    )
    total_ref[...] = jnp.zeros_like(total_ref)

    @pl.loop(0, 9)
    def _(tap):
        start = pl.multiple_of((tap // 3) * PITCH, 16)
        total_ref[...] += jnp.dot(
            stack_ref[tap % 3, pl.ds(start, rows_all), :],
            w_ref[:, pl.ds(pl.multiple_of(tap * 512, 512), 512)],
            preferred_element_type=F32,
        )

    for k, cots in enumerate((cot_keep, cot_got)):

        @pl.loop(0, 4)
        def _(r):
            source = pl.ds(pl.multiple_of(r * PITCH, 16), PITCH)
            at = pl.multiple_of(at_ref[2 * k + r // 2] + (r % 2) * PITCH, 16)
            rows = pl.ds(at, PITCH)
            inside = inside_ref[rows, :]
            message = total_ref[rows, :]
            gate = 1.0 / (1.0 + jnp.exp(-gate_ref[rows, :]))
            cot_depth = cots[source, :deep].astype(F32) * inside
            cot_seg = cots[source, deep:].astype(F32) * inside
            receive = jnp.where(
                number == 0, cot_seg, jnp.where(number == 1, cot_depth, cot_depth + cot_seg)
            )
            direct = jnp.where(
                number == 0, cot_depth, jnp.where(number == 1, cot_seg, jnp.zeros_like(cot_seg))
            )
            task = task_ref[rows, :]
            gated = (gate * message).astype(BF16)
            slot = pl.ds(pl.multiple_of((r % 2) * PITCH, 16), PITCH)
            streams_ref = (streams_keep, streams_give)[k]
            streams_ref[r // 2, slot, :deep] = jnp.where(number == 0, task, gated)
            streams_ref[r // 2, slot, deep:] = jnp.where(number == 1, task, gated)
            d_logit_ref[rows, :] = (receive * message * gate * (1.0 - gate)).astype(BF16)
            d_message = receive * gate
            d_message_ref[rows, :] = d_message.astype(BF16)
            store_moved(stack_ref, pl.multiple_of(at + PITCH, 16), d_message, 1)
            total_ref[rows, :] = direct

    total_ref[...] += times_turned(d_logit_ref[...], w_ref[:, 9 * 512 : 10 * 512])

    @pl.loop(0, 9)
    def _(tap):
        start = pl.multiple_of((2 - tap // 3) * PITCH, 16)
        total_ref[...] += times_turned(
            stack_ref[2 - tap % 3, pl.ds(start, rows_all), :],
            w_ref[:, pl.ds(pl.multiple_of(tap * 512, 512), 512)],
        )

    out_sums[...] = jnp.zeros_like(out_sums)

    @pl.loop(0, 8)
    def _(r):
        rows = pl.ds(pl.multiple_of(r * PITCH, 16), PITCH)
        centred = centred_at(rows)
        upstream = gelu_slope(gain * centred + bias) * total_ref[rows, :] * inside_ref[rows, :]
        d_norm_ref[rows, :] = upstream
        add_sums(out_sums, upstream * centred, upstream)


def message_stage(count, at, y, value, sums, gain, bias, inside, weights, cot_keep, cot_got):
    rows, deep = value.shape
    return call(
        message_kernel,
        (1,),
        [SCALARS] * 3
        + [whole(a.shape) for a in (value, sums, gain, bias, inside, weights)]
        + [whole((rows // 2, 2 * deep))] * 2,
        [
            kept((rows, deep)),
            kept((2, rows // 4, 2 * deep)),
            kept((2, rows // 4, 2 * deep)),
            kept((rows, deep)),
            kept((rows, deep)),
            kept((rows, deep)),
            kept((2, deep)),
        ],
        [
            ((rows, deep), BF16),
            ((2, rows // 4, 2 * deep), BF16),
            ((2, rows // 4, 2 * deep), BF16),
            ((rows, deep), BF16),
            ((rows, deep), BF16),
            ((rows, deep), F32),
            ((2, deep), F32),
        ],
        [
            pltpu.VMEM((3, rows + 2 * PITCH, deep), BF16),
            pltpu.VMEM((rows, deep), F32),
            pltpu.VMEM((rows, deep), F32),
        ],
        40 * rows * deep * 512,
        count,
        at,
        y,
        value,
        sums,
        gain,
        bias,
        inside,
        weights,
        cot_keep,
        cot_got,
    )


def weight_kernel(dilation, chunk, x_ref, g_ref, *rest):
    *more, out_ref, turned_ref, stack_ref = rest
    tap = pl.program_id(0)
    rows = x_ref.shape[0]

    @pl.when(tap == 0)
    def _():
        for c in range(0, x_ref.shape[1], chunk):
            turned_ref[c : c + chunk, :] = x_ref[:, c : c + chunk].T
        move_map(stack_ref, g_ref, dilation)

    def product(g):
        return jnp.dot(turned_ref[...], g, preferred_element_type=F32).astype(BF16)

    @pl.when(tap < 9)
    def _():
        start = pl.multiple_of((2 - tap // 3) * dilation * PITCH, 16)
        out_ref[...] = product(stack_ref[2 - tap % 3, pl.ds(start, rows), :])

    if more:

        @pl.when(tap == 9)
        def _():
            out_ref[...] = product(more[0][...])


def conv_weight(image, upstream, dilation, centre=()):
    rows, deep = image.shape
    wide = upstream.shape[1]
    blocks = 9 + len(centre)
    (out,) = call(
        functools.partial(weight_kernel, dilation, 512),
        (blocks,),
        [whole((rows, deep)), whole((rows, wide))] + [whole((rows, wide)) for a in centre],
        [pl.BlockSpec((deep, wide), lambda t: (0, t))],
        [((deep, blocks * wide), BF16)],
        [
            pltpu.VMEM((deep, rows), BF16),
            pltpu.VMEM((3, rows + 2 * dilation * PITCH, wide), BF16),
        ],
        2 * blocks * rows * deep * wide,
        image,
        upstream,
        *centre,
    )
    return out


def trunk_kernel(
    at_ref, g_ref, slope_ref, steep_ref, w_ref, keep_ref, give_ref, sums_ref, stack_ref, turned_ref, total_ref, line_ref
):
    tap = pl.program_id(0)
    rows = g_ref.shape[0]

    @pl.when(tap == 0)
    def _():
        move_map(stack_ref, g_ref, 1)
        for k in range(9):
            start = (2 - k // 3) * PITCH
            turned_ref[k] = stack_ref[2 - k % 3, start : start + rows, :].T

    part = jnp.dot(w_ref[...], turned_ref[tap], preferred_element_type=F32)

    @pl.when(tap == 0)
    def _():
        total_ref[...] = part

    @pl.when(tap > 0)
    def _():
        total_ref[...] += part

    @pl.when(tap == 8)
    def _():
        for c in range(0, total_ref.shape[0], 512):
            columns = slice(c, c + 512)
            value = total_ref[columns, :].T
            line_ref[...] = value
            sums_ref[0:1, columns] = jnp.sum(
                value * steep_ref[:, columns].astype(F32), axis=0, keepdims=True
            )
            sums_ref[1:2, columns] = jnp.sum(
                value * slope_ref[:, columns].astype(F32), axis=0, keepdims=True
            )
            for k in range(4):
                start = pl.multiple_of(at_ref[k], 16)
                out_ref = (keep_ref, give_ref)[k // 2]
                out_ref[k % 2, :, columns] = line_ref[pl.ds(start, rows // 4), :].astype(BF16)


def trunk_back(at, upstream, slope, steep, weights):
    rows, wide = upstream.shape
    deep = weights.shape[0]
    return call(
        trunk_kernel,
        (9,),
        [SCALARS, whole((rows, wide)), whole((rows, deep)), whole((rows, deep))]
        + [pl.BlockSpec((deep, wide), lambda t: (0, t))],
        [whole((2, rows // 4, deep))] * 2 + [kept((2, deep))],
        [((2, rows // 4, deep), BF16)] * 2 + [((2, deep), F32)],
        [
            pltpu.VMEM((3, rows + 2 * PITCH, wide), BF16),
            pltpu.VMEM((9, wide, rows), BF16),
            pltpu.VMEM((deep, rows), F32),
            pltpu.VMEM((rows, 512), F32),
        ],
        18 * rows * deep * wide,
        at,
        upstream,
        slope,
        steep,
        weights,
    )
def joined_kernel(
    count_ref, at_ref, own_ref, near_ref, far_ref, pre_ref, base_ref, sums_ref, gain_ref, bias_ref, inside_ref, back_ref,
    w_ref, low_ref, low_sums, low_gain, low_bias,
    d_joined_ref, c0, c1, c2, c3, d_norm_ref, out_sums, d_pre_ref,
):
    count = count_ref[0]
    mean, inverse = moments(sums_ref, count)
    inside = inside_ref[...]
    for c in range(4):
        columns = slice(c * 512, (c + 1) * 512)
        centred = (pre_ref[:, columns].astype(F32) - mean[:, columns]) * inverse[:, columns]
        gain = gain_ref[:, columns]
        joined = gain * centred + bias_ref[:, columns] + base_ref[:, columns].astype(F32)
        d_trunk = (
            own_ref[:, columns].astype(F32)
            + near_ref[:, columns].astype(F32)
            + far_ref[:, columns].astype(F32)
        )
        d_joined = gelu_slope(joined) * d_trunk * inside
        d_joined_ref[:, columns] = d_joined
        shift = (back_ref[1:2, columns] + centred * back_ref[0:1, columns]) / count
        d_pre_ref[:, columns] = (
            inside * gain * inverse[:, columns] * (d_joined - shift)
        ).astype(BF16)
    for k, part_ref in enumerate((c0, c1, c2, c3)):
        first = pl.multiple_of(at_ref[k] // (2 * PITCH) * 512, 512)
        part_ref[...] = d_pre_ref[:, pl.ds(first, 512)]
    d_act = times_turned(d_pre_ref[...], w_ref[...])
    mean, inverse = moments(low_sums, count)
    centred = (low_ref[...].astype(F32) - mean) * inverse
    upstream = gelu_slope(low_gain[...] * centred + low_bias[...]) * d_act * inside
    upstream = upstream.astype(BF16)
    d_norm_ref[...] = upstream
    upstream = upstream.astype(F32)
    store_sums(out_sums, upstream * centred, upstream)


def joined_back(count, at, pieces, pre, base, sums, gain, bias, inside, back, weights, low, low_sums, low_gain, low_bias):
    rows, deep = pre.shape
    narrow = low.shape[1]
    operands = (*pieces, pre, base, sums, gain, bias, inside, back)
    lower = (low, low_sums, low_gain, low_bias)
    out_d_joined, *columns, out_d_norm, out_sums = call(
        joined_kernel,
        (1,),
        [SCALARS, SCALARS]
        + [whole(a.shape) for a in pieces]
        + [whole(pre.shape)] * 2
        + [whole(a.shape) for a in operands[5:]]
        + [whole((narrow, deep))]
        + [whole(a.shape) for a in lower],
        [kept((rows, deep))] + [kept((rows, 512))] * 4 + [kept((rows, narrow)), kept((2, narrow))],
        [((rows, deep), F32)]
        + [((rows, 512), BF16)] * 4
        + [((rows, narrow), BF16), ((2, narrow), F32)],
        [pltpu.VMEM((rows, deep), BF16)],
        2 * rows * deep * narrow,
        count,
        at,
        *operands,
        weights,
        *lower,
    )
    return out_d_joined, columns, out_d_norm, out_sums


def dilated_back_kernel(
    count_ref, at_ref, u0, u1, u2, u3, p0, p1, p2, p3, sums_ref, back_ref, gain_ref, inside_ref,
    w_ref, low_ref, low_sums, low_gain, low_bias, mine_ref,
    d_norm_ref, out_sums, part_ref,
    image_ref, stack_ref, turned_ref, total_ref,
):
    tap = pl.program_id(0)
    strip = 2 * PITCH
    count = count_ref[0]

    @pl.when(tap == 0)
    def _():
        clear_image(image_ref)
        mean, inverse = moments(sums_ref, count)
        for k, (up, value) in enumerate(((u0, p0), (u1, p1), (u2, p2), (u3, p3))):
            start = pl.multiple_of(at_ref[k], 16)
            centred = (value[...].astype(F32) - mean) * inverse
            shift = (back_ref[1:2, :] + centred * back_ref[0:1, :]) / count
            scale = inside_ref[pl.ds(start, strip), :] * (gain_ref[...] * inverse)
            lowered = (scale * (up[...].astype(F32) - shift)).astype(BF16)
            image_ref[pl.ds(pl.multiple_of(start + strip, 16), strip), :] = lowered
        window_moved(stack_ref, image_ref, at_ref[0])
        mine = pl.multiple_of(at_ref[0] // strip * 128, 128)
        part_ref[...] = image_ref[strip : 5 * strip, pl.ds(mine, 128)]
        for k in range(9):
            start = (2 - k // 3) * strip
            turned_ref[k] = stack_ref[2 - k % 3, start : start + strip, :].T
        total_ref[...] = jnp.zeros_like(total_ref)

    total_ref[...] += jnp.dot(w_ref[...], turned_ref[tap], preferred_element_type=F32)

    @pl.when(tap == 8)
    def _():
        mean, inverse = moments(low_sums, count)
        centred = (low_ref[...].astype(F32) - mean) * inverse
        slope = gelu_slope(low_gain[...] * centred + low_bias[...])
        upstream = (slope * total_ref[...].T * mine_ref[...]).astype(BF16)
        d_norm_ref[...] = upstream
        upstream = upstream.astype(F32)
        store_sums(out_sums, upstream * centred, upstream)


def dilated_back(
    count, at, ups, values, sums, back, gain, inside, weights, first_block, low, low_sums, low_gain, low_bias, mine
):
    strip, wide = ups[0].shape
    operands = (*ups, *values, sums, back, gain, inside)
    lower = (low, low_sums, low_gain, low_bias, mine)
    return call(
        dilated_back_kernel,
        (9,),
        [SCALARS, SCALARS]
        + [whole(a.shape) for a in operands]
        + [pl.BlockSpec((512, wide), lambda t: (0, first_block + t))]
        + [whole(a.shape) for a in lower],
        [kept((strip, 512)), kept((2, 512)), kept((4 * strip, 128))],
        [((strip, 512), BF16), ((2, 512), F32), ((4 * strip, 128), BF16)],
        [
            pltpu.VMEM((6 * strip, wide), BF16),
            pltpu.VMEM((3, 3 * strip, wide), BF16),
            pltpu.VMEM((9, wide, strip), BF16),
            pltpu.VMEM((512, strip), F32),
        ],
        18 * strip * wide * 512,
        count,
        at,
        *operands,
        weights,
        *lower,
    )


def heads_kernel(at_ref, local_ref, *refs):
    *pieces, got_ref = refs[:5]
    outs = refs[5:]

    def put(k, value):
        first = 0
        for out_ref in outs:
            last = first + out_ref.shape[2]
            out_ref[at_ref[k]] = value[:, first:last].astype(F32)
            first = last

    @pl.when(local_ref[0] == 1)
    def _():
        for k, piece in enumerate(pieces):
            put(k, piece)

    @pl.when(local_ref[0] == 0)
    def _():
        for k in range(4):
            put(k, got_ref.at[k])


def heads_placed(at, local, pieces, got, widths):
    rows, deep = pieces[0].shape
    return call(
        heads_kernel,
        (1,),
        [SCALARS, SCALARS] + [whole((rows, deep))] * 4 + [whole((4, rows, deep))],
        [whole((4, rows, wide)) for wide in widths],
        [((4, rows, wide), F32) for wide in widths],
        [],
        0,
        at,
        local,
        *pieces,
        got,
    )


def sums_of(value):
    return jnp.stack([jnp.sum(value, axis=0), jnp.sum(value * value, axis=0)])


def centred_by(value, sums, count):
    mean = sums[0] / count
    inverse = lax.rsqrt(sums[1] / count - mean * mean + EPS)
    return (value.astype(F32) - mean) * inverse, inverse


def norm_back(upstream, value, sums, gain, inside, back, count):
    centred, inverse = centred_by(value, sums, count)
    return (
        inside * gain * inverse * (upstream.astype(F32) - (back[1] + centred * back[0]) / count)
    ).astype(BF16)


def turned_dot(first, second):
    return lax.dot_general(first, second, (((0,), (0,)), ((), ())), preferred_element_type=F32)


def strips_of(value):
    _, rows, across, deep = value.shape
    padded = jnp.pad(value[0], ((0, 0), (0, PITCH - across), (0, 0)))
    return padded.reshape(rows * PITCH, deep)


def maps_of(value, across):
    rows = value.shape[0] // PITCH
    return value.reshape(1, rows, PITCH, -1)[:, :, :across]


def shares_summed(value, axes, dtype=BF16):
    count = lax.axis_size(axes)
    parts = lax.all_to_all(
        value.reshape(count, value.shape[0] // count, value.shape[1]), axes, 0, 0
    )
    return jnp.sum(parts.astype(F32), axis=0).astype(dtype)


def shards(
    features,
    image_size,
    reduce_weight,
    dilated_weight,
    expand_weight,
    head_weight,
    message_weight,
    gate_weight,
    bottleneck_gain,
    bottleneck_bias,
    expand_gain,
    expand_bias,
    head_gain,
    head_bias,
    depth_cotangent,
    seg_cotangent,
):
    ylo, core, yhi = (lax.axis_index(a) for a in ("ylo", "core", "yhi"))
    plane = lax.axis_index("x") * 4 + lax.axis_index("z")
    y = yhi * 2 + ylo
    strip = ylo * 2 + core
    across = features.shape[2]
    local = core == yhi

    count = jnp.sum(image_size[:, 0].astype(F32) * image_size[:, 1].astype(F32))
    count_here = count.reshape(1)

    def inside_of(sizes, image, first, rows):
        size = lax.dynamic_index_in_dim(sizes, image, 0, keepdims=False)
        at = jnp.arange(rows * PITCH, dtype=jnp.int32)
        valid = (first + at // PITCH < size[0]) & (at % PITCH < size[1])
        return valid.astype(F32)[:, None]

    length = 2 * PITCH
    row_at = (jnp.stack([strip, strip ^ 2, strip ^ 1, strip ^ 3]) * length).astype(jnp.int32)
    head_at = (
        jnp.stack(
            [
                ylo * 2 + core,
                (1 - ylo) * 2 + core,
                ylo * 2 + 1 - core,
                (1 - ylo) * 2 + 1 - core,
            ]
        )
        * length
    ).astype(jnp.int32)

    group = [(i, i ^ 5) for i in range(8) if (i >> 1) & 1 == i & 1]

    def brought(mine, sent):
        return jnp.where(local, mine, lax.ppermute(sent, GROUP, group))

    def of_head(stacked, head):
        return lax.dynamic_index_in_dim(stacked, head, 0, keepdims=False)

    planes = 16
    deep = features.shape[3]
    same = yhi == core
    reduce_part = brought(reduce_weight, reduce_weight)
    copies, y_first, sizes_first, feature_maps, dilated_first, expand_first = hold(
        jnp.broadcast_to(reduce_part[None], (planes,) + reduce_part.shape),
        y,
        image_size,
        features,
        dilated_weight,
        expand_weight,
    )
    reduce_half = lax.all_to_all(copies, ("x", "z"), 0, 0)
    whole_reduce = jnp.stack(
        in_order(reduce_half, over_core(reduce_half), core), axis=1
    ).reshape(-1, reduce_weight.shape[1])
    inside = inside_of(sizes_first, plane * 2 + yhi, strip * 2, 2)
    inside_own = inside_of(sizes_first, plane * 2 + yhi, 0, 8)
    inside_whole = inside_of(sizes_first, plane * 2 + core, 0, 8)
    base = strips_of(feature_maps) * inside.astype(BF16)
    near, far = beside_y(base)
    trunk_weights = jnp.concatenate([expand_first, dilated_first], axis=1)
    trunk_part = brought(trunk_weights, trunk_weights)
    whole_trunk = lax.all_gather(trunk_part, POOL, axis=0, tiled=True)
    first_tap = expand_weight.shape[1] // 512
    task_weights = jnp.concatenate([message_weight, gate_weight], axis=2)
    head_part = brought(of_head(head_weight, y_first), of_head(head_weight, y_first ^ 3))
    task_part = brought(of_head(task_weights, y_first), of_head(task_weights, y_first ^ 3))
    whole_reduce, near, far, head_part, task_part, inside, inside_own, inside_whole = hold(
        whole_reduce, near, far, head_part, task_part, inside, inside_own, inside_whole
    )
    whole_head = lax.all_gather(head_part, POOL, axis=0, tiled=True)
    whole_task = lax.all_gather(task_part, POOL, axis=0, tiled=True)

    pre_one = jnp.dot(base, whole_reduce, preferred_element_type=F32).astype(BF16)
    wide_one = pre_one.astype(F32)
    sums_one = sums_of(wide_one)
    across_low, across_high = across_y(near, far)
    sums_one = fold(sums_one, CORE, *LINE)
    sums_one, ones = hold(sums_one, beside_rows(pre_one))
    sums_one = fold(sums_one, *PLANE, *RIDGE)
    pre_two, sums_two, act_one_image = dilated_forward(
        count_here,
        row_at,
        ones,
        sums_one,
        bottleneck_gain[:1],
        bottleneck_bias[:1],
        inside_own,
        inside,
        whole_trunk,
        first_tap,
    )
    pre_two, sums_two, near, far, across_low, across_high = hold(
        pre_two, sums_two, near, far, across_low, across_high
    )
    base_own = jnp.concatenate([base, near])
    base_other = jnp.concatenate([across_low, across_high, far])
    base_keep = jnp.where(same, base_own, base_other)
    base_got = over_core(jnp.where(same, base_other, base_own))
    base_image = jnp.concatenate([base_own, over_core(base_own)])
    sums_two = fold(sums_two, CORE, *LINE, *PLANE)
    sums_two, base_keep, base_got, base_image = hold(sums_two, base_keep, base_got, base_image)
    sums_two = fold(sums_two, *RIDGE)
    act_two, pre_three, sums_three = expand_forward(
        count_here, pre_two, sums_two, bottleneck_gain[1:], bottleneck_bias[1:], inside, whole_trunk
    )
    near, far = beside_y(pre_three)
    sums_three = fold(sums_three, CORE, *LINE)
    sums_three, near, far = hold(sums_three, near, far)
    across_low, across_high = across_y(near, far)
    sums_three = fold(sums_three, *PLANE)
    sums_three, near, far, across_low, across_high = hold(
        sums_three, near, far, across_low, across_high
    )
    pre_own = jnp.concatenate([pre_three, near])
    pre_other = jnp.concatenate([across_low, across_high, far])
    pre_keep = jnp.where(same, pre_own, pre_other)
    pre_got = over_core(jnp.where(same, pre_other, pre_own))
    sums_three = fold(sums_three, *RIDGE)
    sums_three, depth_cots, seg_cots = hold(sums_three, depth_cotangent, seg_cotangent)

    gain_here, bias_here = of_head(head_gain, y)[None], of_head(head_bias, y)[None]
    wide_gain, wide_bias = expand_gain[None], expand_bias[None]
    pre_head, sums_head, trunk, slope, steep = head_forward(
        count_here,
        head_at,
        pre_keep,
        pre_got,
        base_keep,
        base_got,
        sums_three,
        wide_gain,
        wide_bias,
        inside_whole,
        whole_head,
    )
    cots = jnp.concatenate([strips_of(depth_cots), strips_of(seg_cots)], axis=1)
    near, far = beside_y(cots)
    sums_head, near, far = hold(sums_head, near, far)
    across_low, across_high = across_y(near, far)
    sums_head = fold(sums_head, CORE, *LINE)
    sums_head, near, far, across_low, across_high = hold(
        sums_head, near, far, across_low, across_high
    )
    cots_own = jnp.concatenate([cots, near])
    cots_other = jnp.concatenate([across_low, across_high, far])
    cots_keep = jnp.where(same, cots_own, cots_other)
    cots_got = over_core(jnp.where(same, cots_other, cots_own))
    sums_head = fold(sums_head, *PLANE)
    task, streams_keep, streams_give, d_message, d_logit, d_norm_head, back_here = message_stage(
        count_here,
        head_at,
        y.astype(jnp.int32).reshape(1),
        pre_head,
        sums_head,
        gain_here,
        bias_here,
        inside_whole,
        whole_task,
        cots_keep,
        cots_got,
    )
    task_grad, back_here = hold(conv_weight(task, d_message, 1, (d_logit,)), back_here)
    task_share = lax.psum_scatter(task_grad, POOL, scatter_dimension=0, tiled=True)
    back_head = fold(back_here, CORE, *LINE)
    back_head, twos = hold(back_head, beside_rows(pre_two))
    back_head = fold(back_head, *PLANE)
    back_head, streams_keep, streams_got = hold(
        back_head, streams_keep, over_core(streams_give)
    )
    d_pre_head = norm_back(
        d_norm_head, pre_head, sums_head, gain_here, inside_whole, back_head, count
    )
    streams_own, streams_other = sent_home(streams_keep, streams_got, same)
    d_pre_head, streams_own, streams_other = hold(d_pre_head, streams_own, streams_other)
    from_near, from_far = half_way(streams_other)
    head_grad = conv_weight(trunk, d_pre_head, 1)
    head_grad, d_pre_head, from_near, from_far = hold(head_grad, d_pre_head, from_near, from_far)
    streams = last_way(streams_own, streams_other, from_near, from_far)
    trunk_keep, trunk_give, back_three = trunk_back(head_at, d_pre_head, slope, steep, whole_head)
    trunk_keep, trunk_give, back_three, streams, head_grad, task_share = hold(
        trunk_keep, trunk_give, back_three, streams, head_grad, task_share
    )
    head_share = lax.psum_scatter(head_grad, POOL, scatter_dimension=0, tiled=True)
    placed = jnp.where(
        jnp.arange(4)[None, :, None] == y, back_here[:, None], jnp.zeros((1, 1, 1), F32)
    ).reshape(2, -1)
    back_wide = fold(jnp.concatenate([back_three, placed], axis=1), CORE)
    back_wide, trunk_keep, trunk_got = hold(back_wide, trunk_keep, over_core(trunk_give))
    trunk_own, trunk_other = sent_home(trunk_keep, trunk_got, same)
    from_near, from_far = half_way(trunk_other)
    back_wide = fold(back_wide, *LINE)
    back_wide, from_near, from_far = hold(back_wide, from_near, from_far)
    pieces = last_way(trunk_own, trunk_other, from_near, from_far)
    back_wide = fold(back_wide, *PLANE)
    back_wide, pieces = hold(back_wide, pieces)
    back_wide = fold(back_wide, *RIDGE)
    back_three, back_heads = back_wide[:, :deep], back_wide[:, deep:]
    d_joined, d_three_parts, d_norm_two, back_two = joined_back(
        count_here,
        row_at,
        pieces,
        pre_three,
        base,
        sums_three,
        wide_gain,
        wide_bias,
        inside,
        back_three,
        whole_trunk,
        pre_two,
        sums_two,
        bottleneck_gain[1:],
        bottleneck_bias[1:],
    )
    back_two = fold(back_two, CORE, *LINE)
    back_two, d_norm_twos = hold(back_two, beside_rows(d_norm_two))
    back_two = fold(back_two, *PLANE, *RIDGE)

    d_three_part = jnp.concatenate(from_rows(d_three_parts))
    normed_rows, unused = centred_by(jnp.concatenate(twos), sums_two, count)
    act_two_rows = jax.nn.gelu(
        bottleneck_gain[1] * normed_rows + bottleneck_bias[1]
    ).astype(BF16)
    grad_expand = turned_dot(act_two_rows, d_three_part).astype(BF16)
    back_two, grad_expand = hold(back_two, grad_expand)
    d_norm_one, back_one, d_two_part = dilated_back(
        count_here,
        row_at,
        d_norm_twos,
        twos,
        sums_two,
        back_two,
        bottleneck_gain[1:],
        inside_own,
        whole_trunk,
        first_tap,
        pre_one,
        sums_one,
        bottleneck_gain[:1],
        bottleneck_bias[:1],
        inside,
    )
    def to_chips(share):
        pieces = [share]
        for flip in (1, 2, 3):
            pairs = []
            for i in range(8):
                low, c, high = i >> 2, (i >> 1) & 1, i & 1
                to = (high * 2 + low) ^ flip
                if to >> 1 == c:
                    pairs.append((i, ((to & 1) << 2) | (c << 1) | (to >> 1)))
            pieces.append(lax.ppermute(share, GROUP, pairs))
        return tuple(pieces)

    heads_at = jnp.stack([y, y ^ 1, y ^ 2, y ^ 3]).astype(jnp.int32)
    local_here = local.astype(jnp.int32).reshape(1)

    def to_cores(pieces, *widths):
        pairs = [(i, i ^ 2) for i in range(8) if (i >> 1) & 1 == i & 1]
        got = lax.ppermute(jnp.stack(pieces), GROUP, pairs)
        return heads_placed(heads_at, local_here, pieces, got, widths)

    back_one = fold(back_one, CORE, *RIDGE)
    grad_dilated = conv_weight(act_one_image, d_two_part, 2)
    trunk_grad = jnp.concatenate([grad_expand, grad_dilated], axis=1)
    back_one = fold(back_one, *LINE, *PLANE)
    back_one, trunk_grad, head_share = hold(back_one, trunk_grad, head_share)
    d_pre_one = norm_back(
        d_norm_one, pre_one, sums_one, bottleneck_gain[0], inside, back_one, count
    )
    d_one_parts = [
        lax.dynamic_slice_in_dim(d_pre_one, (strip ^ flip) * 128, 128, 1) for flip in (0, 2, 1, 3)
    ]
    d_one_part = jnp.concatenate(from_rows(d_one_parts))
    trunk_share = shares_summed(trunk_grad, IMG)
    grad_reduce = turned_dot(base_image, d_one_part).astype(BF16)
    reduce_share = shares_summed(grad_reduce, IMG)
    head_pieces = to_chips(head_share)

    def all_strips(value):
        pair = in_order(value, over_core(value), core)
        pair = jnp.stack(pair)
        return jnp.concatenate(in_order(pair, over_y(pair, 1), ylo))

    all_trunk = all_strips(trunk_share)
    sum_expand = jnp.moveaxis(all_trunk[:, :, :512], 0, 1).reshape(16, -1).astype(F32)
    sum_dilated = (
        jnp.moveaxis(all_trunk[:, :, 512:].reshape(4, 16, 9, 128), 0, 2)
        .reshape(16, -1)
        .astype(F32)
    )
    sum_reduce = jnp.moveaxis(all_strips(reduce_share), 0, 1).reshape(-1, 512).astype(F32)

    wide = message_weight.shape[2]
    (sum_head,) = to_cores(head_pieces, wide)
    task_share, d_pre_one = hold(task_share, d_pre_one)
    sum_message, sum_gate = to_cores(to_chips(task_share), wide, gate_weight.shape[2])

    d_base = d_joined + times_turned(d_pre_one, whole_reduce)
    input_grad = maps_of(d_base * inside, across)

    streams = maps_of(sum(a.astype(F32) for a in streams) * inside, across)
    depth_out, seg_out = jnp.split(streams, 2, axis=3)

    return (
        depth_out,
        seg_out,
        input_grad,
        sum_reduce,
        sum_dilated,
        sum_expand,
        sum_head,
        sum_message,
        sum_gate,
        jnp.stack([back_one[0], back_two[0]]),
        jnp.stack([back_one[1], back_two[1]]),
        back_three[0],
        back_three[1],
        back_heads[0].reshape(4, -1),
        back_heads[1].reshape(4, -1),
    )


def solution(mesh):
    fine = Mesh(mesh.devices.reshape(2, 2, 4, 4, 2), FINE)
    maps = P(IMG, ROWS, None, None)
    placed = (
        maps,
        P(),
        P(IMG, None),
        P(IMG, None),
        P(IMG, None),
        P(None, IMG, None),
        P(None, IMG, None),
        P(None, IMG, None),
        P(),
        P(),
        P(),
        P(),
        P(),
        P(),
        maps,
        maps,
    )
    return jax.shard_map(
        shards,
        mesh=fine,
        in_specs=placed,
        out_specs=(
            maps,
            maps,
            maps,
            P(IMG, None),
            P(IMG, None),
            P(IMG, None),
            P(None, IMG, None),
            P(None, IMG, None),
            P(None, IMG, None),
            P(),
            P(),
            P(),
            P(),
            P(),
            P(),
        ),
        check_vma=False,
    )
```

```python
import functools

import jax
import jax.numpy as jnp
from jax import lax
from jax.experimental import pallas as pl
from jax.experimental.pallas import tpu as pltpu
from jax.sharding import Mesh, PartitionSpec as P

EPS = 1e-05
PITCH = 80
ROOT = 0.7978845608028654
CUBE = 0.044715
F32 = jnp.float32
BF16 = jnp.bfloat16

FINE = ("ylo", "core", "x", "z", "yhi")
ROWS = ("ylo", "core")
IMG = ("x", "z", "yhi")
RING = ("ylo", "yhi")
GROUP = ("ylo", "core", "yhi")
POOL = ("x", "z", "core")


def swap(value, axis, flip):
    count = lax.axis_size(axis)
    return lax.ppermute(value, axis, [(i, i ^ flip) for i in range(count)])


def over_core(value):
    return swap(value, "core", 1)


def over_y(value, flip):
    return swap(value, RING, {1: 2, 2: 1, 3: 3}[flip])


def fold(value, *partners):
    for axis, flip in partners:
        value = value + (over_y(value, flip) if axis == "y" else swap(value, axis, flip))
    return value


CORE, LINE, PLANE, RIDGE = ("core", 1), (("x", 1), ("x", 3)), (("z", 1), ("z", 3)), (("y", 1), ("y", 3))


def hold(*arrays):
    return lax.optimization_barrier(arrays)


def in_order(mine, other, bit):
    first = bit == 0
    return jnp.where(first, mine, other), jnp.where(first, other, mine)


def around_y(value):
    return value, over_y(value, 1), over_y(value, 2), over_y(value, 3)


def for_me(parts):
    own, near, across, far = parts
    return own, over_y(near, 1), over_y(across, 2), over_y(far, 3)


HOME = [(i, ((i & 1) << 2) | (((i >> 2) & 1) << 1) | ((i >> 1) & 1)) for i in range(8)]


def sent_home(value):
    return lax.ppermute(value, GROUP, HOME)


def beside_y(value):
    return over_y(value, 1), over_y(value, 3)


def across_y(near, far):
    half = near.shape[0] // 2
    return over_y(far[:half], 1), over_y(near[half:], 3)


def half_way(across):
    half = across.shape[0] // 2
    return over_y(across[:half], 1), over_y(across[half:], 3)


def last_way(own, near, far, from_near, from_far):
    half = own.shape[0] // 2
    near = jnp.concatenate(
        [near[:half], (near[half:].astype(F32) + from_far.astype(F32)).astype(BF16)]
    )
    far = jnp.concatenate(
        [(far[:half].astype(F32) + from_near.astype(F32)).astype(BF16), far[half:]]
    )
    return own, over_y(near, 1), over_y(far, 3)


def gelu_parts(value):
    squared = value * value
    bend = jnp.tanh(ROOT * value * (1.0 + CUBE * squared))
    return 0.5 * (1.0 + bend), bend, squared


def gelu(value):
    return value * gelu_parts(value)[0]


def gelu_slope(value):
    level, bend, squared = gelu_parts(value)
    return level + 0.5 * value * (1.0 - bend * bend) * ROOT * (1.0 + 3.0 * CUBE * squared)


def moments(sums_ref, count):
    mean = sums_ref[0:1, :] / count
    return mean, lax.rsqrt(sums_ref[1:2, :] / count - mean * mean + EPS)


def store_sums(sums_ref, first, second):
    sums_ref[0:1, :] = jnp.sum(first, axis=0, keepdims=True)
    sums_ref[1:2, :] = jnp.sum(second, axis=0, keepdims=True)


def add_sums(sums_ref, first, second, columns=slice(None)):
    sums_ref[0:1, columns] += jnp.sum(first, axis=0, keepdims=True)
    sums_ref[1:2, columns] += jnp.sum(second, axis=0, keepdims=True)


def store_moved(stack_ref, start, value, dilation, columns=slice(None)):
    rows = pl.ds(start, PITCH)
    stack_ref[0, rows, columns] = pltpu.roll(value, dilation, 0).astype(BF16)
    stack_ref[1, rows, columns] = value.astype(BF16)
    stack_ref[2, rows, columns] = pltpu.roll(value, PITCH - dilation, 0).astype(BF16)


def clear_ends(stack_ref, rows):
    length = stack_ref.shape[1]
    empty = jnp.zeros((3, rows, stack_ref.shape[2]), BF16)
    stack_ref[:, 0:rows, :] = empty
    stack_ref[:, length - rows : length, :] = empty


def move_map(stack_ref, map_ref, dilation):
    clear_ends(stack_ref, dilation * PITCH)

    @pl.loop(0, 8)
    def _(r):
        at = pl.multiple_of(r * PITCH, 16)
        store_moved(
            stack_ref,
            pl.multiple_of(at + dilation * PITCH, 16),
            map_ref[pl.ds(at, PITCH), :].astype(F32),
            dilation,
        )


def times_turned(first, second):
    return lax.dot_general(first, second, (((1,), (1,)), ((), ())), preferred_element_type=F32)


def whole(shape):
    return pl.BlockSpec(shape, lambda *at: (0,) * len(shape), pipeline_mode=pl.Buffered(1))


def kept(shape):
    return pl.BlockSpec(shape, lambda *at: (0,) * len(shape))


SCALARS = pl.BlockSpec(memory_space=pltpu.SMEM)


def call(kernel, grid, in_specs, out_specs, outs, scratch, flops, *operands):
    moved = sum(a.size * a.dtype.itemsize for a in operands)
    return pl.pallas_call(
        kernel,
        grid=grid,
        in_specs=in_specs,
        out_specs=out_specs,
        out_shape=[jax.ShapeDtypeStruct(*o) for o in outs],
        scratch_shapes=scratch,
        compiler_params=pltpu.CompilerParams(vmem_limit_bytes=56 << 20),
        cost_estimate=pl.CostEstimate(flops=flops, bytes_accessed=moved, transcendentals=0),
    )(*operands)


def clear_image(image_ref):
    strip = 2 * PITCH
    empty = jnp.zeros((strip, image_ref.shape[1]), BF16)
    image_ref[0:strip, :] = empty
    image_ref[5 * strip : 6 * strip, :] = empty


def window_moved(stack_ref, image_ref, start, rows):
    @pl.loop(0, rows)
    def _(r):
        at = pl.multiple_of(r * PITCH, 16)
        value = image_ref[pl.ds(pl.multiple_of(start + at, 16), PITCH), :]
        store_moved(stack_ref, at, value.astype(F32), 2)


def dilated_kernel(
    count_ref, at_ref, value_ref, sums_ref, gain_ref, bias_ref, inside_ref, w_ref,
    out_ref, out_sums, image_out, value_out, image_ref, stack_ref, total_ref,
):
    tap = pl.program_id(0)
    strip = 2 * PITCH

    @pl.when(tap == 0)
    def _():
        clear_image(image_ref)
        mean, inverse = moments(sums_ref, count_ref[0])
        for k in range(4):
            start = pl.multiple_of(at_ref[k], 16)
            value = value_ref[k * strip : (k + 1) * strip, :]
            value_out[pl.ds(start, strip), :] = value
            normed = gain_ref[...] * ((value.astype(F32) - mean) * inverse) + bias_ref[...]
            act = (gelu(normed) * inside_ref[pl.ds(start, strip), :]).astype(BF16)
            image_ref[pl.ds(pl.multiple_of(start + strip, 16), strip), :] = act
            image_out[pl.ds(start, strip), :] = act
        window_moved(stack_ref, image_ref, 0, 12)
        total_ref[...] = jnp.zeros_like(total_ref)

    start = pl.multiple_of((tap // 3) * strip, 16)
    total_ref[...] += jnp.dot(
        stack_ref[tap % 3, pl.ds(start, 4 * strip), :], w_ref[...], preferred_element_type=F32
    )

    @pl.when(tap == 8)
    def _():
        out = total_ref[...].astype(BF16)
        out_ref[...] = out
        out = out.astype(F32)
        value = out * inside_ref[...]
        store_sums(out_sums, value, value * out)


def dilated_forward(count, at, value, sums, gain, bias, inside, weights, first_block):
    rows, deep = value.shape
    strip = 2 * PITCH
    operands = (value, sums, gain, bias, inside)
    return call(
        dilated_kernel,
        (9,),
        [SCALARS, SCALARS]
        + [whole(a.shape) for a in operands]
        + [pl.BlockSpec((deep, 512), lambda t: (0, first_block + t))],
        [kept((rows, 512)), kept((2, 512)), kept((rows, deep)), kept((rows, deep))],
        [((rows, 512), BF16), ((2, 512), F32), ((rows, deep), BF16), ((rows, deep), BF16)],
        [
            pltpu.VMEM((rows + 2 * strip, deep), BF16),
            pltpu.VMEM((3, rows + 2 * strip, deep), BF16),
            pltpu.VMEM((rows, 512), F32),
        ],
        18 * rows * deep * 512,
        count,
        at,
        *operands,
        weights,
    )


def expand_kernel(count_ref, value_ref, sums_ref, gain_ref, bias_ref, inside_ref, w_ref, act_ref, out_ref, out_sums):
    mean, inverse = moments(sums_ref, count_ref[0])
    normed = gain_ref[...] * ((value_ref[...].astype(F32) - mean) * inverse) + bias_ref[...]
    act = (gelu(normed) * inside_ref[...]).astype(BF16)
    act_ref[...] = act
    for c in range(4):
        columns = slice(c * 512, (c + 1) * 512)
        part = jnp.dot(act, w_ref[:, columns], preferred_element_type=F32).astype(BF16)
        out_ref[:, columns] = part
        part = part.astype(F32)
        out_sums[0:1, columns] = jnp.sum(part, axis=0, keepdims=True)
        out_sums[1:2, columns] = jnp.sum(part * part, axis=0, keepdims=True)


def expand_forward(count, value, sums, gain, bias, inside, weights):
    rows, deep = value.shape
    return call(
        expand_kernel,
        (1,),
        [SCALARS]
        + [whole(a.shape) for a in (value, sums, gain, bias, inside)]
        + [whole((deep, 2048))],
        [kept((rows, deep)), kept((rows, 2048)), kept((2, 2048))],
        [((rows, deep), BF16), ((rows, 2048), BF16), ((2, 2048), F32)],
        [],
        2 * rows * deep * 2048,
        count,
        value,
        sums,
        gain,
        bias,
        inside,
        weights,
    )


def head_kernel(
    count_ref, at_ref, value_ref, base_keep, base_got, sums_ref, gain_ref, bias_ref, inside_ref, w_ref,
    out_ref, out_sums, trunk_ref, slope_ref, steep_ref, base_out, stack_ref,
):
    tap = pl.program_id(0)
    rows_all = out_ref.shape[0]

    @pl.when(tap == 0)
    def _():
        clear_ends(stack_ref, PITCH)
        mean, inverse = moments(sums_ref, count_ref[0])
        for k, bases in enumerate((base_keep, base_got)):

            @pl.loop(0, 4)
            def _(r):
                source = pl.ds(pl.multiple_of(r * PITCH, 16), PITCH)
                first = at_ref[2 * k + r // 2] + (r % 2) * PITCH
                first = pl.multiple_of(first, 16)
                rows = pl.ds(first, PITCH)
                inside = inside_ref[rows, :]
                for c in range(4):
                    columns = slice(c * 512, (c + 1) * 512)
                    centred = (value_ref[rows, columns].astype(F32) - mean[:, columns]) * inverse[:, columns]
                    base = bases[source, columns]
                    base_out[rows, columns] = base
                    joined = gain_ref[:, columns] * centred + bias_ref[:, columns] + base.astype(F32)
                    level, bend, squared = gelu_parts(joined)
                    trunk = joined * level * inside
                    slope = (
                        level + 0.5 * joined * (1.0 - bend * bend) * ROOT * (1.0 + 3.0 * CUBE * squared)
                    ) * inside
                    trunk_ref[rows, columns] = trunk.astype(BF16)
                    slope_ref[rows, columns] = slope.astype(BF16)
                    steep_ref[rows, columns] = (slope * centred).astype(BF16)
                    store_moved(stack_ref, pl.multiple_of(first + PITCH, 16), trunk, 1, columns)

        out_ref[...] = jnp.zeros_like(out_ref)

    start = pl.multiple_of((tap // 3) * PITCH, 16)
    out_ref[...] += jnp.dot(
        stack_ref[tap % 3, pl.ds(start, rows_all), :], w_ref[...], preferred_element_type=F32
    )

    @pl.when(tap == 8)
    def _():
        value = out_ref[...] * inside_ref[...]
        store_sums(out_sums, value, value * out_ref[...])


def head_forward(count, at, value, base_keep, base_got, sums, gain, bias, inside, weights):
    rows, deep = value.shape
    operands = (value, base_keep, base_got, sums, gain, bias, inside)
    return call(
        head_kernel,
        (9,),
        [SCALARS, SCALARS]
        + [whole(a.shape) for a in operands]
        + [pl.BlockSpec((deep, 512), lambda t: (0, t))],
        [whole((rows, 512)), kept((2, 512))] + [whole((rows, deep))] * 4,
        [((rows, 512), F32), ((2, 512), F32)] + [((rows, deep), BF16)] * 4,
        [pltpu.VMEM((3, rows + 2 * PITCH, deep), BF16)],
        18 * rows * deep * 512,
        count,
        at,
        *operands,
        weights,
    )


def message_kernel(
    count_ref, at_ref, ring_ref, y_ref, value_ref, sums_ref, gain_ref, bias_ref, inside_ref, w_ref, cot_keep, cot_got,
    task_ref, s0, s1, s2, s3, d_message_ref, d_logit_ref, d_norm_ref, out_sums,
    stack_ref, total_ref, gate_ref, streams_ref,
):
    rows_all, deep = value_ref.shape
    mean, inverse = moments(sums_ref, count_ref[0])
    gain, bias = gain_ref[...], bias_ref[...]
    number = y_ref[0]
    clear_ends(stack_ref, PITCH)

    def centred_at(rows):
        return (value_ref[rows, :] - mean) * inverse

    @pl.loop(0, 8)
    def _(r):
        at = pl.multiple_of(r * PITCH, 16)
        rows = pl.ds(at, PITCH)
        task = gelu(gain * centred_at(rows) + bias) * inside_ref[rows, :]
        task_ref[rows, :] = task.astype(BF16)
        store_moved(stack_ref, pl.multiple_of(at + PITCH, 16), task, 1)

    gate_ref[...] = jnp.dot(
        task_ref[...], w_ref[:, 9 * 512 : 10 * 512], preferred_element_type=F32
    )
    total_ref[...] = jnp.zeros_like(total_ref)

    @pl.loop(0, 9)
    def _(tap):
        start = pl.multiple_of((tap // 3) * PITCH, 16)
        total_ref[...] += jnp.dot(
            stack_ref[tap % 3, pl.ds(start, rows_all), :],
            w_ref[:, pl.ds(pl.multiple_of(tap * 512, 512), 512)],
            preferred_element_type=F32,
        )

    for k, cots in enumerate((cot_keep, cot_got)):

        @pl.loop(0, 4)
        def _(r):
            source = pl.ds(pl.multiple_of(r * PITCH, 16), PITCH)
            at = pl.multiple_of(at_ref[2 * k + r // 2] + (r % 2) * PITCH, 16)
            rows = pl.ds(at, PITCH)
            inside = inside_ref[rows, :]
            message = total_ref[rows, :]
            gate = 1.0 / (1.0 + jnp.exp(-gate_ref[rows, :]))
            cot_depth = cots[source, :deep].astype(F32) * inside
            cot_seg = cots[source, deep:].astype(F32) * inside
            receive = jnp.where(
                number == 0, cot_seg, jnp.where(number == 1, cot_depth, cot_depth + cot_seg)
            )
            direct = jnp.where(
                number == 0, cot_depth, jnp.where(number == 1, cot_seg, jnp.zeros_like(cot_seg))
            )
            task = task_ref[rows, :]
            gated = (gate * message).astype(BF16)
            streams_ref[rows, :deep] = jnp.where(number == 0, task, gated)
            streams_ref[rows, deep:] = jnp.where(number == 1, task, gated)
            d_logit_ref[rows, :] = (receive * message * gate * (1.0 - gate)).astype(BF16)
            d_message = receive * gate
            d_message_ref[rows, :] = d_message.astype(BF16)
            store_moved(stack_ref, pl.multiple_of(at + PITCH, 16), d_message, 1)
            total_ref[rows, :] = direct

    for k, stream_ref in enumerate((s0, s1, s2, s3)):
        first = pl.multiple_of(ring_ref[k], 16)
        stream_ref[...] = streams_ref[pl.ds(first, 2 * PITCH), :]

    total_ref[...] += times_turned(d_logit_ref[...], w_ref[:, 9 * 512 : 10 * 512])

    @pl.loop(0, 9)
    def _(tap):
        start = pl.multiple_of((2 - tap // 3) * PITCH, 16)
        total_ref[...] += times_turned(
            stack_ref[2 - tap % 3, pl.ds(start, rows_all), :],
            w_ref[:, pl.ds(pl.multiple_of(tap * 512, 512), 512)],
        )

    out_sums[...] = jnp.zeros_like(out_sums)

    @pl.loop(0, 8)
    def _(r):
        rows = pl.ds(pl.multiple_of(r * PITCH, 16), PITCH)
        centred = centred_at(rows)
        upstream = gelu_slope(gain * centred + bias) * total_ref[rows, :] * inside_ref[rows, :]
        d_norm_ref[rows, :] = upstream
        add_sums(out_sums, upstream * centred, upstream)


def message_stage(count, at, ring, y, value, sums, gain, bias, inside, weights, cot_keep, cot_got):
    rows, deep = value.shape
    return call(
        message_kernel,
        (1,),
        [SCALARS] * 4
        + [whole(a.shape) for a in (value, sums, gain, bias, inside, weights)]
        + [whole((rows // 2, 2 * deep))] * 2,
        [
            kept((rows, deep)),
            *[kept((rows // 4, 2 * deep))] * 4,
            kept((rows, deep)),
            kept((rows, deep)),
            kept((rows, deep)),
            kept((2, deep)),
        ],
        [
            ((rows, deep), BF16),
            *[((rows // 4, 2 * deep), BF16)] * 4,
            ((rows, deep), BF16),
            ((rows, deep), BF16),
            ((rows, deep), F32),
            ((2, deep), F32),
        ],
        [
            pltpu.VMEM((3, rows + 2 * PITCH, deep), BF16),
            pltpu.VMEM((rows, deep), F32),
            pltpu.VMEM((rows, deep), F32),
            pltpu.VMEM((rows, 2 * deep), BF16),
        ],
        40 * rows * deep * 512,
        count,
        at,
        ring,
        y,
        value,
        sums,
        gain,
        bias,
        inside,
        weights,
        cot_keep,
        cot_got,
    )


def weight_kernel(dilation, chunk, x_ref, g_ref, *rest):
    *more, out_ref, turned_ref, stack_ref = rest
    tap = pl.program_id(0)
    rows = x_ref.shape[0]

    @pl.when(tap == 0)
    def _():
        for c in range(0, x_ref.shape[1], chunk):
            turned_ref[c : c + chunk, :] = x_ref[:, c : c + chunk].T
        move_map(stack_ref, g_ref, dilation)

    def product(g):
        return jnp.dot(turned_ref[...], g, preferred_element_type=F32).astype(BF16)

    @pl.when(tap < 9)
    def _():
        start = pl.multiple_of((2 - tap // 3) * dilation * PITCH, 16)
        out_ref[...] = product(stack_ref[2 - tap % 3, pl.ds(start, rows), :])

    if more:

        @pl.when(tap == 9)
        def _():
            out_ref[...] = product(more[0][...])


def conv_weight(image, upstream, dilation, centre=()):
    rows, deep = image.shape
    wide = upstream.shape[1]
    blocks = 9 + len(centre)
    (out,) = call(
        functools.partial(weight_kernel, dilation, 512),
        (blocks,),
        [whole((rows, deep)), whole((rows, wide))] + [whole((rows, wide)) for a in centre],
        [pl.BlockSpec((deep, wide), lambda t: (0, t))],
        [((deep, blocks * wide), BF16)],
        [
            pltpu.VMEM((deep, rows), BF16),
            pltpu.VMEM((3, rows + 2 * dilation * PITCH, wide), BF16),
        ],
        2 * blocks * rows * deep * wide,
        image,
        upstream,
        *centre,
    )
    return out


def trunk_kernel(
    at_ref, g_ref, slope_ref, steep_ref, w_ref, o0, o1, o2, o3, sums_ref, stack_ref, turned_ref, total_ref, line_ref
):
    tap = pl.program_id(0)
    rows = g_ref.shape[0]

    @pl.when(tap == 0)
    def _():
        move_map(stack_ref, g_ref, 1)
        for k in range(9):
            start = (2 - k // 3) * PITCH
            turned_ref[k] = stack_ref[2 - k % 3, start : start + rows, :].T

    part = jnp.dot(w_ref[...], turned_ref[tap], preferred_element_type=F32)

    @pl.when(tap == 0)
    def _():
        total_ref[...] = part

    @pl.when(tap > 0)
    def _():
        total_ref[...] += part

    @pl.when(tap == 8)
    def _():
        for c in range(0, total_ref.shape[0], 512):
            columns = slice(c, c + 512)
            value = total_ref[columns, :].T
            line_ref[...] = value
            sums_ref[0:1, columns] = jnp.sum(
                value * steep_ref[:, columns].astype(F32), axis=0, keepdims=True
            )
            sums_ref[1:2, columns] = jnp.sum(
                value * slope_ref[:, columns].astype(F32), axis=0, keepdims=True
            )
            for k in range(4):
                start = pl.multiple_of(at_ref[k], 16)
                out_ref = (o0, o1, o2, o3)[k]
                out_ref[:, columns] = line_ref[pl.ds(start, rows // 4), :].astype(BF16)


def trunk_back(at, upstream, slope, steep, weights):
    rows, wide = upstream.shape
    deep = weights.shape[0]
    return call(
        trunk_kernel,
        (9,),
        [SCALARS, whole((rows, wide)), whole((rows, deep)), whole((rows, deep))]
        + [pl.BlockSpec((deep, wide), lambda t: (0, t))],
        [whole((rows // 4, deep))] * 4 + [kept((2, deep))],
        [((rows // 4, deep), BF16)] * 4 + [((2, deep), F32)],
        [
            pltpu.VMEM((3, rows + 2 * PITCH, wide), BF16),
            pltpu.VMEM((9, wide, rows), BF16),
            pltpu.VMEM((deep, rows), F32),
            pltpu.VMEM((rows, 512), F32),
        ],
        18 * rows * deep * wide,
        at,
        upstream,
        slope,
        steep,
        weights,
    )
def joined_kernel(
    count_ref, at_ref, own_ref, near_ref, far_ref, pre_ref, base_ref, sums_ref, gain_ref, bias_ref, inside_ref, back_ref,
    w_ref, low_ref, low_sums, low_gain, low_bias,
    d_joined_ref, c0, c1, c2, c3, d_norm_ref, out_sums, d_pre_ref,
):
    count = count_ref[0]
    mean, inverse = moments(sums_ref, count)
    inside = inside_ref[...]
    for c in range(4):
        columns = slice(c * 512, (c + 1) * 512)
        centred = (pre_ref[:, columns].astype(F32) - mean[:, columns]) * inverse[:, columns]
        gain = gain_ref[:, columns]
        joined = gain * centred + bias_ref[:, columns] + base_ref[:, columns].astype(F32)
        d_trunk = (
            own_ref[:, columns].astype(F32)
            + near_ref[:, columns].astype(F32)
            + far_ref[:, columns].astype(F32)
        )
        d_joined = gelu_slope(joined) * d_trunk * inside
        d_joined_ref[:, columns] = d_joined.astype(BF16)
        shift = (back_ref[1:2, columns] + centred * back_ref[0:1, columns]) / count
        d_pre_ref[:, columns] = (
            inside * gain * inverse[:, columns] * (d_joined - shift)
        ).astype(BF16)
    for k, part_ref in enumerate((c0, c1, c2, c3)):
        first = pl.multiple_of(at_ref[k] // (2 * PITCH) * 512, 512)
        part_ref[...] = d_pre_ref[:, pl.ds(first, 512)]
    d_act = times_turned(d_pre_ref[...], w_ref[...])
    mean, inverse = moments(low_sums, count)
    centred = (low_ref[...].astype(F32) - mean) * inverse
    upstream = gelu_slope(low_gain[...] * centred + low_bias[...]) * d_act * inside
    upstream = upstream.astype(BF16)
    d_norm_ref[...] = upstream
    upstream = upstream.astype(F32)
    store_sums(out_sums, upstream * centred, upstream)


def joined_back(count, at, pieces, pre, base, sums, gain, bias, inside, back, weights, low, low_sums, low_gain, low_bias):
    rows, deep = pre.shape
    narrow = low.shape[1]
    operands = (*pieces, pre, base, sums, gain, bias, inside, back)
    lower = (low, low_sums, low_gain, low_bias)
    out_d_joined, *columns, out_d_norm, out_sums = call(
        joined_kernel,
        (1,),
        [SCALARS, SCALARS]
        + [whole(a.shape) for a in pieces]
        + [whole(pre.shape)] * 2
        + [whole(a.shape) for a in operands[5:]]
        + [whole((narrow, deep))]
        + [whole(a.shape) for a in lower],
        [kept((rows, deep))] + [kept((rows, 512))] * 4 + [kept((rows, narrow)), kept((2, narrow))],
        [((rows, deep), BF16)]
        + [((rows, 512), BF16)] * 4
        + [((rows, narrow), BF16), ((2, narrow), F32)],
        [pltpu.VMEM((rows, deep), BF16)],
        2 * rows * deep * narrow,
        count,
        at,
        *operands,
        weights,
        *lower,
    )
    return out_d_joined, columns, out_d_norm, out_sums


def dilated_back_kernel(
    count_ref, at_ref, u0, u1, u2, u3, value_ref, sums_ref, back_ref, gain_ref, inside_ref,
    w_ref, low_ref, low_sums, low_gain, low_bias,
    d_norm_ref, out_sums, part_ref,
    image_ref, stack_ref, turned_ref, total_ref,
):
    tap = pl.program_id(0)
    strip = 2 * PITCH
    rows = value_ref.shape[0]
    count = count_ref[0]

    @pl.when(tap == 0)
    def _():
        clear_image(image_ref)
        mean, inverse = moments(sums_ref, count)
        for k, up in enumerate((u0, u1, u2, u3)):
            start = pl.multiple_of(at_ref[k], 16)
            centred = (value_ref[pl.ds(start, strip), :].astype(F32) - mean) * inverse
            shift = (back_ref[1:2, :] + centred * back_ref[0:1, :]) / count
            scale = inside_ref[pl.ds(start, strip), :] * (gain_ref[...] * inverse)
            lowered = (scale * (up[...].astype(F32) - shift)).astype(BF16)
            image_ref[pl.ds(pl.multiple_of(start + strip, 16), strip), :] = lowered
        window_moved(stack_ref, image_ref, 0, 12)
        mine = pl.multiple_of(at_ref[0] // strip * 128, 128)
        part_ref[...] = image_ref[strip : 5 * strip, pl.ds(mine, 128)]
        for k in range(9):
            start = (2 - k // 3) * strip
            turned_ref[k] = stack_ref[2 - k % 3, start : start + rows, :].T
        total_ref[...] = jnp.zeros_like(total_ref)

    total_ref[...] += jnp.dot(w_ref[...], turned_ref[tap], preferred_element_type=F32)

    @pl.when(tap == 8)
    def _():
        mean, inverse = moments(low_sums, count)
        centred = (low_ref[...].astype(F32) - mean) * inverse
        slope = gelu_slope(low_gain[...] * centred + low_bias[...])
        upstream = (slope * total_ref[...].T * inside_ref[...]).astype(BF16)
        d_norm_ref[...] = upstream
        upstream = upstream.astype(F32)
        store_sums(out_sums, upstream * centred, upstream)


def dilated_back(
    count, at, ups, value, sums, back, gain, inside, weights, first_block, low, low_sums, low_gain, low_bias
):
    rows, wide = value.shape
    strip = 2 * PITCH
    operands = (*ups, value, sums, back, gain, inside)
    lower = (low, low_sums, low_gain, low_bias)
    return call(
        dilated_back_kernel,
        (9,),
        [SCALARS, SCALARS]
        + [whole(a.shape) for a in operands]
        + [pl.BlockSpec((512, wide), lambda t: (0, first_block + t))]
        + [whole(a.shape) for a in lower],
        [kept((rows, 512)), kept((2, 512)), kept((rows, 128))],
        [((rows, 512), BF16), ((2, 512), F32), ((rows, 128), BF16)],
        [
            pltpu.VMEM((rows + 2 * strip, wide), BF16),
            pltpu.VMEM((3, rows + 2 * strip, wide), BF16),
            pltpu.VMEM((9, wide, rows), BF16),
            pltpu.VMEM((512, rows), F32),
        ],
        18 * rows * wide * 512,
        count,
        at,
        *operands,
        weights,
        *lower,
    )


def heads_kernel(at_ref, local_ref, *refs):
    *pieces, got_ref = refs[:5]
    outs = refs[5:]

    def put(k, value):
        first = 0
        for out_ref in outs:
            last = first + out_ref.shape[2]
            out_ref[at_ref[k]] = value[:, first:last].astype(F32)
            first = last

    @pl.when(local_ref[0] == 1)
    def _():
        for k, piece in enumerate(pieces):
            put(k, piece)

    @pl.when(local_ref[0] == 0)
    def _():
        for k in range(4):
            put(k, got_ref.at[k])


def heads_placed(at, local, pieces, got, widths):
    rows, deep = pieces[0].shape
    return call(
        heads_kernel,
        (1,),
        [SCALARS, SCALARS] + [whole((rows, deep))] * 4 + [whole((4, rows, deep))],
        [whole((4, rows, wide)) for wide in widths],
        [((4, rows, wide), F32) for wide in widths],
        [],
        0,
        at,
        local,
        *pieces,
        got,
    )


def sums_of(value):
    return jnp.stack([jnp.sum(value, axis=0), jnp.sum(value * value, axis=0)])


def centred_by(value, sums, count):
    mean = sums[0] / count
    inverse = lax.rsqrt(sums[1] / count - mean * mean + EPS)
    return (value.astype(F32) - mean) * inverse, inverse


def norm_back(upstream, value, sums, gain, inside, back, count):
    centred, inverse = centred_by(value, sums, count)
    return (
        inside * gain * inverse * (upstream.astype(F32) - (back[1] + centred * back[0]) / count)
    ).astype(BF16)


def turned_dot(first, second):
    return lax.dot_general(first, second, (((0,), (0,)), ((), ())), preferred_element_type=F32)


def strips_of(value):
    _, rows, across, deep = value.shape
    padded = jnp.pad(value[0], ((0, 0), (0, PITCH - across), (0, 0)))
    return padded.reshape(rows * PITCH, deep)


def maps_of(value, across):
    rows = value.shape[0] // PITCH
    return value.reshape(1, rows, PITCH, -1)[:, :, :across]


def shares_sent(value, axes):
    count = lax.axis_size(axes)
    return lax.all_to_all(
        value.reshape(count, value.shape[0] // count, value.shape[1]), axes, 0, 0
    )


def parts_summed(parts):
    return jnp.sum(parts.astype(F32), axis=0).astype(BF16)


def shards(
    features,
    image_size,
    reduce_weight,
    dilated_weight,
    expand_weight,
    head_weight,
    message_weight,
    gate_weight,
    bottleneck_gain,
    bottleneck_bias,
    expand_gain,
    expand_bias,
    head_gain,
    head_bias,
    depth_cotangent,
    seg_cotangent,
):
    ylo, core, yhi = (lax.axis_index(a) for a in ("ylo", "core", "yhi"))
    plane = lax.axis_index("x") * 4 + lax.axis_index("z")
    y = yhi * 2 + ylo
    strip = ylo * 2 + core
    width = features.shape[2]
    local = core == yhi

    count = jnp.sum(image_size[:, 0].astype(F32) * image_size[:, 1].astype(F32))
    count_here = count.reshape(1)

    def inside_of(sizes, image, first, rows):
        size = lax.dynamic_index_in_dim(sizes, image, 0, keepdims=False)
        at = jnp.arange(rows * PITCH, dtype=jnp.int32)
        valid = (first + at // PITCH < size[0]) & (at % PITCH < size[1])
        return valid.astype(F32)[:, None]

    length = 2 * PITCH
    head_at = (
        jnp.stack(
            [
                ylo * 2 + core,
                (1 - ylo) * 2 + core,
                ylo * 2 + 1 - core,
                (1 - ylo) * 2 + 1 - core,
            ]
        )
        * length
    ).astype(jnp.int32)
    ring_at = (jnp.stack([y, y ^ 1, y ^ 2, y ^ 3]) * length).astype(jnp.int32)

    group = [(i, i ^ 5) for i in range(8) if (i >> 1) & 1 == i & 1]

    def brought(mine, sent):
        return jnp.where(local, mine, lax.ppermute(sent, GROUP, group))

    def of_head(stacked, head):
        return lax.dynamic_index_in_dim(stacked, head, 0, keepdims=False)

    planes = 16

    deep = features.shape[3]
    same = yhi == core
    inside = inside_of(image_size, plane * 2 + yhi, strip * 2, 2)
    base = strips_of(features) * inside.astype(BF16)
    near, far = beside_y(base)
    channels = expand_weight.shape[0]
    wide_trunk = expand_weight.shape[1] + dilated_weight.shape[1]
    first_weights = jnp.concatenate(
        [expand_weight, dilated_weight, reduce_weight.reshape(channels, -1)], axis=1
    )
    first_part = brought(first_weights, first_weights)
    reduce_part = first_part[:, wide_trunk:].reshape(reduce_weight.shape)
    copies, sizes_first = hold(
        jnp.broadcast_to(reduce_part[None], (planes,) + reduce_part.shape), image_size
    )
    reduce_half = lax.all_to_all(copies, ("x", "z"), 0, 0)
    whole_reduce = jnp.stack(
        in_order(reduce_half, over_core(reduce_half), core), axis=1
    ).reshape(-1, reduce_weight.shape[1])
    whole_trunk = lax.all_gather(first_part[:, :wide_trunk], POOL, axis=0, tiled=True)
    first_tap = expand_weight.shape[1] // 512
    inside_whole = inside_of(sizes_first, plane * 2 + core, 0, 8)

    def spread(own, near, across_low, across_high, far):
        mine = jnp.concatenate([own, near])
        other = jnp.concatenate([across_low, across_high, far])
        return jnp.where(same, mine, other), over_core(jnp.where(same, other, mine))

    near, far, y_first = hold(near, far, y)
    head_part = brought(of_head(head_weight, y_first), of_head(head_weight, y_first ^ 3))
    base_keep, base_got = spread(base, near, *across_y(near, far), far)
    whole_reduce, base_keep, base_got, inside_whole, head_part = hold(
        whole_reduce, base_keep, base_got, inside_whole, head_part
    )
    whole_head = lax.all_gather(head_part, POOL, axis=0, tiled=True)

    pre_one = jnp.concatenate(
        [
            jnp.dot(a, whole_reduce, preferred_element_type=F32).astype(BF16)
            for a in (base_keep, base_got)
        ]
    )
    sums_one = fold(sums_of(pre_one.astype(F32)), CORE, *LINE, *PLANE)
    pre_two, sums_two, act_one_image, pre_one_image = dilated_forward(
        count_here,
        head_at,
        pre_one,
        sums_one,
        bottleneck_gain[:1],
        bottleneck_bias[:1],
        inside_whole,
        whole_trunk,
        first_tap,
    )
    sums_two = fold(sums_two, CORE, *LINE)
    sums_two, y_later, depth_cots, seg_cots = hold(sums_two, y, depth_cotangent, seg_cotangent)
    task_weights = jnp.concatenate([message_weight, gate_weight], axis=2)
    task_part = brought(of_head(task_weights, y_later), of_head(task_weights, y_later ^ 3))
    cots = jnp.concatenate([strips_of(depth_cots), strips_of(seg_cots)], axis=1)
    near, far = beside_y(cots)
    sums_two = fold(sums_two, *PLANE)
    act_two, pre_three, sums_three = expand_forward(
        count_here,
        pre_two,
        sums_two,
        bottleneck_gain[1:],
        bottleneck_bias[1:],
        inside_whole,
        whole_trunk,
    )
    sums_three, near, far, task_part = hold(fold(sums_three, CORE), near, far, task_part)
    whole_task = lax.all_gather(task_part, POOL, axis=0, tiled=True)
    across_low, across_high = across_y(near, far)
    sums_three = fold(sums_three, *LINE)
    sums_three, near, far, across_low, across_high = hold(
        sums_three, near, far, across_low, across_high
    )
    cots_keep, cots_got = spread(cots, near, across_low, across_high, far)
    sums_three = fold(sums_three, *PLANE)
    sums_three, cots_keep, cots_got = hold(sums_three, cots_keep, cots_got)

    gain_here, bias_here = of_head(head_gain, y)[None], of_head(head_bias, y)[None]
    wide_gain, wide_bias = expand_gain[None], expand_bias[None]
    pre_head, sums_head, trunk, slope, steep, base_image = head_forward(
        count_here,
        head_at,
        pre_three,
        base_keep,
        base_got,
        sums_three,
        wide_gain,
        wide_bias,
        inside_whole,
        whole_head,
    )
    sums_head = fold(sums_head, CORE, *LINE, *PLANE)
    task, *streams, d_message, d_logit, d_norm_head, back_here = message_stage(
        count_here,
        head_at,
        ring_at,
        y.astype(jnp.int32).reshape(1),
        pre_head,
        sums_head,
        gain_here,
        bias_here,
        inside_whole,
        whole_task,
        cots_keep,
        cots_got,
    )
    task_grad, back_here = hold(conv_weight(task, d_message, 1, (d_logit,)), back_here)
    task_share = lax.psum_scatter(task_grad, POOL, scatter_dimension=0, tiled=True)
    back_head = fold(back_here, CORE, *LINE, *PLANE)
    back_head, streams = hold(back_head, streams)
    d_pre_head = norm_back(
        d_norm_head, pre_head, sums_head, gain_here, inside_whole, back_head, count
    )
    own, near, across, far = streams
    from_near, from_far = half_way(across)
    head_grad = conv_weight(trunk, d_pre_head, 1)
    head_grad, d_pre_head, from_near, from_far = hold(head_grad, d_pre_head, from_near, from_far)
    streams = last_way(own, near, far, from_near, from_far)
    *d_trunk, back_three = trunk_back(ring_at, d_pre_head, slope, steep, whole_head)
    d_trunk, back_three, streams, head_grad, task_share = hold(
        d_trunk, back_three, streams, head_grad, task_share
    )
    head_share = lax.psum_scatter(head_grad, POOL, scatter_dimension=0, tiled=True)
    placed = jnp.where(
        jnp.arange(4)[None, :, None] == y, back_here[:, None], jnp.zeros((1, 1, 1), F32)
    ).reshape(2, -1)
    back_wide = jnp.concatenate([back_three, placed], axis=1)
    own, near, across, far = d_trunk
    from_near, from_far = half_way(across)
    back_wide = fold(back_wide, CORE, *LINE)
    back_wide, from_near, from_far = hold(back_wide, from_near, from_far)
    pieces = last_way(own, near, far, from_near, from_far)
    back_wide = fold(back_wide, *PLANE)
    def strip_of(value):
        return lax.dynamic_slice_in_dim(value, y * length, length, 0)

    pre_two_strip, pre_three_strip, base_strip, inside_strip = (
        strip_of(a) for a in (pre_two, pre_three, base_image, inside_whole)
    )

    def ring_order(value):
        return jnp.concatenate(
            [
                lax.dynamic_slice_in_dim(value, (y ^ flip) * length, length, 0)
                for flip in range(4)
            ]
        )

    act_two_ring = ring_order(act_two)
    (
        back_wide,
        pieces,
        pre_two_strip,
        pre_three_strip,
        base_strip,
        inside_strip,
        act_two_ring,
    ) = hold(
        back_wide,
        pieces,
        pre_two_strip,
        pre_three_strip,
        base_strip,
        inside_strip,
        act_two_ring,
    )
    back_wide = fold(back_wide, *RIDGE)
    back_three, back_heads = back_wide[:, :deep], back_wide[:, deep:]
    d_joined, d_three_parts, d_norm_two, back_two = joined_back(
        count_here,
        ring_at,
        pieces,
        pre_three_strip,
        base_strip,
        sums_three,
        wide_gain,
        wide_bias,
        inside_strip,
        back_three,
        whole_trunk,
        pre_two_strip,
        sums_two,
        bottleneck_gain[1:],
        bottleneck_bias[1:],
    )
    back_two = fold(back_two, CORE, *LINE)
    back_two, d_norm_twos = hold(back_two, around_y(d_norm_two))
    back_two = fold(back_two, *PLANE, *RIDGE)

    d_three_part = jnp.concatenate(for_me(d_three_parts))
    grad_expand = turned_dot(act_two_ring, d_three_part).astype(BF16)
    back_two, grad_expand, d_joined = hold(back_two, grad_expand, d_joined)
    homeward = sent_home(
        jnp.concatenate([d_joined, sum(a.astype(F32) for a in streams).astype(BF16)], axis=1)
    )
    d_norm_one, back_one, d_two_part = dilated_back(
        count_here,
        ring_at,
        d_norm_twos,
        pre_two,
        sums_two,
        back_two,
        bottleneck_gain[1:],
        inside_whole,
        whole_trunk,
        first_tap,
        pre_one_image,
        sums_one,
        bottleneck_gain[:1],
        bottleneck_bias[:1],
    )
    def to_chips(share):
        pieces = [share]
        for flip in (1, 2, 3):
            pairs = []
            for i in range(8):
                low, c, high = i >> 2, (i >> 1) & 1, i & 1
                to = (high * 2 + low) ^ flip
                if to >> 1 == c:
                    pairs.append((i, ((to & 1) << 2) | (c << 1) | (to >> 1)))
            pieces.append(lax.ppermute(share, GROUP, pairs))
        return tuple(pieces)

    heads_at = jnp.stack([y, y ^ 1, y ^ 2, y ^ 3]).astype(jnp.int32)
    local_here = local.astype(jnp.int32).reshape(1)

    def to_cores(pieces, *widths):
        pairs = [(i, i ^ 2) for i in range(8) if (i >> 1) & 1 == i & 1]
        got = lax.ppermute(jnp.stack(pieces), GROUP, pairs)
        return heads_placed(heads_at, local_here, pieces, got, widths)

    back_one = fold(back_one, CORE, *LINE)
    grad_dilated = conv_weight(act_one_image, d_two_part, 2)
    trunk_grad = jnp.concatenate([grad_expand, grad_dilated], axis=1)
    back_one, trunk_grad, homeward = hold(back_one, trunk_grad, homeward)
    back_one = fold(back_one, *PLANE)
    d_pre_one = norm_back(
        d_norm_one, pre_one_image, sums_one, bottleneck_gain[0], inside_whole, back_one, count
    )
    grad_reduce = turned_dot(
        base_image, lax.dynamic_slice_in_dim(d_pre_one, y * 128, 128, 1)
    ).astype(BF16)
    trunk_grad = jnp.concatenate(
        [trunk_grad, grad_reduce.reshape(trunk_grad.shape[0], -1)], axis=1
    )
    trunk_grad, head_share, task_share, d_pre_one = hold(
        trunk_grad, head_share, task_share, d_pre_one
    )
    trunk_parts = shares_sent(trunk_grad, POOL)
    wide = message_weight.shape[2]
    (sum_head,) = to_cores(to_chips(head_share), wide)
    sum_message, sum_gate = to_cores(to_chips(task_share), wide, gate_weight.shape[2])
    d_pre_one = sent_home(strip_of(d_pre_one))
    d_base = homeward[:, :deep].astype(F32) + times_turned(d_pre_one, whole_reduce)
    input_grad = maps_of(d_base * inside, width)
    trunk_parts, sum_head, sum_message, sum_gate, input_grad = hold(
        trunk_parts, sum_head, sum_message, sum_gate, input_grad
    )
    all_trunk, all_reduce = to_cores(
        to_chips(parts_summed(trunk_parts)), trunk_grad.shape[1] - 512, 512
    )
    sum_expand = jnp.moveaxis(all_trunk[:, :, :512], 0, 1).reshape(channels, -1)
    sum_dilated = jnp.moveaxis(
        all_trunk[:, :, 512:].reshape(4, channels, 9, 128), 0, 2
    ).reshape(channels, -1)
    sum_reduce = jnp.moveaxis(all_reduce.reshape(4, -1, 128), 0, 1).reshape(-1, 512)


    streams = maps_of(homeward[:, deep:].astype(F32) * inside, width)
    depth_out, seg_out = jnp.split(streams, 2, axis=3)

    return (
        depth_out,
        seg_out,
        input_grad,
        sum_reduce,
        sum_dilated,
        sum_expand,
        sum_head,
        sum_message,
        sum_gate,
        jnp.stack([back_one[0], back_two[0]]),
        jnp.stack([back_one[1], back_two[1]]),
        back_three[0],
        back_three[1],
        back_heads[0].reshape(4, -1),
        back_heads[1].reshape(4, -1),
    )


def solution(mesh):
    fine = Mesh(mesh.devices.reshape(2, 2, 4, 4, 2), FINE)
    maps = P(IMG, ROWS, None, None)
    placed = (
        maps,
        P(),
        P(IMG, None),
        P(IMG, None),
        P(IMG, None),
        P(None, IMG, None),
        P(None, IMG, None),
        P(None, IMG, None),
        P(),
        P(),
        P(),
        P(),
        P(),
        P(),
        maps,
        maps,
    )
    return jax.shard_map(
        shards,
        mesh=fine,
        in_specs=placed,
        out_specs=(
            maps,
            maps,
            maps,
            P(IMG, None),
            P(IMG, None),
            P(IMG, None),
            P(None, IMG, None),
            P(None, IMG, None),
            P(None, IMG, None),
            P(),
            P(),
            P(),
            P(),
            P(),
            P(),
        ),
        check_vma=False,
    )
```

```python
import functools

import jax
import jax.numpy as jnp
from jax import lax
from jax.experimental import pallas as pl
from jax.experimental.pallas import tpu as pltpu
from jax.sharding import Mesh, PartitionSpec as P

EPS = 1e-05
PITCH = 80
ROOT = 0.7978845608028654
CUBE = 0.044715
F32 = jnp.float32
BF16 = jnp.bfloat16

FINE = ("ylo", "core", "x", "z", "yhi")
ROWS = ("ylo", "core")
IMG = ("x", "z", "yhi")
RING = ("ylo", "yhi")
GROUP = ("ylo", "core", "yhi")
POOL = ("x", "z", "core")


def swap(value, axis, flip):
    count = lax.axis_size(axis)
    return lax.ppermute(value, axis, [(i, i ^ flip) for i in range(count)])


def over_core(value):
    return swap(value, "core", 1)


def over_y(value, flip):
    return swap(value, RING, {1: 2, 2: 1, 3: 3}[flip])


def fold(value, *partners):
    for axis, flip in partners:
        value = value + (over_y(value, flip) if axis == "y" else swap(value, axis, flip))
    return value


CORE, LINE, PLANE, RIDGE = ("core", 1), (("x", 1), ("x", 3)), (("z", 1), ("z", 3)), (("y", 1), ("y", 3))


def hold(*arrays):
    return lax.optimization_barrier(arrays)


def in_order(mine, other, bit):
    first = bit == 0
    return jnp.where(first, mine, other), jnp.where(first, other, mine)


def around_y(value):
    return value, over_y(value, 1), over_y(value, 2), over_y(value, 3)


def for_me(parts):
    own, near, across, far = parts
    return own, over_y(near, 1), over_y(across, 2), over_y(far, 3)


HOME = [(i, ((i & 1) << 2) | (((i >> 2) & 1) << 1) | ((i >> 1) & 1)) for i in range(8)]


def sent_home(value):
    return lax.ppermute(value, GROUP, HOME)


def beside_y(value):
    return over_y(value, 1), over_y(value, 3)


def across_y(near, far):
    half = near.shape[0] // 2
    return over_y(far[:half], 1), over_y(near[half:], 3)


def half_way(across):
    half = across.shape[0] // 2
    return over_y(across[:half], 1), over_y(across[half:], 3)


def last_way(own, near, far, from_near, from_far):
    half = own.shape[0] // 2
    near = jnp.concatenate(
        [near[:half], (near[half:].astype(F32) + from_far.astype(F32)).astype(BF16)]
    )
    far = jnp.concatenate(
        [(far[:half].astype(F32) + from_near.astype(F32)).astype(BF16), far[half:]]
    )
    return own, over_y(near, 1), over_y(far, 3)


def gelu_parts(value):
    squared = value * value
    bend = jnp.tanh(ROOT * value * (1.0 + CUBE * squared))
    return 0.5 * (1.0 + bend), bend, squared


def gelu(value):
    return value * gelu_parts(value)[0]


def gelu_slope(value):
    level, bend, squared = gelu_parts(value)
    return level + 0.5 * value * (1.0 - bend * bend) * ROOT * (1.0 + 3.0 * CUBE * squared)


def moments(sums_ref, count):
    mean = sums_ref[0:1, :] / count
    return mean, lax.rsqrt(sums_ref[1:2, :] / count - mean * mean + EPS)


def store_sums(sums_ref, first, second):
    sums_ref[0:1, :] = jnp.sum(first, axis=0, keepdims=True)
    sums_ref[1:2, :] = jnp.sum(second, axis=0, keepdims=True)


def add_sums(sums_ref, first, second, columns=slice(None)):
    sums_ref[0:1, columns] += jnp.sum(first, axis=0, keepdims=True)
    sums_ref[1:2, columns] += jnp.sum(second, axis=0, keepdims=True)


def store_moved(stack_ref, start, value, dilation, columns=slice(None)):
    rows = pl.ds(start, PITCH)
    stack_ref[0, rows, columns] = pltpu.roll(value, dilation, 0).astype(BF16)
    stack_ref[1, rows, columns] = value.astype(BF16)
    stack_ref[2, rows, columns] = pltpu.roll(value, PITCH - dilation, 0).astype(BF16)


def clear_ends(stack_ref, rows):
    length = stack_ref.shape[1]
    empty = jnp.zeros((3, rows, stack_ref.shape[2]), BF16)
    stack_ref[:, 0:rows, :] = empty
    stack_ref[:, length - rows : length, :] = empty


def move_map(stack_ref, map_ref, dilation):
    clear_ends(stack_ref, dilation * PITCH)

    @pl.loop(0, 8)
    def _(r):
        at = pl.multiple_of(r * PITCH, 16)
        store_moved(
            stack_ref,
            pl.multiple_of(at + dilation * PITCH, 16),
            map_ref[pl.ds(at, PITCH), :].astype(F32),
            dilation,
        )


def times_turned(first, second):
    return lax.dot_general(first, second, (((1,), (1,)), ((), ())), preferred_element_type=F32)


def whole(shape):
    return pl.BlockSpec(shape, lambda *at: (0,) * len(shape), pipeline_mode=pl.Buffered(1))


def kept(shape):
    return pl.BlockSpec(shape, lambda *at: (0,) * len(shape))


SCALARS = pl.BlockSpec(memory_space=pltpu.SMEM)


def call(kernel, grid, in_specs, out_specs, outs, scratch, flops, *operands):
    moved = sum(a.size * a.dtype.itemsize for a in operands) if flops else 0
    return pl.pallas_call(
        kernel,
        grid=grid,
        in_specs=in_specs,
        out_specs=out_specs,
        out_shape=[jax.ShapeDtypeStruct(*o) for o in outs],
        scratch_shapes=scratch,
        compiler_params=pltpu.CompilerParams(vmem_limit_bytes=56 << 20),
        cost_estimate=pl.CostEstimate(flops=flops, bytes_accessed=moved, transcendentals=0),
    )(*operands)


def clear_image(image_ref):
    strip = 2 * PITCH
    empty = jnp.zeros((strip, image_ref.shape[1]), BF16)
    image_ref[0:strip, :] = empty
    image_ref[5 * strip : 6 * strip, :] = empty


def window_moved(stack_ref, image_ref, start, rows):
    @pl.loop(0, rows)
    def _(r):
        at = pl.multiple_of(r * PITCH, 16)
        value = image_ref[pl.ds(pl.multiple_of(start + at, 16), PITCH), :]
        store_moved(stack_ref, at, value.astype(F32), 2)


def dilated_kernel(
    count_ref, at_ref, value_ref, sums_ref, gain_ref, bias_ref, inside_ref, w_ref,
    out_ref, out_sums, image_out, value_out, image_ref, stack_ref, total_ref,
):
    tap = pl.program_id(0)
    strip = 2 * PITCH

    @pl.when(tap == 0)
    def _():
        clear_image(image_ref)
        mean, inverse = moments(sums_ref, count_ref[0])
        for k in range(4):
            start = pl.multiple_of(at_ref[k], 16)
            value = value_ref[k * strip : (k + 1) * strip, :]
            value_out[pl.ds(start, strip), :] = value
            normed = gain_ref[...] * ((value.astype(F32) - mean) * inverse) + bias_ref[...]
            act = (gelu(normed) * inside_ref[pl.ds(start, strip), :]).astype(BF16)
            image_ref[pl.ds(pl.multiple_of(start + strip, 16), strip), :] = act
            image_out[pl.ds(start, strip), :] = act
        window_moved(stack_ref, image_ref, 0, 12)
        total_ref[...] = jnp.zeros_like(total_ref)

    start = pl.multiple_of((tap // 3) * strip, 16)
    total_ref[...] += jnp.dot(
        stack_ref[tap % 3, pl.ds(start, 4 * strip), :], w_ref[...], preferred_element_type=F32
    )

    @pl.when(tap == 8)
    def _():
        out = total_ref[...].astype(BF16)
        out_ref[...] = out
        out = out.astype(F32)
        value = out * inside_ref[...]
        store_sums(out_sums, value, value * out)


def dilated_forward(count, at, value, sums, gain, bias, inside, weights, first_block):
    rows, deep = value.shape
    strip = 2 * PITCH
    operands = (value, sums, gain, bias, inside)
    return call(
        dilated_kernel,
        (9,),
        [SCALARS, SCALARS]
        + [whole(a.shape) for a in operands]
        + [pl.BlockSpec((deep, 512), lambda t: (0, first_block + t))],
        [kept((rows, 512)), kept((2, 512)), kept((rows, deep)), kept((rows, deep))],
        [((rows, 512), BF16), ((2, 512), F32), ((rows, deep), BF16), ((rows, deep), BF16)],
        [
            pltpu.VMEM((rows + 2 * strip, deep), BF16),
            pltpu.VMEM((3, rows + 2 * strip, deep), BF16),
            pltpu.VMEM((rows, 512), F32),
        ],
        18 * rows * deep * 512,
        count,
        at,
        *operands,
        weights,
    )


def expand_kernel(count_ref, value_ref, sums_ref, gain_ref, bias_ref, inside_ref, w_ref, act_ref, out_ref, out_sums):
    mean, inverse = moments(sums_ref, count_ref[0])
    normed = gain_ref[...] * ((value_ref[...].astype(F32) - mean) * inverse) + bias_ref[...]
    act = (gelu(normed) * inside_ref[...]).astype(BF16)
    act_ref[...] = act
    for c in range(4):
        columns = slice(c * 512, (c + 1) * 512)
        part = jnp.dot(act, w_ref[:, columns], preferred_element_type=F32).astype(BF16)
        out_ref[:, columns] = part
        part = part.astype(F32)
        out_sums[0:1, columns] = jnp.sum(part, axis=0, keepdims=True)
        out_sums[1:2, columns] = jnp.sum(part * part, axis=0, keepdims=True)


def expand_forward(count, value, sums, gain, bias, inside, weights):
    rows, deep = value.shape
    return call(
        expand_kernel,
        (1,),
        [SCALARS]
        + [whole(a.shape) for a in (value, sums, gain, bias, inside)]
        + [whole((deep, 2048))],
        [kept((rows, deep)), kept((rows, 2048)), kept((2, 2048))],
        [((rows, deep), BF16), ((rows, 2048), BF16), ((2, 2048), F32)],
        [],
        2 * rows * deep * 2048,
        count,
        value,
        sums,
        gain,
        bias,
        inside,
        weights,
    )


def trunk_kernel_forward(
    count_ref, at_ref, value_ref, base_keep, base_got, sums_ref, gain_ref, bias_ref, inside_ref,
    trunk_ref, slope_ref, steep_ref, base_out, turned_ref,
):
    mean, inverse = moments(sums_ref, count_ref[0])
    for k, bases in enumerate((base_keep, base_got)):

        @pl.loop(0, 4)
        def _(r):
            source = pl.ds(pl.multiple_of(r * PITCH, 16), PITCH)
            first = at_ref[2 * k + r // 2] + (r % 2) * PITCH
            first = pl.multiple_of(first, 16)
            rows = pl.ds(first, PITCH)
            inside = inside_ref[rows, :]
            for c in range(4):
                columns = slice(c * 512, (c + 1) * 512)
                centred = (value_ref[rows, columns].astype(F32) - mean[:, columns]) * inverse[:, columns]
                base = bases[source, columns]
                base_out[rows, columns] = base
                joined = gain_ref[:, columns] * centred + bias_ref[:, columns] + base.astype(F32)
                level, bend, squared = gelu_parts(joined)
                trunk = joined * level * inside
                slope = (
                    level + 0.5 * joined * (1.0 - bend * bend) * ROOT * (1.0 + 3.0 * CUBE * squared)
                ) * inside
                trunk_ref[rows, columns] = trunk.astype(BF16)
                slope_ref[rows, columns] = slope.astype(BF16)
                steep_ref[rows, columns] = (slope * centred).astype(BF16)

    for c in range(4):
        columns = slice(c * 512, (c + 1) * 512)
        turned_ref[columns, :] = trunk_ref[:, columns].T


def trunk_forward(count, at, value, base_keep, base_got, sums, gain, bias, inside):
    rows, deep = value.shape
    operands = (value, base_keep, base_got, sums, gain, bias, inside)
    return call(
        trunk_kernel_forward,
        (1,),
        [SCALARS, SCALARS] + [whole(a.shape) for a in operands],
        [whole((rows, deep))] * 4 + [whole((deep, rows))],
        [((rows, deep), BF16)] * 4 + [((deep, rows), BF16)],
        [],
        40 * rows * deep,
        count,
        at,
        *operands,
    )


def head_kernel(trunk_ref, inside_ref, w_ref, out_ref, out_sums, stack_ref):
    tap = pl.program_id(0)
    rows_all = out_ref.shape[0]

    @pl.when(tap == 0)
    def _():
        clear_ends(stack_ref, PITCH)

        @pl.loop(0, 8)
        def _(r):
            at = pl.multiple_of(r * PITCH, 16)
            for c in range(4):
                columns = slice(c * 512, (c + 1) * 512)
                store_moved(
                    stack_ref,
                    pl.multiple_of(at + PITCH, 16),
                    trunk_ref[pl.ds(at, PITCH), columns].astype(F32),
                    1,
                    columns,
                )

        out_ref[...] = jnp.zeros_like(out_ref)

    start = pl.multiple_of((tap // 3) * PITCH, 16)
    out_ref[...] += jnp.dot(
        stack_ref[tap % 3, pl.ds(start, rows_all), :], w_ref[...], preferred_element_type=F32
    )

    @pl.when(tap == 8)
    def _():
        value = out_ref[...] * inside_ref[...]
        store_sums(out_sums, value, value * out_ref[...])


def head_forward(trunk, inside, weights):
    rows, deep = trunk.shape
    return call(
        head_kernel,
        (9,),
        [whole((rows, deep)), whole(inside.shape), pl.BlockSpec((deep, 512), lambda t: (0, t))],
        [whole((rows, 512)), kept((2, 512))],
        [((rows, 512), F32), ((2, 512), F32)],
        [pltpu.VMEM((3, rows + 2 * PITCH, deep), BF16)],
        18 * rows * deep * 512,
        trunk,
        inside,
        weights,
    )


def message_kernel(
    count_ref, at_ref, ring_ref, y_ref, value_ref, sums_ref, gain_ref, bias_ref, inside_ref, w_ref, cot_keep, cot_got,
    task_ref, s0, s1, s2, s3, d_message_ref, d_logit_ref, d_norm_ref, out_sums,
    stack_ref, total_ref, gate_ref, streams_ref,
):
    rows_all, deep = value_ref.shape
    mean, inverse = moments(sums_ref, count_ref[0])
    gain, bias = gain_ref[...], bias_ref[...]
    number = y_ref[0]
    clear_ends(stack_ref, PITCH)

    def centred_at(rows):
        return (value_ref[rows, :] - mean) * inverse

    @pl.loop(0, 8)
    def _(r):
        at = pl.multiple_of(r * PITCH, 16)
        rows = pl.ds(at, PITCH)
        task = gelu(gain * centred_at(rows) + bias) * inside_ref[rows, :]
        task_ref[rows, :] = task.astype(BF16)
        store_moved(stack_ref, pl.multiple_of(at + PITCH, 16), task, 1)

    gate_ref[...] = jnp.dot(
        task_ref[...], w_ref[:, 9 * 512 : 10 * 512], preferred_element_type=F32
    )
    total_ref[...] = jnp.zeros_like(total_ref)

    @pl.loop(0, 9)
    def _(tap):
        start = pl.multiple_of((tap // 3) * PITCH, 16)
        total_ref[...] += jnp.dot(
            stack_ref[tap % 3, pl.ds(start, rows_all), :],
            w_ref[:, pl.ds(pl.multiple_of(tap * 512, 512), 512)],
            preferred_element_type=F32,
        )

    for k, cots in enumerate((cot_keep, cot_got)):

        @pl.loop(0, 4)
        def _(r):
            source = pl.ds(pl.multiple_of(r * PITCH, 16), PITCH)
            at = pl.multiple_of(at_ref[2 * k + r // 2] + (r % 2) * PITCH, 16)
            rows = pl.ds(at, PITCH)
            inside = inside_ref[rows, :]
            message = total_ref[rows, :]
            gate = 1.0 / (1.0 + jnp.exp(-gate_ref[rows, :]))
            cot_depth = cots[source, :deep].astype(F32) * inside
            cot_seg = cots[source, deep:].astype(F32) * inside
            receive = jnp.where(
                number == 0, cot_seg, jnp.where(number == 1, cot_depth, cot_depth + cot_seg)
            )
            direct = jnp.where(
                number == 0, cot_depth, jnp.where(number == 1, cot_seg, jnp.zeros_like(cot_seg))
            )
            task = task_ref[rows, :]
            gated = (gate * message).astype(BF16)
            streams_ref[rows, :deep] = jnp.where(number == 0, task, gated)
            streams_ref[rows, deep:] = jnp.where(number == 1, task, gated)
            d_logit_ref[rows, :] = (receive * message * gate * (1.0 - gate)).astype(BF16)
            d_message = receive * gate
            d_message_ref[rows, :] = d_message.astype(BF16)
            store_moved(stack_ref, pl.multiple_of(at + PITCH, 16), d_message, 1)
            total_ref[rows, :] = direct

    for k, stream_ref in enumerate((s0, s1, s2, s3)):
        first = pl.multiple_of(ring_ref[k], 16)
        stream_ref[...] = streams_ref[pl.ds(first, 2 * PITCH), :]

    total_ref[...] += times_turned(d_logit_ref[...], w_ref[:, 9 * 512 : 10 * 512])

    @pl.loop(0, 9)
    def _(tap):
        start = pl.multiple_of((2 - tap // 3) * PITCH, 16)
        total_ref[...] += times_turned(
            stack_ref[2 - tap % 3, pl.ds(start, rows_all), :],
            w_ref[:, pl.ds(pl.multiple_of(tap * 512, 512), 512)],
        )

    out_sums[...] = jnp.zeros_like(out_sums)

    @pl.loop(0, 8)
    def _(r):
        rows = pl.ds(pl.multiple_of(r * PITCH, 16), PITCH)
        centred = centred_at(rows)
        upstream = gelu_slope(gain * centred + bias) * total_ref[rows, :] * inside_ref[rows, :]
        d_norm_ref[rows, :] = upstream
        add_sums(out_sums, upstream * centred, upstream)


def message_stage(count, at, ring, y, value, sums, gain, bias, inside, weights, cot_keep, cot_got):
    rows, deep = value.shape
    return call(
        message_kernel,
        (1,),
        [SCALARS] * 4
        + [whole(a.shape) for a in (value, sums, gain, bias, inside, weights)]
        + [whole((rows // 2, 2 * deep))] * 2,
        [
            kept((rows, deep)),
            *[kept((rows // 4, 2 * deep))] * 4,
            kept((rows, deep)),
            kept((rows, deep)),
            kept((rows, deep)),
            kept((2, deep)),
        ],
        [
            ((rows, deep), BF16),
            *[((rows // 4, 2 * deep), BF16)] * 4,
            ((rows, deep), BF16),
            ((rows, deep), BF16),
            ((rows, deep), F32),
            ((2, deep), F32),
        ],
        [
            pltpu.VMEM((3, rows + 2 * PITCH, deep), BF16),
            pltpu.VMEM((rows, deep), F32),
            pltpu.VMEM((rows, deep), F32),
            pltpu.VMEM((rows, 2 * deep), BF16),
        ],
        40 * rows * deep * 512,
        count,
        at,
        ring,
        y,
        value,
        sums,
        gain,
        bias,
        inside,
        weights,
        cot_keep,
        cot_got,
    )


def weight_kernel(dilation, is_turned, x_ref, g_ref, *rest):
    *more, out_ref, turned_ref, stack_ref = rest
    tap = pl.program_id(0)
    rows = g_ref.shape[0]
    source_ref = x_ref if is_turned else turned_ref

    @pl.when(tap == 0)
    def _():
        if not is_turned:
            turned_ref[...] = x_ref[...].T
        move_map(stack_ref, g_ref, dilation)

    def product(g):
        return jnp.dot(source_ref[...], g, preferred_element_type=F32).astype(BF16)

    @pl.when(tap < 9)
    def _():
        start = pl.multiple_of((2 - tap // 3) * dilation * PITCH, 16)
        out_ref[...] = product(stack_ref[2 - tap % 3, pl.ds(start, rows), :])

    if more:

        @pl.when(tap == 9)
        def _():
            out_ref[...] = product(more[0][...])


def conv_weight(image, upstream, dilation, centre=(), is_turned=False):
    rows, wide = upstream.shape
    deep = image.size // rows
    blocks = 9 + len(centre)
    (out,) = call(
        functools.partial(weight_kernel, dilation, is_turned),
        (blocks,),
        [whole(image.shape), whole((rows, wide))] + [whole((rows, wide)) for a in centre],
        [pl.BlockSpec((deep, wide), lambda t: (0, t))],
        [((deep, blocks * wide), BF16)],
        [
            pltpu.VMEM((16, 128) if is_turned else (deep, rows), BF16),
            pltpu.VMEM((3, rows + 2 * dilation * PITCH, wide), BF16),
        ],
        2 * blocks * rows * deep * wide,
        image,
        upstream,
        *centre,
    )
    return out


def trunk_kernel(
    at_ref, g_ref, slope_ref, steep_ref, w_ref, o0, o1, o2, o3, sums_ref, stack_ref, turned_ref, total_ref, line_ref
):
    tap = pl.program_id(0)
    rows = g_ref.shape[0]

    @pl.when(tap == 0)
    def _():
        move_map(stack_ref, g_ref, 1)
        for k in range(9):
            start = (2 - k // 3) * PITCH
            turned_ref[k] = stack_ref[2 - k % 3, start : start + rows, :].T

    part = jnp.dot(w_ref[...], turned_ref[tap], preferred_element_type=F32)

    @pl.when(tap == 0)
    def _():
        total_ref[...] = part

    @pl.when(tap > 0)
    def _():
        total_ref[...] += part

    @pl.when(tap == 8)
    def _():
        for c in range(0, total_ref.shape[0], 512):
            columns = slice(c, c + 512)
            value = total_ref[columns, :].T
            line_ref[...] = value
            sums_ref[0:1, columns] = jnp.sum(
                value * steep_ref[:, columns].astype(F32), axis=0, keepdims=True
            )
            sums_ref[1:2, columns] = jnp.sum(
                value * slope_ref[:, columns].astype(F32), axis=0, keepdims=True
            )
            for k in range(4):
                start = pl.multiple_of(at_ref[k], 16)
                out_ref = (o0, o1, o2, o3)[k]
                out_ref[:, columns] = line_ref[pl.ds(start, rows // 4), :].astype(BF16)


def trunk_back(at, upstream, slope, steep, weights):
    rows, wide = upstream.shape
    deep = weights.shape[0]
    return call(
        trunk_kernel,
        (9,),
        [SCALARS, whole((rows, wide)), whole((rows, deep)), whole((rows, deep))]
        + [pl.BlockSpec((deep, wide), lambda t: (0, t))],
        [whole((rows // 4, deep))] * 4 + [kept((2, deep))],
        [((rows // 4, deep), BF16)] * 4 + [((2, deep), F32)],
        [
            pltpu.VMEM((3, rows + 2 * PITCH, wide), BF16),
            pltpu.VMEM((9, wide, rows), BF16),
            pltpu.VMEM((deep, rows), F32),
            pltpu.VMEM((rows, 512), F32),
        ],
        18 * rows * deep * wide,
        at,
        upstream,
        slope,
        steep,
        weights,
    )
def joined_kernel(
    count_ref, at_ref, own_ref, near_ref, far_ref, pre_ref, base_ref, sums_ref, gain_ref, bias_ref, inside_ref, back_ref,
    w_ref, low_ref, low_sums, low_gain, low_bias,
    d_joined_ref, c0, c1, c2, c3, d_norm_ref, out_sums, d_pre_ref,
):
    count = count_ref[0]
    mean, inverse = moments(sums_ref, count)
    inside = inside_ref[...]
    for c in range(4):
        columns = slice(c * 512, (c + 1) * 512)
        centred = (pre_ref[:, columns].astype(F32) - mean[:, columns]) * inverse[:, columns]
        gain = gain_ref[:, columns]
        joined = gain * centred + bias_ref[:, columns] + base_ref[:, columns].astype(F32)
        d_trunk = (
            own_ref[:, columns].astype(F32)
            + near_ref[:, columns].astype(F32)
            + far_ref[:, columns].astype(F32)
        )
        d_joined = gelu_slope(joined) * d_trunk * inside
        d_joined_ref[:, columns] = d_joined.astype(BF16)
        shift = (back_ref[1:2, columns] + centred * back_ref[0:1, columns]) / count
        d_pre_ref[:, columns] = (
            inside * gain * inverse[:, columns] * (d_joined - shift)
        ).astype(BF16)
    for k, part_ref in enumerate((c0, c1, c2, c3)):
        first = pl.multiple_of(at_ref[k] // (2 * PITCH) * 512, 512)
        part_ref[...] = d_pre_ref[:, pl.ds(first, 512)]
    d_act = times_turned(d_pre_ref[...], w_ref[...])
    mean, inverse = moments(low_sums, count)
    centred = (low_ref[...].astype(F32) - mean) * inverse
    upstream = gelu_slope(low_gain[...] * centred + low_bias[...]) * d_act * inside
    upstream = upstream.astype(BF16)
    d_norm_ref[...] = upstream
    upstream = upstream.astype(F32)
    store_sums(out_sums, upstream * centred, upstream)


def joined_back(count, at, pieces, pre, base, sums, gain, bias, inside, back, weights, low, low_sums, low_gain, low_bias):
    rows, deep = pre.shape
    narrow = low.shape[1]
    operands = (*pieces, pre, base, sums, gain, bias, inside, back)
    lower = (low, low_sums, low_gain, low_bias)
    out_d_joined, *columns, out_d_norm, out_sums = call(
        joined_kernel,
        (1,),
        [SCALARS, SCALARS]
        + [whole(a.shape) for a in pieces]
        + [whole(pre.shape)] * 2
        + [whole(a.shape) for a in operands[5:]]
        + [whole((narrow, deep))]
        + [whole(a.shape) for a in lower],
        [kept((rows, deep))] + [kept((rows, 512))] * 4 + [kept((rows, narrow)), kept((2, narrow))],
        [((rows, deep), BF16)]
        + [((rows, 512), BF16)] * 4
        + [((rows, narrow), BF16), ((2, narrow), F32)],
        [pltpu.VMEM((rows, deep), BF16)],
        2 * rows * deep * narrow,
        count,
        at,
        *operands,
        weights,
        *lower,
    )
    return out_d_joined, columns, out_d_norm, out_sums


def dilated_back_kernel(
    count_ref, at_ref, u0, u1, u2, u3, value_ref, sums_ref, back_ref, gain_ref, inside_ref,
    w_ref, low_ref, low_sums, low_gain, low_bias,
    d_norm_ref, out_sums, part_ref,
    image_ref, stack_ref, turned_ref, total_ref,
):
    tap = pl.program_id(0)
    strip = 2 * PITCH
    rows = value_ref.shape[0]
    count = count_ref[0]

    @pl.when(tap == 0)
    def _():
        clear_image(image_ref)
        mean, inverse = moments(sums_ref, count)
        for k, up in enumerate((u0, u1, u2, u3)):
            start = pl.multiple_of(at_ref[k], 16)
            centred = (value_ref[pl.ds(start, strip), :].astype(F32) - mean) * inverse
            shift = (back_ref[1:2, :] + centred * back_ref[0:1, :]) / count
            scale = inside_ref[pl.ds(start, strip), :] * (gain_ref[...] * inverse)
            lowered = (scale * (up[...].astype(F32) - shift)).astype(BF16)
            image_ref[pl.ds(pl.multiple_of(start + strip, 16), strip), :] = lowered
        window_moved(stack_ref, image_ref, 0, 12)
        mine = pl.multiple_of(at_ref[0] // strip * 128, 128)
        part_ref[...] = image_ref[strip : 5 * strip, pl.ds(mine, 128)]
        for k in range(9):
            start = (2 - k // 3) * strip
            turned_ref[k] = stack_ref[2 - k % 3, start : start + rows, :].T
        total_ref[...] = jnp.zeros_like(total_ref)

    total_ref[...] += jnp.dot(w_ref[...], turned_ref[tap], preferred_element_type=F32)

    @pl.when(tap == 8)
    def _():
        mean, inverse = moments(low_sums, count)
        centred = (low_ref[...].astype(F32) - mean) * inverse
        slope = gelu_slope(low_gain[...] * centred + low_bias[...])
        upstream = (slope * total_ref[...].T * inside_ref[...]).astype(BF16)
        d_norm_ref[...] = upstream
        upstream = upstream.astype(F32)
        store_sums(out_sums, upstream * centred, upstream)


def dilated_back(
    count, at, ups, value, sums, back, gain, inside, weights, first_block, low, low_sums, low_gain, low_bias
):
    rows, wide = value.shape
    strip = 2 * PITCH
    operands = (*ups, value, sums, back, gain, inside)
    lower = (low, low_sums, low_gain, low_bias)
    return call(
        dilated_back_kernel,
        (9,),
        [SCALARS, SCALARS]
        + [whole(a.shape) for a in operands]
        + [pl.BlockSpec((512, wide), lambda t: (0, first_block + t))]
        + [whole(a.shape) for a in lower],
        [kept((rows, 512)), kept((2, 512)), kept((rows, 128))],
        [((rows, 512), BF16), ((2, 512), F32), ((rows, 128), BF16)],
        [
            pltpu.VMEM((rows + 2 * strip, wide), BF16),
            pltpu.VMEM((3, rows + 2 * strip, wide), BF16),
            pltpu.VMEM((9, wide, rows), BF16),
            pltpu.VMEM((512, rows), F32),
        ],
        18 * rows * wide * 512,
        count,
        at,
        *operands,
        weights,
        *lower,
    )


def heads_kernel(at_ref, local_ref, *refs):
    *pieces, got_ref = refs[:5]
    outs = refs[5:]

    def put(k, value):
        first = 0
        for out_ref in outs:
            last = first + out_ref.shape[2]
            out_ref[at_ref[k]] = value[:, first:last].astype(F32)
            first = last

    @pl.when(local_ref[0] == 1)
    def _():
        for k, piece in enumerate(pieces):
            put(k, piece)

    @pl.when(local_ref[0] == 0)
    def _():
        for k in range(4):
            put(k, got_ref.at[k])


def heads_placed(at, local, pieces, got, widths):
    rows, deep = pieces[0].shape
    return call(
        heads_kernel,
        (1,),
        [SCALARS, SCALARS] + [whole((rows, deep))] * 4 + [whole((4, rows, deep))],
        [whole((4, rows, wide)) for wide in widths],
        [((4, rows, wide), F32) for wide in widths],
        [],
        0,
        at,
        local,
        *pieces,
        got,
    )


def sums_of(value):
    return jnp.stack([jnp.sum(value, axis=0), jnp.sum(value * value, axis=0)])


def centred_by(value, sums, count):
    mean = sums[0] / count
    inverse = lax.rsqrt(sums[1] / count - mean * mean + EPS)
    return (value.astype(F32) - mean) * inverse, inverse


def norm_back(upstream, value, sums, gain, inside, back, count):
    centred, inverse = centred_by(value, sums, count)
    return (
        inside * gain * inverse * (upstream.astype(F32) - (back[1] + centred * back[0]) / count)
    ).astype(BF16)


def turned_dot(first, second):
    return lax.dot_general(first, second, (((0,), (0,)), ((), ())), preferred_element_type=F32)


def strips_of(value):
    _, rows, across, deep = value.shape
    padded = jnp.pad(value[0], ((0, 0), (0, PITCH - across), (0, 0)))
    return padded.reshape(rows * PITCH, deep)


def maps_of(value, across):
    rows = value.shape[0] // PITCH
    return value.reshape(1, rows, PITCH, -1)[:, :, :across]


def shares_sent(value, axes):
    count = lax.axis_size(axes)
    return lax.all_to_all(
        value.reshape(count, value.shape[0] // count, value.shape[1]), axes, 0, 0
    )


def parts_summed(parts):
    return jnp.sum(parts.astype(F32), axis=0).astype(BF16)


def shards(
    features,
    image_size,
    reduce_weight,
    dilated_weight,
    expand_weight,
    head_weight,
    message_weight,
    gate_weight,
    bottleneck_gain,
    bottleneck_bias,
    expand_gain,
    expand_bias,
    head_gain,
    head_bias,
    depth_cotangent,
    seg_cotangent,
):
    ylo, core, yhi = (lax.axis_index(a) for a in ("ylo", "core", "yhi"))
    plane = lax.axis_index("x") * 4 + lax.axis_index("z")
    y = yhi * 2 + ylo
    strip = ylo * 2 + core
    width = features.shape[2]
    local = core == yhi

    count = jnp.sum(image_size[:, 0].astype(F32) * image_size[:, 1].astype(F32))
    count_here = count.reshape(1)

    def inside_of(sizes, image, first, rows):
        size = lax.dynamic_index_in_dim(sizes, image, 0, keepdims=False)
        at = jnp.arange(rows * PITCH, dtype=jnp.int32)
        valid = (first + at // PITCH < size[0]) & (at % PITCH < size[1])
        return valid.astype(F32)[:, None]

    length = 2 * PITCH
    head_at = (
        jnp.stack(
            [
                ylo * 2 + core,
                (1 - ylo) * 2 + core,
                ylo * 2 + 1 - core,
                (1 - ylo) * 2 + 1 - core,
            ]
        )
        * length
    ).astype(jnp.int32)
    ring_at = (jnp.stack([y, y ^ 1, y ^ 2, y ^ 3]) * length).astype(jnp.int32)

    group = [(i, i ^ 5) for i in range(8) if (i >> 1) & 1 == i & 1]

    def brought(mine, sent):
        return jnp.where(local, mine, lax.ppermute(sent, GROUP, group))

    def of_head(stacked, head):
        return lax.dynamic_index_in_dim(stacked, head, 0, keepdims=False)

    planes = 16

    deep = features.shape[3]
    same = yhi == core
    inside = inside_of(image_size, plane * 2 + yhi, strip * 2, 2)
    base = strips_of(features) * inside.astype(BF16)
    near, far = beside_y(base)
    channels = expand_weight.shape[0]
    wide_trunk = expand_weight.shape[1] + dilated_weight.shape[1]
    first_weights = jnp.concatenate(
        [expand_weight, dilated_weight, reduce_weight.reshape(channels, -1)], axis=1
    )
    first_part = brought(first_weights, first_weights)
    reduce_part = first_part[:, wide_trunk:].reshape(reduce_weight.shape)
    copies, sizes_first = hold(
        jnp.broadcast_to(reduce_part[None], (planes,) + reduce_part.shape), image_size
    )
    reduce_half = lax.all_to_all(copies, ("x", "z"), 0, 0)
    whole_reduce = jnp.stack(
        in_order(reduce_half, over_core(reduce_half), core), axis=1
    ).reshape(-1, reduce_weight.shape[1])
    whole_trunk = lax.all_gather(first_part[:, :wide_trunk], POOL, axis=0, tiled=True)
    first_tap = expand_weight.shape[1] // 512
    inside_whole = inside_of(sizes_first, plane * 2 + core, 0, 8)

    def spread(own, near, across_low, across_high, far):
        mine = jnp.concatenate([own, near])
        other = jnp.concatenate([across_low, across_high, far])
        return jnp.where(same, mine, other), over_core(jnp.where(same, other, mine))

    near, far, y_first = hold(near, far, y)
    head_part = brought(of_head(head_weight, y_first), of_head(head_weight, y_first ^ 3))
    base_keep, base_got = spread(base, near, *across_y(near, far), far)
    whole_reduce, base_keep, base_got, inside_whole, head_part = hold(
        whole_reduce, base_keep, base_got, inside_whole, head_part
    )
    whole_head = lax.all_gather(head_part, POOL, axis=0, tiled=True)

    pre_one = jnp.concatenate(
        [
            jnp.dot(a, whole_reduce, preferred_element_type=F32).astype(BF16)
            for a in (base_keep, base_got)
        ]
    )
    sums_one = fold(sums_of(pre_one.astype(F32)), CORE, *LINE, *PLANE)
    pre_two, sums_two, act_one_image, pre_one_image = dilated_forward(
        count_here,
        head_at,
        pre_one,
        sums_one,
        bottleneck_gain[:1],
        bottleneck_bias[:1],
        inside_whole,
        whole_trunk,
        first_tap,
    )
    sums_two = fold(sums_two, CORE, *LINE)
    sums_two, y_later, depth_cots, seg_cots = hold(sums_two, y, depth_cotangent, seg_cotangent)
    task_weights = jnp.concatenate([message_weight, gate_weight], axis=2)
    task_part = brought(of_head(task_weights, y_later), of_head(task_weights, y_later ^ 3))
    cots = jnp.concatenate([strips_of(depth_cots), strips_of(seg_cots)], axis=1)
    near, far = beside_y(cots)
    sums_two = fold(sums_two, *PLANE)
    act_two, pre_three, sums_three = expand_forward(
        count_here,
        pre_two,
        sums_two,
        bottleneck_gain[1:],
        bottleneck_bias[1:],
        inside_whole,
        whole_trunk,
    )
    sums_three, task_part = hold(fold(sums_three, CORE, *LINE), task_part)
    whole_task = lax.all_gather(task_part, POOL, axis=0, tiled=True)
    sums_three = fold(sums_three, *PLANE)

    gain_here, bias_here = of_head(head_gain, y)[None], of_head(head_bias, y)[None]
    wide_gain, wide_bias = expand_gain[None], expand_bias[None]
    trunk, slope, steep, base_image, trunk_turned = trunk_forward(
        count_here,
        head_at,
        pre_three,
        base_keep,
        base_got,
        sums_three,
        wide_gain,
        wide_bias,
        inside_whole,
    )
    trunk, near, far = hold(trunk, near, far)
    across_low, across_high = across_y(near, far)
    pre_head, sums_head = head_forward(trunk, inside_whole, whole_head)
    sums_head, near, far, across_low, across_high = hold(
        sums_head, near, far, across_low, across_high
    )
    cots_keep, cots_got = spread(cots, near, across_low, across_high, far)
    sums_head = fold(sums_head, CORE, *LINE, *PLANE)
    task, *streams, d_message, d_logit, d_norm_head, back_here = message_stage(
        count_here,
        head_at,
        ring_at,
        y.astype(jnp.int32).reshape(1),
        pre_head,
        sums_head,
        gain_here,
        bias_here,
        inside_whole,
        whole_task,
        cots_keep,
        cots_got,
    )
    back_head = fold(back_here, CORE, *LINE, *PLANE)
    back_head, streams = hold(back_head, streams)
    d_pre_head = norm_back(
        d_norm_head, pre_head, sums_head, gain_here, inside_whole, back_head, count
    )
    own, near, across, far = streams
    from_near, from_far = half_way(across)
    head_grad = conv_weight(trunk_turned, d_pre_head, 1, is_turned=True)
    head_grad, d_pre_head, from_near, from_far = hold(head_grad, d_pre_head, from_near, from_far)
    head_share = lax.psum_scatter(head_grad, POOL, scatter_dimension=0, tiled=True)
    streams = last_way(own, near, far, from_near, from_far)
    *d_trunk, back_three = trunk_back(ring_at, d_pre_head, slope, steep, whole_head)
    d_trunk, back_three, streams = hold(d_trunk, back_three, streams)
    placed = jnp.where(
        jnp.arange(4)[None, :, None] == y, back_here[:, None], jnp.zeros((1, 1, 1), F32)
    ).reshape(2, -1)
    back_wide = jnp.concatenate([back_three, placed], axis=1)
    own, near, across, far = d_trunk
    from_near, from_far = half_way(across)
    back_wide, from_near, from_far = hold(fold(back_wide, CORE, *LINE), from_near, from_far)
    pieces = last_way(own, near, far, from_near, from_far)
    back_wide = fold(back_wide, *PLANE)
    def strip_of(value):
        return lax.dynamic_slice_in_dim(value, y * length, length, 0)

    pre_two_strip, pre_three_strip, base_strip, inside_strip = (
        strip_of(a) for a in (pre_two, pre_three, base_image, inside_whole)
    )

    def ring_order(value):
        return jnp.concatenate(
            [
                lax.dynamic_slice_in_dim(value, (y ^ flip) * length, length, 0)
                for flip in range(4)
            ]
        )

    act_two_ring = ring_order(act_two)
    task_grad = conv_weight(task, d_message, 1, (d_logit,))
    (
        back_wide,
        pieces,
        pre_two_strip,
        pre_three_strip,
        base_strip,
        inside_strip,
        act_two_ring,
        task_grad,
    ) = hold(
        back_wide,
        pieces,
        pre_two_strip,
        pre_three_strip,
        base_strip,
        inside_strip,
        act_two_ring,
        task_grad,
    )
    task_share = lax.psum_scatter(task_grad, POOL, scatter_dimension=0, tiled=True)
    back_wide = fold(back_wide, *RIDGE)
    back_three, back_heads = back_wide[:, :deep], back_wide[:, deep:]
    d_joined, d_three_parts, d_norm_two, back_two = joined_back(
        count_here,
        ring_at,
        pieces,
        pre_three_strip,
        base_strip,
        sums_three,
        wide_gain,
        wide_bias,
        inside_strip,
        back_three,
        whole_trunk,
        pre_two_strip,
        sums_two,
        bottleneck_gain[1:],
        bottleneck_bias[1:],
    )
    back_two = fold(back_two, CORE, *LINE)
    back_two, d_norm_twos = hold(back_two, around_y(d_norm_two))
    back_two = fold(back_two, *PLANE, *RIDGE)

    d_three_part = jnp.concatenate(for_me(d_three_parts))
    grad_expand = turned_dot(act_two_ring, d_three_part).astype(BF16)
    back_two, grad_expand, d_joined = hold(back_two, grad_expand, d_joined)
    homeward = sent_home(
        jnp.concatenate([d_joined, sum(a.astype(F32) for a in streams).astype(BF16)], axis=1)
    )
    d_norm_one, back_one, d_two_part = dilated_back(
        count_here,
        ring_at,
        d_norm_twos,
        pre_two,
        sums_two,
        back_two,
        bottleneck_gain[1:],
        inside_whole,
        whole_trunk,
        first_tap,
        pre_one_image,
        sums_one,
        bottleneck_gain[:1],
        bottleneck_bias[:1],
    )
    def to_chips(share):
        pieces = [share]
        for flip in (1, 2, 3):
            pairs = []
            for i in range(8):
                low, c, high = i >> 2, (i >> 1) & 1, i & 1
                to = (high * 2 + low) ^ flip
                if to >> 1 == c:
                    pairs.append((i, ((to & 1) << 2) | (c << 1) | (to >> 1)))
            pieces.append(lax.ppermute(share, GROUP, pairs))
        return tuple(pieces)

    heads_at = jnp.stack([y, y ^ 1, y ^ 2, y ^ 3]).astype(jnp.int32)
    local_here = local.astype(jnp.int32).reshape(1)

    def to_cores(pieces, *widths):
        pairs = [(i, i ^ 2) for i in range(8) if (i >> 1) & 1 == i & 1]
        got = lax.ppermute(jnp.stack(pieces), GROUP, pairs)
        return heads_placed(heads_at, local_here, pieces, got, widths)

    back_one = fold(back_one, CORE, *LINE)
    grad_dilated = conv_weight(act_one_image, d_two_part, 2)
    trunk_grad = jnp.concatenate([grad_expand, grad_dilated], axis=1)
    back_one, trunk_grad, homeward, head_share = hold(back_one, trunk_grad, homeward, head_share)
    head_pieces = to_chips(head_share)
    back_one = fold(back_one, *PLANE)
    d_pre_one = norm_back(
        d_norm_one, pre_one_image, sums_one, bottleneck_gain[0], inside_whole, back_one, count
    )
    grad_reduce = turned_dot(
        base_image, lax.dynamic_slice_in_dim(d_pre_one, y * 128, 128, 1)
    ).astype(BF16)
    trunk_grad = jnp.concatenate(
        [trunk_grad, grad_reduce.reshape(trunk_grad.shape[0], -1)], axis=1
    )
    trunk_grad, head_pieces, d_pre_one = hold(trunk_grad, head_pieces, d_pre_one)
    trunk_parts = shares_sent(trunk_grad, POOL)
    wide = message_weight.shape[2]
    (sum_head,) = to_cores(head_pieces, wide)
    d_pre_one = sent_home(strip_of(d_pre_one))
    d_base = homeward[:, :deep].astype(F32) + times_turned(d_pre_one, whole_reduce)
    input_grad = maps_of(d_base * inside, width)
    trunk_parts, sum_head, input_grad, task_share = hold(
        trunk_parts, sum_head, input_grad, task_share
    )
    small_share = jnp.concatenate([task_share, parts_summed(trunk_parts)], axis=1)
    sum_message, sum_gate, all_trunk, all_reduce = to_cores(
        to_chips(small_share), wide, gate_weight.shape[2], trunk_grad.shape[1] - 512, 512
    )
    sum_expand = jnp.moveaxis(all_trunk[:, :, :512], 0, 1).reshape(channels, -1)
    sum_dilated = jnp.moveaxis(
        all_trunk[:, :, 512:].reshape(4, channels, 9, 128), 0, 2
    ).reshape(channels, -1)
    sum_reduce = jnp.moveaxis(all_reduce.reshape(4, -1, 128), 0, 1).reshape(-1, 512)


    streams = maps_of(homeward[:, deep:].astype(F32) * inside, width)
    depth_out, seg_out = jnp.split(streams, 2, axis=3)

    return (
        depth_out,
        seg_out,
        input_grad,
        sum_reduce,
        sum_dilated,
        sum_expand,
        sum_head,
        sum_message,
        sum_gate,
        jnp.stack([back_one[0], back_two[0]]),
        jnp.stack([back_one[1], back_two[1]]),
        back_three[0],
        back_three[1],
        back_heads[0].reshape(4, -1),
        back_heads[1].reshape(4, -1),
    )


def solution(mesh):
    fine = Mesh(mesh.devices.reshape(2, 2, 4, 4, 2), FINE)
    maps = P(IMG, ROWS, None, None)
    placed = (
        maps,
        P(),
        P(IMG, None),
        P(IMG, None),
        P(IMG, None),
        P(None, IMG, None),
        P(None, IMG, None),
        P(None, IMG, None),
        P(),
        P(),
        P(),
        P(),
        P(),
        P(),
        maps,
        maps,
    )
    return jax.shard_map(
        shards,
        mesh=fine,
        in_specs=placed,
        out_specs=(
            maps,
            maps,
            maps,
            P(IMG, None),
            P(IMG, None),
            P(IMG, None),
            P(None, IMG, None),
            P(None, IMG, None),
            P(None, IMG, None),
            P(),
            P(),
            P(),
            P(),
            P(),
            P(),
        ),
        check_vma=False,
    )
```

```python
import functools

import jax
import jax.numpy as jnp
from jax import lax
from jax.experimental import pallas as pl
from jax.experimental.pallas import tpu as pltpu
from jax.sharding import Mesh, PartitionSpec as P

EPS = 1e-05
PITCH = 80
ROOT = 0.7978845608028654
CUBE = 0.044715
F32 = jnp.float32
BF16 = jnp.bfloat16

FINE = ("ylo", "core", "x", "z", "yhi")
ROWS = ("ylo", "core")
IMG = ("x", "z", "yhi")
RING = ("ylo", "yhi")
GROUP = ("ylo", "core", "yhi")
POOL = ("x", "z", "core")


def swap(value, axis, flip):
    count = lax.axis_size(axis)
    return lax.ppermute(value, axis, [(i, i ^ flip) for i in range(count)])


def over_core(value):
    return swap(value, "core", 1)


def over_y(value, flip):
    return swap(value, RING, {1: 2, 2: 1, 3: 3}[flip])


def fold(value, *partners):
    for axis, flip in partners:
        value = value + (over_y(value, flip) if axis == "y" else swap(value, axis, flip))
    return value


CORE, LINE, PLANE, RIDGE = ("core", 1), (("x", 1), ("x", 3)), (("z", 1), ("z", 3)), (("y", 1), ("y", 3))


def hold(*arrays):
    return lax.optimization_barrier(arrays)


def in_order(mine, other, bit):
    first = bit == 0
    return jnp.where(first, mine, other), jnp.where(first, other, mine)


def around_y(value):
    return value, over_y(value, 1), over_y(value, 2), over_y(value, 3)


def for_me(parts):
    own, near, across, far = parts
    return own, over_y(near, 1), over_y(across, 2), over_y(far, 3)


HOME = [(i, ((i & 1) << 2) | (((i >> 2) & 1) << 1) | ((i >> 1) & 1)) for i in range(8)]


def sent_home(value):
    return lax.ppermute(value, GROUP, HOME)


def beside_y(value):
    return over_y(value, 1), over_y(value, 3)


def across_y(near, far):
    half = near.shape[0] // 2
    return over_y(far[:half], 1), over_y(near[half:], 3)


def half_way(across):
    half = across.shape[0] // 2
    return over_y(across[:half], 1), over_y(across[half:], 3)


def last_way(own, near, far, from_near, from_far):
    half = own.shape[0] // 2
    near = jnp.concatenate(
        [near[:half], (near[half:].astype(F32) + from_far.astype(F32)).astype(BF16)]
    )
    far = jnp.concatenate(
        [(far[:half].astype(F32) + from_near.astype(F32)).astype(BF16), far[half:]]
    )
    return own, over_y(near, 1), over_y(far, 3)


def gelu_parts(value):
    squared = value * value
    bend = jnp.tanh(ROOT * value * (1.0 + CUBE * squared))
    return 0.5 * (1.0 + bend), bend, squared


def gelu(value):
    return value * gelu_parts(value)[0]


def gelu_slope(value):
    level, bend, squared = gelu_parts(value)
    return level + 0.5 * value * (1.0 - bend * bend) * ROOT * (1.0 + 3.0 * CUBE * squared)


def moments(sums_ref, count):
    mean = sums_ref[0:1, :] / count
    return mean, lax.rsqrt(sums_ref[1:2, :] / count - mean * mean + EPS)


def store_sums(sums_ref, first, second):
    sums_ref[0:1, :] = jnp.sum(first, axis=0, keepdims=True)
    sums_ref[1:2, :] = jnp.sum(second, axis=0, keepdims=True)


def add_sums(sums_ref, first, second, columns=slice(None)):
    sums_ref[0:1, columns] += jnp.sum(first, axis=0, keepdims=True)
    sums_ref[1:2, columns] += jnp.sum(second, axis=0, keepdims=True)


def store_moved(stack_ref, start, value, dilation, columns=slice(None)):
    rows = pl.ds(start, PITCH)
    stack_ref[0, rows, columns] = pltpu.roll(value, dilation, 0).astype(BF16)
    stack_ref[1, rows, columns] = value.astype(BF16)
    stack_ref[2, rows, columns] = pltpu.roll(value, PITCH - dilation, 0).astype(BF16)


def clear_ends(stack_ref, rows):
    length = stack_ref.shape[1]
    empty = jnp.zeros((3, rows, stack_ref.shape[2]), BF16)
    stack_ref[:, 0:rows, :] = empty
    stack_ref[:, length - rows : length, :] = empty


def move_map(stack_ref, map_ref, dilation):
    clear_ends(stack_ref, dilation * PITCH)

    @pl.loop(0, 8)
    def _(r):
        at = pl.multiple_of(r * PITCH, 16)
        store_moved(
            stack_ref,
            pl.multiple_of(at + dilation * PITCH, 16),
            map_ref[pl.ds(at, PITCH), :].astype(F32),
            dilation,
        )


def times_turned(first, second):
    return lax.dot_general(first, second, (((1,), (1,)), ((), ())), preferred_element_type=F32)


def whole(shape):
    return pl.BlockSpec(shape, lambda *at: (0,) * len(shape), pipeline_mode=pl.Buffered(1))


def kept(shape):
    return pl.BlockSpec(shape, lambda *at: (0,) * len(shape))


SCALARS = pl.BlockSpec(memory_space=pltpu.SMEM)


def call(kernel, grid, in_specs, out_specs, outs, scratch, flops, *operands):
    moved = sum(a.size * a.dtype.itemsize for a in operands) if flops else 0
    return pl.pallas_call(
        kernel,
        grid=grid,
        in_specs=in_specs,
        out_specs=out_specs,
        out_shape=[jax.ShapeDtypeStruct(*o) for o in outs],
        scratch_shapes=scratch,
        compiler_params=pltpu.CompilerParams(vmem_limit_bytes=56 << 20),
        cost_estimate=pl.CostEstimate(flops=flops, bytes_accessed=moved, transcendentals=0),
    )(*operands)


def clear_image(image_ref):
    strip = 2 * PITCH
    empty = jnp.zeros((strip, image_ref.shape[1]), BF16)
    image_ref[0:strip, :] = empty
    image_ref[5 * strip : 6 * strip, :] = empty


def window_moved(stack_ref, image_ref, start, rows):
    @pl.loop(0, rows)
    def _(r):
        at = pl.multiple_of(r * PITCH, 16)
        value = image_ref[pl.ds(pl.multiple_of(start + at, 16), PITCH), :]
        store_moved(stack_ref, at, value.astype(F32), 2)


def dilated_kernel(
    count_ref, at_ref, value_ref, sums_ref, gain_ref, bias_ref, inside_ref, w_ref,
    out_ref, out_sums, image_out, value_out, image_ref, stack_ref, total_ref,
):
    tap = pl.program_id(0)
    strip = 2 * PITCH

    @pl.when(tap == 0)
    def _():
        clear_image(image_ref)
        mean, inverse = moments(sums_ref, count_ref[0])
        for k in range(4):
            start = pl.multiple_of(at_ref[k], 16)
            value = value_ref[k * strip : (k + 1) * strip, :]
            value_out[pl.ds(start, strip), :] = value
            normed = gain_ref[...] * ((value.astype(F32) - mean) * inverse) + bias_ref[...]
            act = (gelu(normed) * inside_ref[pl.ds(start, strip), :]).astype(BF16)
            image_ref[pl.ds(pl.multiple_of(start + strip, 16), strip), :] = act
            image_out[pl.ds(start, strip), :] = act
        window_moved(stack_ref, image_ref, 0, 12)
        total_ref[...] = jnp.zeros_like(total_ref)

    start = pl.multiple_of((tap // 3) * strip, 16)
    total_ref[...] += jnp.dot(
        stack_ref[tap % 3, pl.ds(start, 4 * strip), :], w_ref[...], preferred_element_type=F32
    )

    @pl.when(tap == 8)
    def _():
        out = total_ref[...].astype(BF16)
        out_ref[...] = out
        out = out.astype(F32)
        value = out * inside_ref[...]
        store_sums(out_sums, value, value * out)


def dilated_forward(count, at, value, sums, gain, bias, inside, weights, first_block):
    rows, deep = value.shape
    strip = 2 * PITCH
    operands = (value, sums, gain, bias, inside)
    return call(
        dilated_kernel,
        (9,),
        [SCALARS, SCALARS]
        + [whole(a.shape) for a in operands]
        + [pl.BlockSpec((deep, 512), lambda t: (0, first_block + t))],
        [kept((rows, 512)), kept((2, 512)), kept((rows, deep)), kept((rows, deep))],
        [((rows, 512), BF16), ((2, 512), F32), ((rows, deep), BF16), ((rows, deep), BF16)],
        [
            pltpu.VMEM((rows + 2 * strip, deep), BF16),
            pltpu.VMEM((3, rows + 2 * strip, deep), BF16),
            pltpu.VMEM((rows, 512), F32),
        ],
        18 * rows * deep * 512,
        count,
        at,
        *operands,
        weights,
    )


def expand_kernel(count_ref, value_ref, sums_ref, gain_ref, bias_ref, inside_ref, w_ref, act_ref, out_ref, out_sums):
    mean, inverse = moments(sums_ref, count_ref[0])
    normed = gain_ref[...] * ((value_ref[...].astype(F32) - mean) * inverse) + bias_ref[...]
    act = (gelu(normed) * inside_ref[...]).astype(BF16)
    act_ref[...] = act
    for c in range(4):
        columns = slice(c * 512, (c + 1) * 512)
        part = jnp.dot(act, w_ref[:, columns], preferred_element_type=F32).astype(BF16)
        out_ref[:, columns] = part
        part = part.astype(F32)
        out_sums[0:1, columns] = jnp.sum(part, axis=0, keepdims=True)
        out_sums[1:2, columns] = jnp.sum(part * part, axis=0, keepdims=True)


def expand_forward(count, value, sums, gain, bias, inside, weights):
    rows, deep = value.shape
    return call(
        expand_kernel,
        (1,),
        [SCALARS]
        + [whole(a.shape) for a in (value, sums, gain, bias, inside)]
        + [whole((deep, 2048))],
        [kept((rows, deep)), kept((rows, 2048)), kept((2, 2048))],
        [((rows, deep), BF16), ((rows, 2048), BF16), ((2, 2048), F32)],
        [],
        2 * rows * deep * 2048,
        count,
        value,
        sums,
        gain,
        bias,
        inside,
        weights,
    )


def trunk_kernel_forward(
    count_ref, at_ref, value_ref, base_keep, base_got, sums_ref, gain_ref, bias_ref, inside_ref,
    trunk_ref, slope_ref, steep_ref, base_out, turned_ref,
):
    mean, inverse = moments(sums_ref, count_ref[0])
    for k, bases in enumerate((base_keep, base_got)):

        @pl.loop(0, 4)
        def _(r):
            source = pl.ds(pl.multiple_of(r * PITCH, 16), PITCH)
            first = at_ref[2 * k + r // 2] + (r % 2) * PITCH
            first = pl.multiple_of(first, 16)
            rows = pl.ds(first, PITCH)
            inside = inside_ref[rows, :]
            for c in range(4):
                columns = slice(c * 512, (c + 1) * 512)
                centred = (value_ref[rows, columns].astype(F32) - mean[:, columns]) * inverse[:, columns]
                base = bases[source, columns]
                base_out[rows, columns] = base
                joined = gain_ref[:, columns] * centred + bias_ref[:, columns] + base.astype(F32)
                level, bend, squared = gelu_parts(joined)
                trunk = joined * level * inside
                slope = (
                    level + 0.5 * joined * (1.0 - bend * bend) * ROOT * (1.0 + 3.0 * CUBE * squared)
                ) * inside
                trunk_ref[rows, columns] = trunk.astype(BF16)
                slope_ref[rows, columns] = slope.astype(BF16)
                steep_ref[rows, columns] = (slope * centred).astype(BF16)

    for c in range(4):
        columns = slice(c * 512, (c + 1) * 512)
        turned_ref[columns, :] = trunk_ref[:, columns].T


def trunk_forward(count, at, value, base_keep, base_got, sums, gain, bias, inside):
    rows, deep = value.shape
    operands = (value, base_keep, base_got, sums, gain, bias, inside)
    return call(
        trunk_kernel_forward,
        (1,),
        [SCALARS, SCALARS] + [whole(a.shape) for a in operands],
        [whole((rows, deep))] * 4 + [whole((deep, rows))],
        [((rows, deep), BF16)] * 4 + [((deep, rows), BF16)],
        [],
        40 * rows * deep,
        count,
        at,
        *operands,
    )


def head_kernel(trunk_ref, inside_ref, w_ref, out_ref, out_sums, stack_ref):
    tap = pl.program_id(0)
    rows_all = out_ref.shape[0]

    @pl.when(tap == 0)
    def _():
        clear_ends(stack_ref, PITCH)

        @pl.loop(0, 8)
        def _(r):
            at = pl.multiple_of(r * PITCH, 16)
            for c in range(4):
                columns = slice(c * 512, (c + 1) * 512)
                store_moved(
                    stack_ref,
                    pl.multiple_of(at + PITCH, 16),
                    trunk_ref[pl.ds(at, PITCH), columns].astype(F32),
                    1,
                    columns,
                )

        out_ref[...] = jnp.zeros_like(out_ref)

    start = pl.multiple_of((tap // 3) * PITCH, 16)
    out_ref[...] += jnp.dot(
        stack_ref[tap % 3, pl.ds(start, rows_all), :], w_ref[...], preferred_element_type=F32
    )

    @pl.when(tap == 8)
    def _():
        value = out_ref[...] * inside_ref[...]
        store_sums(out_sums, value, value * out_ref[...])


def head_forward(trunk, inside, weights):
    rows, deep = trunk.shape
    return call(
        head_kernel,
        (9,),
        [whole((rows, deep)), whole(inside.shape), pl.BlockSpec((deep, 512), lambda t: (0, t))],
        [whole((rows, 512)), kept((2, 512))],
        [((rows, 512), F32), ((2, 512), F32)],
        [pltpu.VMEM((3, rows + 2 * PITCH, deep), BF16)],
        18 * rows * deep * 512,
        trunk,
        inside,
        weights,
    )


def message_kernel(
    count_ref, at_ref, ring_ref, y_ref, value_ref, sums_ref, gain_ref, bias_ref, inside_ref, w_ref, cot_keep, cot_got,
    task_ref, s0, s1, s2, s3, d_message_ref, d_logit_ref, d_norm_ref, out_sums,
    stack_ref, total_ref, gate_ref, streams_ref,
):
    rows_all, deep = value_ref.shape
    mean, inverse = moments(sums_ref, count_ref[0])
    gain, bias = gain_ref[...], bias_ref[...]
    number = y_ref[0]
    clear_ends(stack_ref, PITCH)

    def centred_at(rows):
        return (value_ref[rows, :] - mean) * inverse

    @pl.loop(0, 8)
    def _(r):
        at = pl.multiple_of(r * PITCH, 16)
        rows = pl.ds(at, PITCH)
        task = gelu(gain * centred_at(rows) + bias) * inside_ref[rows, :]
        task_ref[rows, :] = task.astype(BF16)
        store_moved(stack_ref, pl.multiple_of(at + PITCH, 16), task, 1)

    gate_ref[...] = jnp.dot(
        task_ref[...], w_ref[:, 9 * 512 : 10 * 512], preferred_element_type=F32
    )
    total_ref[...] = jnp.zeros_like(total_ref)

    @pl.loop(0, 9)
    def _(tap):
        start = pl.multiple_of((tap // 3) * PITCH, 16)
        total_ref[...] += jnp.dot(
            stack_ref[tap % 3, pl.ds(start, rows_all), :],
            w_ref[:, pl.ds(pl.multiple_of(tap * 512, 512), 512)],
            preferred_element_type=F32,
        )

    for k, cots in enumerate((cot_keep, cot_got)):

        @pl.loop(0, 4)
        def _(r):
            source = pl.ds(pl.multiple_of(r * PITCH, 16), PITCH)
            at = pl.multiple_of(at_ref[2 * k + r // 2] + (r % 2) * PITCH, 16)
            rows = pl.ds(at, PITCH)
            inside = inside_ref[rows, :]
            message = total_ref[rows, :]
            gate = 1.0 / (1.0 + jnp.exp(-gate_ref[rows, :]))
            cot_depth = cots[source, :deep].astype(F32) * inside
            cot_seg = cots[source, deep:].astype(F32) * inside
            receive = jnp.where(
                number == 0, cot_seg, jnp.where(number == 1, cot_depth, cot_depth + cot_seg)
            )
            direct = jnp.where(
                number == 0, cot_depth, jnp.where(number == 1, cot_seg, jnp.zeros_like(cot_seg))
            )
            task = task_ref[rows, :]
            gated = (gate * message).astype(BF16)
            streams_ref[rows, :deep] = jnp.where(number == 0, task, gated)
            streams_ref[rows, deep:] = jnp.where(number == 1, task, gated)
            d_logit_ref[rows, :] = (receive * message * gate * (1.0 - gate)).astype(BF16)
            d_message = receive * gate
            d_message_ref[rows, :] = d_message.astype(BF16)
            store_moved(stack_ref, pl.multiple_of(at + PITCH, 16), d_message, 1)
            total_ref[rows, :] = direct

    for k, stream_ref in enumerate((s0, s1, s2, s3)):
        first = pl.multiple_of(ring_ref[k], 16)
        stream_ref[...] = streams_ref[pl.ds(first, 2 * PITCH), :]

    total_ref[...] += times_turned(d_logit_ref[...], w_ref[:, 9 * 512 : 10 * 512])

    @pl.loop(0, 9)
    def _(tap):
        start = pl.multiple_of((2 - tap // 3) * PITCH, 16)
        total_ref[...] += times_turned(
            stack_ref[2 - tap % 3, pl.ds(start, rows_all), :],
            w_ref[:, pl.ds(pl.multiple_of(tap * 512, 512), 512)],
        )

    out_sums[...] = jnp.zeros_like(out_sums)

    @pl.loop(0, 8)
    def _(r):
        rows = pl.ds(pl.multiple_of(r * PITCH, 16), PITCH)
        centred = centred_at(rows)
        upstream = gelu_slope(gain * centred + bias) * total_ref[rows, :] * inside_ref[rows, :]
        d_norm_ref[rows, :] = upstream
        add_sums(out_sums, upstream * centred, upstream)


def message_stage(count, at, ring, y, value, sums, gain, bias, inside, weights, cot_keep, cot_got):
    rows, deep = value.shape
    return call(
        message_kernel,
        (1,),
        [SCALARS] * 4
        + [whole(a.shape) for a in (value, sums, gain, bias, inside, weights)]
        + [whole((rows // 2, 2 * deep))] * 2,
        [
            kept((rows, deep)),
            *[kept((rows // 4, 2 * deep))] * 4,
            kept((rows, deep)),
            kept((rows, deep)),
            kept((rows, deep)),
            kept((2, deep)),
        ],
        [
            ((rows, deep), BF16),
            *[((rows // 4, 2 * deep), BF16)] * 4,
            ((rows, deep), BF16),
            ((rows, deep), BF16),
            ((rows, deep), F32),
            ((2, deep), F32),
        ],
        [
            pltpu.VMEM((3, rows + 2 * PITCH, deep), BF16),
            pltpu.VMEM((rows, deep), F32),
            pltpu.VMEM((rows, deep), F32),
            pltpu.VMEM((rows, 2 * deep), BF16),
        ],
        40 * rows * deep * 512,
        count,
        at,
        ring,
        y,
        value,
        sums,
        gain,
        bias,
        inside,
        weights,
        cot_keep,
        cot_got,
    )


def weight_kernel(dilation, is_turned, x_ref, g_ref, *rest):
    *more, out_ref, turned_ref, stack_ref = rest
    tap = pl.program_id(0)
    rows = g_ref.shape[0]
    source_ref = x_ref if is_turned else turned_ref

    @pl.when(tap == 0)
    def _():
        if not is_turned:
            turned_ref[...] = x_ref[...].T
        move_map(stack_ref, g_ref, dilation)

    def product(g):
        return jnp.dot(source_ref[...], g, preferred_element_type=F32).astype(BF16)

    @pl.when(tap < 9)
    def _():
        start = pl.multiple_of((2 - tap // 3) * dilation * PITCH, 16)
        out_ref[...] = product(stack_ref[2 - tap % 3, pl.ds(start, rows), :])

    if more:

        @pl.when(tap == 9)
        def _():
            out_ref[...] = product(more[0][...])


def conv_weight(image, upstream, dilation, centre=(), is_turned=False):
    rows, wide = upstream.shape
    deep = image.size // rows
    blocks = 9 + len(centre)
    (out,) = call(
        functools.partial(weight_kernel, dilation, is_turned),
        (blocks,),
        [whole(image.shape), whole((rows, wide))] + [whole((rows, wide)) for a in centre],
        [pl.BlockSpec((deep, wide), lambda t: (0, t))],
        [((deep, blocks * wide), BF16)],
        [
            pltpu.VMEM((16, 128) if is_turned else (deep, rows), BF16),
            pltpu.VMEM((3, rows + 2 * dilation * PITCH, wide), BF16),
        ],
        2 * blocks * rows * deep * wide,
        image,
        upstream,
        *centre,
    )
    return out


def trunk_kernel(
    at_ref, g_ref, slope_ref, steep_ref, w_ref, o0, o1, o2, o3, sums_ref, stack_ref, turned_ref, total_ref, line_ref
):
    tap = pl.program_id(0)
    rows = g_ref.shape[0]

    @pl.when(tap == 0)
    def _():
        move_map(stack_ref, g_ref, 1)
        for k in range(9):
            start = (2 - k // 3) * PITCH
            turned_ref[k] = stack_ref[2 - k % 3, start : start + rows, :].T

    part = jnp.dot(w_ref[...], turned_ref[tap], preferred_element_type=F32)

    @pl.when(tap == 0)
    def _():
        total_ref[...] = part

    @pl.when(tap > 0)
    def _():
        total_ref[...] += part

    @pl.when(tap == 8)
    def _():
        for c in range(0, total_ref.shape[0], 512):
            columns = slice(c, c + 512)
            value = total_ref[columns, :].T
            line_ref[...] = value
            sums_ref[0:1, columns] = jnp.sum(
                value * steep_ref[:, columns].astype(F32), axis=0, keepdims=True
            )
            sums_ref[1:2, columns] = jnp.sum(
                value * slope_ref[:, columns].astype(F32), axis=0, keepdims=True
            )
            for k in range(4):
                start = pl.multiple_of(at_ref[k], 16)
                out_ref = (o0, o1, o2, o3)[k]
                out_ref[:, columns] = line_ref[pl.ds(start, rows // 4), :].astype(BF16)


def trunk_back(at, upstream, slope, steep, weights):
    rows, wide = upstream.shape
    deep = weights.shape[0]
    return call(
        trunk_kernel,
        (9,),
        [SCALARS, whole((rows, wide)), whole((rows, deep)), whole((rows, deep))]
        + [pl.BlockSpec((deep, wide), lambda t: (0, t))],
        [whole((rows // 4, deep))] * 4 + [kept((2, deep))],
        [((rows // 4, deep), BF16)] * 4 + [((2, deep), F32)],
        [
            pltpu.VMEM((3, rows + 2 * PITCH, wide), BF16),
            pltpu.VMEM((9, wide, rows), BF16),
            pltpu.VMEM((deep, rows), F32),
            pltpu.VMEM((rows, 512), F32),
        ],
        18 * rows * deep * wide,
        at,
        upstream,
        slope,
        steep,
        weights,
    )
def joined_kernel(
    count_ref, at_ref, own_ref, near_ref, far_ref, pre_ref, base_ref, sums_ref, gain_ref, bias_ref, inside_ref, back_ref,
    w_ref, low_ref, low_sums, low_gain, low_bias,
    d_joined_ref, c0, c1, c2, c3, d_norm_ref, out_sums, d_pre_ref,
):
    count = count_ref[0]
    mean, inverse = moments(sums_ref, count)
    inside = inside_ref[...]
    for c in range(4):
        columns = slice(c * 512, (c + 1) * 512)
        centred = (pre_ref[:, columns].astype(F32) - mean[:, columns]) * inverse[:, columns]
        gain = gain_ref[:, columns]
        joined = gain * centred + bias_ref[:, columns] + base_ref[:, columns].astype(F32)
        d_trunk = (
            own_ref[:, columns].astype(F32)
            + near_ref[:, columns].astype(F32)
            + far_ref[:, columns].astype(F32)
        )
        d_joined = gelu_slope(joined) * d_trunk * inside
        d_joined_ref[:, columns] = d_joined.astype(BF16)
        shift = (back_ref[1:2, columns] + centred * back_ref[0:1, columns]) / count
        d_pre_ref[:, columns] = (
            inside * gain * inverse[:, columns] * (d_joined - shift)
        ).astype(BF16)
    for k, part_ref in enumerate((c0, c1, c2, c3)):
        first = pl.multiple_of(at_ref[k] // (2 * PITCH) * 512, 512)
        part_ref[...] = d_pre_ref[:, pl.ds(first, 512)]
    d_act = times_turned(d_pre_ref[...], w_ref[...])
    mean, inverse = moments(low_sums, count)
    centred = (low_ref[...].astype(F32) - mean) * inverse
    upstream = gelu_slope(low_gain[...] * centred + low_bias[...]) * d_act * inside
    upstream = upstream.astype(BF16)
    d_norm_ref[...] = upstream
    upstream = upstream.astype(F32)
    store_sums(out_sums, upstream * centred, upstream)


def joined_back(count, at, pieces, pre, base, sums, gain, bias, inside, back, weights, low, low_sums, low_gain, low_bias):
    rows, deep = pre.shape
    narrow = low.shape[1]
    operands = (*pieces, pre, base, sums, gain, bias, inside, back)
    lower = (low, low_sums, low_gain, low_bias)
    out_d_joined, *columns, out_d_norm, out_sums = call(
        joined_kernel,
        (1,),
        [SCALARS, SCALARS]
        + [whole(a.shape) for a in pieces]
        + [whole(pre.shape)] * 2
        + [whole(a.shape) for a in operands[5:]]
        + [whole((narrow, deep))]
        + [whole(a.shape) for a in lower],
        [kept((rows, deep))] + [kept((rows, 512))] * 4 + [kept((rows, narrow)), kept((2, narrow))],
        [((rows, deep), BF16)]
        + [((rows, 512), BF16)] * 4
        + [((rows, narrow), BF16), ((2, narrow), F32)],
        [pltpu.VMEM((rows, deep), BF16)],
        2 * rows * deep * narrow,
        count,
        at,
        *operands,
        weights,
        *lower,
    )
    return out_d_joined, columns, out_d_norm, out_sums


def dilated_back_kernel(
    count_ref, at_ref, u0, u1, u2, u3, value_ref, sums_ref, back_ref, gain_ref, inside_ref,
    w_ref, low_ref, low_sums, low_gain, low_bias,
    d_norm_ref, out_sums, part_ref,
    image_ref, stack_ref, turned_ref, total_ref,
):
    tap = pl.program_id(0)
    strip = 2 * PITCH
    rows = value_ref.shape[0]
    count = count_ref[0]

    @pl.when(tap == 0)
    def _():
        clear_image(image_ref)
        mean, inverse = moments(sums_ref, count)
        for k, up in enumerate((u0, u1, u2, u3)):
            start = pl.multiple_of(at_ref[k], 16)
            centred = (value_ref[pl.ds(start, strip), :].astype(F32) - mean) * inverse
            shift = (back_ref[1:2, :] + centred * back_ref[0:1, :]) / count
            scale = inside_ref[pl.ds(start, strip), :] * (gain_ref[...] * inverse)
            lowered = (scale * (up[...].astype(F32) - shift)).astype(BF16)
            image_ref[pl.ds(pl.multiple_of(start + strip, 16), strip), :] = lowered
        window_moved(stack_ref, image_ref, 0, 12)
        mine = pl.multiple_of(at_ref[0] // strip * 128, 128)
        part_ref[...] = image_ref[strip : 5 * strip, pl.ds(mine, 128)]
        for k in range(9):
            start = (2 - k // 3) * strip
            turned_ref[k] = stack_ref[2 - k % 3, start : start + rows, :].T
        total_ref[...] = jnp.zeros_like(total_ref)

    total_ref[...] += jnp.dot(w_ref[...], turned_ref[tap], preferred_element_type=F32)

    @pl.when(tap == 8)
    def _():
        mean, inverse = moments(low_sums, count)
        centred = (low_ref[...].astype(F32) - mean) * inverse
        slope = gelu_slope(low_gain[...] * centred + low_bias[...])
        upstream = (slope * total_ref[...].T * inside_ref[...]).astype(BF16)
        d_norm_ref[...] = upstream
        upstream = upstream.astype(F32)
        store_sums(out_sums, upstream * centred, upstream)


def dilated_back(
    count, at, ups, value, sums, back, gain, inside, weights, first_block, low, low_sums, low_gain, low_bias
):
    rows, wide = value.shape
    strip = 2 * PITCH
    operands = (*ups, value, sums, back, gain, inside)
    lower = (low, low_sums, low_gain, low_bias)
    return call(
        dilated_back_kernel,
        (9,),
        [SCALARS, SCALARS]
        + [whole(a.shape) for a in operands]
        + [pl.BlockSpec((512, wide), lambda t: (0, first_block + t))]
        + [whole(a.shape) for a in lower],
        [kept((rows, 512)), kept((2, 512)), kept((rows, 128))],
        [((rows, 512), BF16), ((2, 512), F32), ((rows, 128), BF16)],
        [
            pltpu.VMEM((rows + 2 * strip, wide), BF16),
            pltpu.VMEM((3, rows + 2 * strip, wide), BF16),
            pltpu.VMEM((9, wide, rows), BF16),
            pltpu.VMEM((512, rows), F32),
        ],
        18 * rows * wide * 512,
        count,
        at,
        *operands,
        weights,
        *lower,
    )


def heads_kernel(at_ref, local_ref, *refs):
    *pieces, got_ref = refs[:5]
    outs = refs[5:]

    def put(k, value):
        first = 0
        for out_ref in outs:
            last = first + out_ref.shape[2]
            out_ref[at_ref[k]] = value[:, first:last].astype(F32)
            first = last

    @pl.when(local_ref[0] == 1)
    def _():
        for k, piece in enumerate(pieces):
            put(k, piece)

    @pl.when(local_ref[0] == 0)
    def _():
        for k in range(4):
            put(k, got_ref.at[k])


def heads_placed(at, local, pieces, got, widths):
    rows, deep = pieces[0].shape
    return call(
        heads_kernel,
        (1,),
        [SCALARS, SCALARS] + [whole((rows, deep))] * 4 + [whole((4, rows, deep))],
        [whole((4, rows, wide)) for wide in widths],
        [((4, rows, wide), F32) for wide in widths],
        [],
        0,
        at,
        local,
        *pieces,
        got,
    )


def sums_of(value):
    return jnp.stack([jnp.sum(value, axis=0), jnp.sum(value * value, axis=0)])


def centred_by(value, sums, count):
    mean = sums[0] / count
    inverse = lax.rsqrt(sums[1] / count - mean * mean + EPS)
    return (value.astype(F32) - mean) * inverse, inverse


def norm_back(upstream, value, sums, gain, inside, back, count):
    centred, inverse = centred_by(value, sums, count)
    return (
        inside * gain * inverse * (upstream.astype(F32) - (back[1] + centred * back[0]) / count)
    ).astype(BF16)


def turned_dot(first, second):
    return lax.dot_general(first, second, (((0,), (0,)), ((), ())), preferred_element_type=F32)


def strips_of(value):
    _, rows, across, deep = value.shape
    padded = jnp.pad(value[0], ((0, 0), (0, PITCH - across), (0, 0)))
    return padded.reshape(rows * PITCH, deep)


def maps_of(value, across):
    rows = value.shape[0] // PITCH
    return value.reshape(1, rows, PITCH, -1)[:, :, :across]


def shares_sent(value, axes):
    count = lax.axis_size(axes)
    return lax.all_to_all(
        value.reshape(count, value.shape[0] // count, value.shape[1]), axes, 0, 0
    )


def parts_summed(parts):
    return jnp.sum(parts.astype(F32), axis=0).astype(BF16)


def shards(
    features,
    image_size,
    reduce_weight,
    dilated_weight,
    expand_weight,
    head_weight,
    message_weight,
    gate_weight,
    bottleneck_gain,
    bottleneck_bias,
    expand_gain,
    expand_bias,
    head_gain,
    head_bias,
    depth_cotangent,
    seg_cotangent,
):
    ylo, core, yhi = (lax.axis_index(a) for a in ("ylo", "core", "yhi"))
    plane = lax.axis_index("x") * 4 + lax.axis_index("z")
    y = yhi * 2 + ylo
    strip = ylo * 2 + core
    width = features.shape[2]
    local = core == yhi

    count = jnp.sum(image_size[:, 0].astype(F32) * image_size[:, 1].astype(F32))
    count_here = count.reshape(1)

    def inside_of(sizes, image, first, rows):
        size = lax.dynamic_index_in_dim(sizes, image, 0, keepdims=False)
        at = jnp.arange(rows * PITCH, dtype=jnp.int32)
        valid = (first + at // PITCH < size[0]) & (at % PITCH < size[1])
        return valid.astype(F32)[:, None]

    length = 2 * PITCH
    head_at = (
        jnp.stack(
            [
                ylo * 2 + core,
                (1 - ylo) * 2 + core,
                ylo * 2 + 1 - core,
                (1 - ylo) * 2 + 1 - core,
            ]
        )
        * length
    ).astype(jnp.int32)
    ring_at = (jnp.stack([y, y ^ 1, y ^ 2, y ^ 3]) * length).astype(jnp.int32)

    group = [(i, i ^ 5) for i in range(8) if (i >> 1) & 1 == i & 1]

    def brought(mine, sent):
        return jnp.where(local, mine, lax.ppermute(sent, GROUP, group))

    def of_head(stacked, head):
        return lax.dynamic_index_in_dim(stacked, head, 0, keepdims=False)

    planes = 16

    deep = features.shape[3]
    same = yhi == core
    inside = inside_of(image_size, plane * 2 + yhi, strip * 2, 2)
    base = strips_of(features) * inside.astype(BF16)
    near, far = beside_y(base)
    channels = expand_weight.shape[0]
    wide_trunk = expand_weight.shape[1] + dilated_weight.shape[1]
    first_weights = jnp.concatenate(
        [expand_weight, dilated_weight, reduce_weight.reshape(channels, -1)], axis=1
    )
    first_part = brought(first_weights, first_weights)
    reduce_part = first_part[:, wide_trunk:].reshape(reduce_weight.shape)
    copies, sizes_first = hold(
        jnp.broadcast_to(reduce_part[None], (planes,) + reduce_part.shape), image_size
    )
    reduce_half = lax.all_to_all(copies, ("x", "z"), 0, 0)
    whole_reduce = jnp.stack(
        in_order(reduce_half, over_core(reduce_half), core), axis=1
    ).reshape(-1, reduce_weight.shape[1])
    whole_trunk = lax.all_gather(first_part[:, :wide_trunk], POOL, axis=0, tiled=True)
    first_tap = expand_weight.shape[1] // 512
    inside_whole = inside_of(sizes_first, plane * 2 + core, 0, 8)

    def spread(own, near, across_low, across_high, far):
        mine = jnp.concatenate([own, near])
        other = jnp.concatenate([across_low, across_high, far])
        return jnp.where(same, mine, other), over_core(jnp.where(same, other, mine))

    near, far, y_first = hold(near, far, y)
    head_part = brought(of_head(head_weight, y_first), of_head(head_weight, y_first ^ 3))
    base_keep, base_got = spread(base, near, *across_y(near, far), far)
    whole_reduce, base_keep, base_got, inside_whole, head_part = hold(
        whole_reduce, base_keep, base_got, inside_whole, head_part
    )
    whole_head = lax.all_gather(head_part, POOL, axis=0, tiled=True)

    pre_one = jnp.concatenate(
        [
            jnp.dot(a, whole_reduce, preferred_element_type=F32).astype(BF16)
            for a in (base_keep, base_got)
        ]
    )
    sums_one = fold(sums_of(pre_one.astype(F32)), CORE, *LINE, *PLANE)
    pre_two, sums_two, act_one_image, pre_one_image = dilated_forward(
        count_here,
        head_at,
        pre_one,
        sums_one,
        bottleneck_gain[:1],
        bottleneck_bias[:1],
        inside_whole,
        whole_trunk,
        first_tap,
    )
    sums_two = fold(sums_two, CORE, *LINE)
    sums_two, y_later, depth_cots, seg_cots = hold(sums_two, y, depth_cotangent, seg_cotangent)
    task_weights = jnp.concatenate([message_weight, gate_weight], axis=2)
    task_part = brought(of_head(task_weights, y_later), of_head(task_weights, y_later ^ 3))
    cots = jnp.concatenate([strips_of(depth_cots), strips_of(seg_cots)], axis=1)
    near, far = beside_y(cots)
    sums_two = fold(sums_two, *PLANE)
    act_two, pre_three, sums_three = expand_forward(
        count_here,
        pre_two,
        sums_two,
        bottleneck_gain[1:],
        bottleneck_bias[1:],
        inside_whole,
        whole_trunk,
    )
    sums_three, task_part = hold(fold(sums_three, CORE, *LINE), task_part)
    whole_task = lax.all_gather(task_part, POOL, axis=0, tiled=True)
    sums_three = fold(sums_three, *PLANE)

    gain_here, bias_here = of_head(head_gain, y)[None], of_head(head_bias, y)[None]
    wide_gain, wide_bias = expand_gain[None], expand_bias[None]
    trunk, slope, steep, base_image, trunk_turned = trunk_forward(
        count_here,
        head_at,
        pre_three,
        base_keep,
        base_got,
        sums_three,
        wide_gain,
        wide_bias,
        inside_whole,
    )
    trunk, near, far = hold(trunk, near, far)
    across_low, across_high = across_y(near, far)
    pre_head, sums_head = head_forward(trunk, inside_whole, whole_head)
    sums_head, near, far, across_low, across_high = hold(
        sums_head, near, far, across_low, across_high
    )
    cots_keep, cots_got = spread(cots, near, across_low, across_high, far)
    sums_head = fold(sums_head, CORE, *LINE, *PLANE)
    task, *streams, d_message, d_logit, d_norm_head, back_here = message_stage(
        count_here,
        head_at,
        ring_at,
        y.astype(jnp.int32).reshape(1),
        pre_head,
        sums_head,
        gain_here,
        bias_here,
        inside_whole,
        whole_task,
        cots_keep,
        cots_got,
    )
    back_head = fold(back_here, CORE, *LINE, *PLANE)
    back_head, streams = hold(back_head, streams)
    d_pre_head = norm_back(
        d_norm_head, pre_head, sums_head, gain_here, inside_whole, back_head, count
    )
    own, near, across, far = streams
    from_near, from_far = half_way(across)
    head_grad = conv_weight(trunk_turned, d_pre_head, 1, is_turned=True)
    head_grad, d_pre_head, from_near, from_far = hold(head_grad, d_pre_head, from_near, from_far)
    head_share = lax.psum_scatter(head_grad, POOL, scatter_dimension=0, tiled=True)
    streams = last_way(own, near, far, from_near, from_far)
    *d_trunk, back_three = trunk_back(ring_at, d_pre_head, slope, steep, whole_head)
    d_trunk, back_three, streams = hold(d_trunk, back_three, streams)
    placed = jnp.where(
        jnp.arange(4)[None, :, None] == y, back_here[:, None], jnp.zeros((1, 1, 1), F32)
    ).reshape(2, -1)
    back_wide = jnp.concatenate([back_three, placed], axis=1)
    own, near, across, far = d_trunk
    from_near, from_far = half_way(across)
    back_wide, from_near, from_far = hold(fold(back_wide, CORE, *LINE), from_near, from_far)
    pieces = last_way(own, near, far, from_near, from_far)
    back_wide = fold(back_wide, *PLANE)
    def strip_of(value):
        return lax.dynamic_slice_in_dim(value, y * length, length, 0)

    pre_two_strip, pre_three_strip, base_strip, inside_strip = (
        strip_of(a) for a in (pre_two, pre_three, base_image, inside_whole)
    )

    def ring_order(value):
        return jnp.concatenate(
            [
                lax.dynamic_slice_in_dim(value, (y ^ flip) * length, length, 0)
                for flip in range(4)
            ]
        )

    act_two_ring = ring_order(act_two)
    task_grad = conv_weight(task, d_message, 1, (d_logit,))
    (
        back_wide,
        pieces,
        pre_two_strip,
        pre_three_strip,
        base_strip,
        inside_strip,
        act_two_ring,
        task_grad,
    ) = hold(
        back_wide,
        pieces,
        pre_two_strip,
        pre_three_strip,
        base_strip,
        inside_strip,
        act_two_ring,
        task_grad,
    )
    task_share = lax.psum_scatter(task_grad, POOL, scatter_dimension=0, tiled=True)
    back_wide = fold(back_wide, *RIDGE)
    back_three, back_heads = back_wide[:, :deep], back_wide[:, deep:]
    d_joined, d_three_parts, d_norm_two, back_two = joined_back(
        count_here,
        ring_at,
        pieces,
        pre_three_strip,
        base_strip,
        sums_three,
        wide_gain,
        wide_bias,
        inside_strip,
        back_three,
        whole_trunk,
        pre_two_strip,
        sums_two,
        bottleneck_gain[1:],
        bottleneck_bias[1:],
    )
    back_two = fold(back_two, CORE, *LINE)
    back_two, d_norm_twos = hold(back_two, around_y(d_norm_two))
    back_two = fold(back_two, *PLANE, *RIDGE)

    d_three_part = jnp.concatenate(for_me(d_three_parts))
    grad_expand = turned_dot(act_two_ring, d_three_part).astype(BF16)
    back_two, grad_expand, d_joined = hold(back_two, grad_expand, d_joined)
    homeward = sent_home(
        jnp.concatenate([d_joined, sum(a.astype(F32) for a in streams).astype(BF16)], axis=1)
    )
    d_norm_one, back_one, d_two_part = dilated_back(
        count_here,
        ring_at,
        d_norm_twos,
        pre_two,
        sums_two,
        back_two,
        bottleneck_gain[1:],
        inside_whole,
        whole_trunk,
        first_tap,
        pre_one_image,
        sums_one,
        bottleneck_gain[:1],
        bottleneck_bias[:1],
    )
    def to_chips(share):
        pieces = [share]
        for flip in (1, 2, 3):
            pairs = []
            for i in range(8):
                low, c, high = i >> 2, (i >> 1) & 1, i & 1
                to = (high * 2 + low) ^ flip
                if to >> 1 == c:
                    pairs.append((i, ((to & 1) << 2) | (c << 1) | (to >> 1)))
            pieces.append(lax.ppermute(share, GROUP, pairs))
        return tuple(pieces)

    heads_at = jnp.stack([y, y ^ 1, y ^ 2, y ^ 3]).astype(jnp.int32)
    local_here = local.astype(jnp.int32).reshape(1)

    def to_cores(pieces, *widths):
        pairs = [(i, i ^ 2) for i in range(8) if (i >> 1) & 1 == i & 1]
        got = lax.ppermute(jnp.stack(pieces), GROUP, pairs)
        return heads_placed(heads_at, local_here, pieces, got, widths)

    back_one = fold(back_one, CORE, *LINE)
    grad_dilated = conv_weight(act_one_image, d_two_part, 2)
    trunk_grad = jnp.concatenate([grad_expand, grad_dilated], axis=1)
    back_one, trunk_grad, homeward, head_share = hold(back_one, trunk_grad, homeward, head_share)
    head_pieces = to_chips(head_share)
    back_one = fold(back_one, *PLANE)
    d_pre_one = norm_back(
        d_norm_one, pre_one_image, sums_one, bottleneck_gain[0], inside_whole, back_one, count
    )
    grad_reduce = turned_dot(
        base_image, lax.dynamic_slice_in_dim(d_pre_one, y * 128, 128, 1)
    ).astype(BF16)
    trunk_grad = jnp.concatenate(
        [trunk_grad, grad_reduce.reshape(trunk_grad.shape[0], -1)], axis=1
    )
    trunk_grad, d_pre_one = hold(trunk_grad, d_pre_one)
    trunk_parts = shares_sent(trunk_grad, POOL)
    wide = message_weight.shape[2]
    d_pre_one = sent_home(strip_of(d_pre_one))
    d_base = homeward[:, :deep].astype(F32) + times_turned(d_pre_one, whole_reduce)
    input_grad = maps_of(d_base * inside, width)
    trunk_parts, head_pieces, input_grad = hold(trunk_parts, head_pieces, input_grad)
    (sum_head,) = to_cores(head_pieces, wide)
    small_share = jnp.concatenate([task_share, parts_summed(trunk_parts)], axis=1)
    sum_message, sum_gate, all_trunk, all_reduce = to_cores(
        to_chips(small_share), wide, gate_weight.shape[2], trunk_grad.shape[1] - 512, 512
    )
    sum_expand = jnp.moveaxis(all_trunk[:, :, :512], 0, 1).reshape(channels, -1)
    sum_dilated = jnp.moveaxis(
        all_trunk[:, :, 512:].reshape(4, channels, 9, 128), 0, 2
    ).reshape(channels, -1)
    sum_reduce = jnp.moveaxis(all_reduce.reshape(4, -1, 128), 0, 1).reshape(-1, 512)


    streams = maps_of(homeward[:, deep:].astype(F32) * inside, width)
    depth_out, seg_out = jnp.split(streams, 2, axis=3)

    return (
        depth_out,
        seg_out,
        input_grad,
        sum_reduce,
        sum_dilated,
        sum_expand,
        sum_head,
        sum_message,
        sum_gate,
        jnp.stack([back_one[0], back_two[0]]),
        jnp.stack([back_one[1], back_two[1]]),
        back_three[0],
        back_three[1],
        back_heads[0].reshape(4, -1),
        back_heads[1].reshape(4, -1),
    )


def solution(mesh):
    fine = Mesh(mesh.devices.reshape(2, 2, 4, 4, 2), FINE)
    maps = P(IMG, ROWS, None, None)
    placed = (
        maps,
        P(),
        P(IMG, None),
        P(IMG, None),
        P(IMG, None),
        P(None, IMG, None),
        P(None, IMG, None),
        P(None, IMG, None),
        P(),
        P(),
        P(),
        P(),
        P(),
        P(),
        maps,
        maps,
    )
    return jax.shard_map(
        shards,
        mesh=fine,
        in_specs=placed,
        out_specs=(
            maps,
            maps,
            maps,
            P(IMG, None),
            P(IMG, None),
            P(IMG, None),
            P(None, IMG, None),
            P(None, IMG, None),
            P(None, IMG, None),
            P(),
            P(),
            P(),
            P(),
            P(),
            P(),
        ),
        check_vma=False,
    )
```

```python
import functools

import jax
import jax.numpy as jnp
from jax import lax
from jax.experimental import pallas as pl
from jax.experimental.pallas import tpu as pltpu
from jax.sharding import Mesh, PartitionSpec as P

EPS = 1e-05
PITCH = 80
ROOT = 0.7978845608028654
CUBE = 0.044715
F32 = jnp.float32
BF16 = jnp.bfloat16

FINE = ("ylo", "core", "x", "z", "yhi")
ROWS = ("ylo", "core")
IMG = ("x", "z", "yhi")
RING = ("ylo", "yhi")
GROUP = ("ylo", "core", "yhi")
POOL = ("x", "z", "core")


def swap(value, axis, flip):
    count = lax.axis_size(axis)
    return lax.ppermute(value, axis, [(i, i ^ flip) for i in range(count)])


def over_core(value):
    return swap(value, "core", 1)


def over_y(value, flip):
    return swap(value, RING, {1: 2, 2: 1, 3: 3}[flip])


def fold(value, *partners):
    for axis, flip in partners:
        value = value + (over_y(value, flip) if axis == "y" else swap(value, axis, flip))
    return value


CORE, LINE, PLANE, RIDGE = ("core", 1), (("x", 1), ("x", 3)), (("z", 1), ("z", 3)), (("y", 1), ("y", 3))


def hold(*arrays):
    return lax.optimization_barrier(arrays)


def in_order(mine, other, bit):
    first = bit == 0
    return jnp.where(first, mine, other), jnp.where(first, other, mine)


def around_y(value):
    return value, over_y(value, 1), over_y(value, 2), over_y(value, 3)


def for_me(parts):
    own, near, across, far = parts
    return own, over_y(near, 1), over_y(across, 2), over_y(far, 3)


HOME = [(i, ((i & 1) << 2) | (((i >> 2) & 1) << 1) | ((i >> 1) & 1)) for i in range(8)]


def sent_home(value):
    return lax.ppermute(value, GROUP, HOME)


def beside_y(value):
    return over_y(value, 1), over_y(value, 3)


def across_y(near, far):
    half = near.shape[0] // 2
    return over_y(far[:half], 1), over_y(near[half:], 3)


def half_way(across):
    half = across.shape[0] // 2
    return over_y(across[:half], 1), over_y(across[half:], 3)


def last_way(own, near, far, from_near, from_far):
    half = own.shape[0] // 2
    near = jnp.concatenate(
        [near[:half], (near[half:].astype(F32) + from_far.astype(F32)).astype(BF16)]
    )
    far = jnp.concatenate(
        [(far[:half].astype(F32) + from_near.astype(F32)).astype(BF16), far[half:]]
    )
    return own, over_y(near, 1), over_y(far, 3)


def gelu_parts(value):
    squared = value * value
    bend = jnp.tanh(ROOT * value * (1.0 + CUBE * squared))
    return 0.5 * (1.0 + bend), bend, squared


def gelu(value):
    return value * gelu_parts(value)[0]


def gelu_slope(value):
    level, bend, squared = gelu_parts(value)
    return level + 0.5 * value * (1.0 - bend * bend) * ROOT * (1.0 + 3.0 * CUBE * squared)


def moments(sums_ref, count):
    mean = sums_ref[0:1, :] / count
    return mean, lax.rsqrt(sums_ref[1:2, :] / count - mean * mean + EPS)


def store_sums(sums_ref, first, second):
    sums_ref[0:1, :] = jnp.sum(first, axis=0, keepdims=True)
    sums_ref[1:2, :] = jnp.sum(second, axis=0, keepdims=True)


def add_sums(sums_ref, first, second, columns=slice(None)):
    sums_ref[0:1, columns] += jnp.sum(first, axis=0, keepdims=True)
    sums_ref[1:2, columns] += jnp.sum(second, axis=0, keepdims=True)


def store_moved(stack_ref, start, value, dilation, columns=slice(None)):
    rows = pl.ds(start, PITCH)
    stack_ref[0, rows, columns] = pltpu.roll(value, dilation, 0).astype(BF16)
    stack_ref[1, rows, columns] = value.astype(BF16)
    stack_ref[2, rows, columns] = pltpu.roll(value, PITCH - dilation, 0).astype(BF16)


def clear_ends(stack_ref, rows):
    length = stack_ref.shape[1]
    empty = jnp.zeros((3, rows, stack_ref.shape[2]), BF16)
    stack_ref[:, 0:rows, :] = empty
    stack_ref[:, length - rows : length, :] = empty


def move_map(stack_ref, map_ref, dilation):
    clear_ends(stack_ref, dilation * PITCH)

    @pl.loop(0, 8)
    def _(r):
        at = pl.multiple_of(r * PITCH, 16)
        store_moved(
            stack_ref,
            pl.multiple_of(at + dilation * PITCH, 16),
            map_ref[pl.ds(at, PITCH), :].astype(F32),
            dilation,
        )


def times_turned(first, second):
    return lax.dot_general(first, second, (((1,), (1,)), ((), ())), preferred_element_type=F32)


def whole(shape):
    return pl.BlockSpec(shape, lambda *at: (0,) * len(shape), pipeline_mode=pl.Buffered(1))


def kept(shape):
    return pl.BlockSpec(shape, lambda *at: (0,) * len(shape))


SCALARS = pl.BlockSpec(memory_space=pltpu.SMEM)


def call(kernel, grid, in_specs, out_specs, outs, scratch, flops, *operands):
    moved = sum(a.size * a.dtype.itemsize for a in operands) if flops else 0
    return pl.pallas_call(
        kernel,
        grid=grid,
        in_specs=in_specs,
        out_specs=out_specs,
        out_shape=[jax.ShapeDtypeStruct(*o) for o in outs],
        scratch_shapes=scratch,
        compiler_params=pltpu.CompilerParams(vmem_limit_bytes=56 << 20),
        cost_estimate=pl.CostEstimate(flops=flops, bytes_accessed=moved, transcendentals=0),
    )(*operands)


def clear_image(image_ref):
    strip = 2 * PITCH
    empty = jnp.zeros((strip, image_ref.shape[1]), BF16)
    image_ref[0:strip, :] = empty
    image_ref[5 * strip : 6 * strip, :] = empty


def window_moved(stack_ref, image_ref, start, rows):
    @pl.loop(0, rows)
    def _(r):
        at = pl.multiple_of(r * PITCH, 16)
        value = image_ref[pl.ds(pl.multiple_of(start + at, 16), PITCH), :]
        store_moved(stack_ref, at, value.astype(F32), 2)


def dilated_kernel(
    count_ref, at_ref, value_ref, sums_ref, gain_ref, bias_ref, inside_ref, w_ref,
    out_ref, out_sums, image_out, value_out, image_ref, stack_ref, total_ref,
):
    tap = pl.program_id(0)
    strip = 2 * PITCH

    @pl.when(tap == 0)
    def _():
        clear_image(image_ref)
        mean, inverse = moments(sums_ref, count_ref[0])
        for k in range(4):
            start = pl.multiple_of(at_ref[k], 16)
            value = value_ref[k * strip : (k + 1) * strip, :]
            value_out[pl.ds(start, strip), :] = value
            normed = gain_ref[...] * ((value.astype(F32) - mean) * inverse) + bias_ref[...]
            act = (gelu(normed) * inside_ref[pl.ds(start, strip), :]).astype(BF16)
            image_ref[pl.ds(pl.multiple_of(start + strip, 16), strip), :] = act
            image_out[pl.ds(start, strip), :] = act
        window_moved(stack_ref, image_ref, 0, 12)
        total_ref[...] = jnp.zeros_like(total_ref)

    start = pl.multiple_of((tap // 3) * strip, 16)
    total_ref[...] += jnp.dot(
        stack_ref[tap % 3, pl.ds(start, 4 * strip), :], w_ref[...], preferred_element_type=F32
    )

    @pl.when(tap == 8)
    def _():
        out = total_ref[...].astype(BF16)
        out_ref[...] = out
        out = out.astype(F32)
        value = out * inside_ref[...]
        store_sums(out_sums, value, value * out)


def dilated_forward(count, at, value, sums, gain, bias, inside, weights, first_block):
    rows, deep = value.shape
    strip = 2 * PITCH
    operands = (value, sums, gain, bias, inside)
    return call(
        dilated_kernel,
        (9,),
        [SCALARS, SCALARS]
        + [whole(a.shape) for a in operands]
        + [pl.BlockSpec((deep, 512), lambda t: (0, first_block + t))],
        [kept((rows, 512)), kept((2, 512)), kept((rows, deep)), kept((rows, deep))],
        [((rows, 512), BF16), ((2, 512), F32), ((rows, deep), BF16), ((rows, deep), BF16)],
        [
            pltpu.VMEM((rows + 2 * strip, deep), BF16),
            pltpu.VMEM((3, rows + 2 * strip, deep), BF16),
            pltpu.VMEM((rows, 512), F32),
        ],
        18 * rows * deep * 512,
        count,
        at,
        *operands,
        weights,
    )


def expand_kernel(count_ref, value_ref, sums_ref, gain_ref, bias_ref, inside_ref, w_ref, act_ref, out_ref, out_sums):
    mean, inverse = moments(sums_ref, count_ref[0])
    normed = gain_ref[...] * ((value_ref[...].astype(F32) - mean) * inverse) + bias_ref[...]
    act = (gelu(normed) * inside_ref[...]).astype(BF16)
    act_ref[...] = act
    for c in range(4):
        columns = slice(c * 512, (c + 1) * 512)
        part = jnp.dot(act, w_ref[:, columns], preferred_element_type=F32).astype(BF16)
        out_ref[:, columns] = part
        part = part.astype(F32)
        out_sums[0:1, columns] = jnp.sum(part, axis=0, keepdims=True)
        out_sums[1:2, columns] = jnp.sum(part * part, axis=0, keepdims=True)


def expand_forward(count, value, sums, gain, bias, inside, weights):
    rows, deep = value.shape
    return call(
        expand_kernel,
        (1,),
        [SCALARS]
        + [whole(a.shape) for a in (value, sums, gain, bias, inside)]
        + [whole((deep, 2048))],
        [kept((rows, deep)), kept((rows, 2048)), kept((2, 2048))],
        [((rows, deep), BF16), ((rows, 2048), BF16), ((2, 2048), F32)],
        [],
        2 * rows * deep * 2048,
        count,
        value,
        sums,
        gain,
        bias,
        inside,
        weights,
    )


def trunk_kernel_forward(
    count_ref, at_ref, value_ref, base_keep, base_got, sums_ref, gain_ref, bias_ref, inside_ref,
    trunk_ref, slope_ref, steep_ref, base_out, turned_ref,
):
    mean, inverse = moments(sums_ref, count_ref[0])
    for k, bases in enumerate((base_keep, base_got)):

        @pl.loop(0, 4)
        def _(r):
            source = pl.ds(pl.multiple_of(r * PITCH, 16), PITCH)
            first = at_ref[2 * k + r // 2] + (r % 2) * PITCH
            first = pl.multiple_of(first, 16)
            rows = pl.ds(first, PITCH)
            inside = inside_ref[rows, :]
            for c in range(4):
                columns = slice(c * 512, (c + 1) * 512)
                centred = (value_ref[rows, columns].astype(F32) - mean[:, columns]) * inverse[:, columns]
                base = bases[source, columns]
                base_out[rows, columns] = base
                joined = gain_ref[:, columns] * centred + bias_ref[:, columns] + base.astype(F32)
                level, bend, squared = gelu_parts(joined)
                trunk = joined * level * inside
                slope = (
                    level + 0.5 * joined * (1.0 - bend * bend) * ROOT * (1.0 + 3.0 * CUBE * squared)
                ) * inside
                trunk_ref[rows, columns] = trunk.astype(BF16)
                slope_ref[rows, columns] = slope.astype(BF16)
                steep_ref[rows, columns] = (slope * centred).astype(BF16)

    for c in range(4):
        columns = slice(c * 512, (c + 1) * 512)
        turned_ref[columns, :] = trunk_ref[:, columns].T


def trunk_forward(count, at, value, base_keep, base_got, sums, gain, bias, inside):
    rows, deep = value.shape
    operands = (value, base_keep, base_got, sums, gain, bias, inside)
    return call(
        trunk_kernel_forward,
        (1,),
        [SCALARS, SCALARS] + [whole(a.shape) for a in operands],
        [whole((rows, deep))] * 4 + [whole((deep, rows))],
        [((rows, deep), BF16)] * 4 + [((deep, rows), BF16)],
        [],
        40 * rows * deep,
        count,
        at,
        *operands,
    )


def head_kernel(trunk_ref, inside_ref, w_ref, out_ref, out_sums, stack_ref):
    tap = pl.program_id(0)
    rows_all = out_ref.shape[0]

    @pl.when(tap == 0)
    def _():
        clear_ends(stack_ref, PITCH)

        @pl.loop(0, 8)
        def _(r):
            at = pl.multiple_of(r * PITCH, 16)
            for c in range(4):
                columns = slice(c * 512, (c + 1) * 512)
                store_moved(
                    stack_ref,
                    pl.multiple_of(at + PITCH, 16),
                    trunk_ref[pl.ds(at, PITCH), columns].astype(F32),
                    1,
                    columns,
                )

        out_ref[...] = jnp.zeros_like(out_ref)

    start = pl.multiple_of((tap // 3) * PITCH, 16)
    out_ref[...] += jnp.dot(
        stack_ref[tap % 3, pl.ds(start, rows_all), :], w_ref[...], preferred_element_type=F32
    )

    @pl.when(tap == 8)
    def _():
        value = out_ref[...] * inside_ref[...]
        store_sums(out_sums, value, value * out_ref[...])


def head_forward(trunk, inside, weights):
    rows, deep = trunk.shape
    return call(
        head_kernel,
        (9,),
        [whole((rows, deep)), whole(inside.shape), pl.BlockSpec((deep, 512), lambda t: (0, t))],
        [whole((rows, 512)), kept((2, 512))],
        [((rows, 512), F32), ((2, 512), F32)],
        [pltpu.VMEM((3, rows + 2 * PITCH, deep), BF16)],
        18 * rows * deep * 512,
        trunk,
        inside,
        weights,
    )


def message_kernel(
    count_ref, at_ref, ring_ref, y_ref, value_ref, sums_ref, gain_ref, bias_ref, inside_ref, w_ref, cot_keep, cot_got,
    task_ref, s0, s1, s2, s3, d_message_ref, d_logit_ref, d_norm_ref, out_sums,
    stack_ref, total_ref, gate_ref, streams_ref,
):
    rows_all, deep = value_ref.shape
    mean, inverse = moments(sums_ref, count_ref[0])
    gain, bias = gain_ref[...], bias_ref[...]
    number = y_ref[0]
    clear_ends(stack_ref, PITCH)

    def centred_at(rows):
        return (value_ref[rows, :] - mean) * inverse

    @pl.loop(0, 8)
    def _(r):
        at = pl.multiple_of(r * PITCH, 16)
        rows = pl.ds(at, PITCH)
        task = gelu(gain * centred_at(rows) + bias) * inside_ref[rows, :]
        task_ref[rows, :] = task.astype(BF16)
        store_moved(stack_ref, pl.multiple_of(at + PITCH, 16), task, 1)

    gate_ref[...] = jnp.dot(
        task_ref[...], w_ref[:, 9 * 512 : 10 * 512], preferred_element_type=F32
    )
    total_ref[...] = jnp.zeros_like(total_ref)

    @pl.loop(0, 9)
    def _(tap):
        start = pl.multiple_of((tap // 3) * PITCH, 16)
        total_ref[...] += jnp.dot(
            stack_ref[tap % 3, pl.ds(start, rows_all), :],
            w_ref[:, pl.ds(pl.multiple_of(tap * 512, 512), 512)],
            preferred_element_type=F32,
        )

    for k, cots in enumerate((cot_keep, cot_got)):

        @pl.loop(0, 4)
        def _(r):
            source = pl.ds(pl.multiple_of(r * PITCH, 16), PITCH)
            at = pl.multiple_of(at_ref[2 * k + r // 2] + (r % 2) * PITCH, 16)
            rows = pl.ds(at, PITCH)
            inside = inside_ref[rows, :]
            message = total_ref[rows, :]
            gate = 1.0 / (1.0 + jnp.exp(-gate_ref[rows, :]))
            cot_depth = cots[source, :deep].astype(F32) * inside
            cot_seg = cots[source, deep:].astype(F32) * inside
            receive = jnp.where(
                number == 0, cot_seg, jnp.where(number == 1, cot_depth, cot_depth + cot_seg)
            )
            direct = jnp.where(
                number == 0, cot_depth, jnp.where(number == 1, cot_seg, jnp.zeros_like(cot_seg))
            )
            task = task_ref[rows, :]
            gated = (gate * message).astype(BF16)
            streams_ref[rows, :deep] = jnp.where(number == 0, task, gated)
            streams_ref[rows, deep:] = jnp.where(number == 1, task, gated)
            d_logit_ref[rows, :] = (receive * message * gate * (1.0 - gate)).astype(BF16)
            d_message = receive * gate
            d_message_ref[rows, :] = d_message.astype(BF16)
            store_moved(stack_ref, pl.multiple_of(at + PITCH, 16), d_message, 1)
            total_ref[rows, :] = direct

    for k, stream_ref in enumerate((s0, s1, s2, s3)):
        first = pl.multiple_of(ring_ref[k], 16)
        stream_ref[...] = streams_ref[pl.ds(first, 2 * PITCH), :]

    total_ref[...] += times_turned(d_logit_ref[...], w_ref[:, 9 * 512 : 10 * 512])

    @pl.loop(0, 9)
    def _(tap):
        start = pl.multiple_of((2 - tap // 3) * PITCH, 16)
        total_ref[...] += times_turned(
            stack_ref[2 - tap % 3, pl.ds(start, rows_all), :],
            w_ref[:, pl.ds(pl.multiple_of(tap * 512, 512), 512)],
        )

    out_sums[...] = jnp.zeros_like(out_sums)

    @pl.loop(0, 8)
    def _(r):
        rows = pl.ds(pl.multiple_of(r * PITCH, 16), PITCH)
        centred = centred_at(rows)
        upstream = gelu_slope(gain * centred + bias) * total_ref[rows, :] * inside_ref[rows, :]
        d_norm_ref[rows, :] = upstream
        add_sums(out_sums, upstream * centred, upstream)


def message_stage(count, at, ring, y, value, sums, gain, bias, inside, weights, cot_keep, cot_got):
    rows, deep = value.shape
    return call(
        message_kernel,
        (1,),
        [SCALARS] * 4
        + [whole(a.shape) for a in (value, sums, gain, bias, inside, weights)]
        + [whole((rows // 2, 2 * deep))] * 2,
        [
            kept((rows, deep)),
            *[kept((rows // 4, 2 * deep))] * 4,
            kept((rows, deep)),
            kept((rows, deep)),
            kept((rows, deep)),
            kept((2, deep)),
        ],
        [
            ((rows, deep), BF16),
            *[((rows // 4, 2 * deep), BF16)] * 4,
            ((rows, deep), BF16),
            ((rows, deep), BF16),
            ((rows, deep), F32),
            ((2, deep), F32),
        ],
        [
            pltpu.VMEM((3, rows + 2 * PITCH, deep), BF16),
            pltpu.VMEM((rows, deep), F32),
            pltpu.VMEM((rows, deep), F32),
            pltpu.VMEM((rows, 2 * deep), BF16),
        ],
        40 * rows * deep * 512,
        count,
        at,
        ring,
        y,
        value,
        sums,
        gain,
        bias,
        inside,
        weights,
        cot_keep,
        cot_got,
    )


def weight_kernel(dilation, is_turned, x_ref, g_ref, *rest):
    *more, out_ref, turned_ref, stack_ref = rest
    tap = pl.program_id(0)
    rows = g_ref.shape[0]
    source_ref = x_ref if is_turned else turned_ref

    @pl.when(tap == 0)
    def _():
        if not is_turned:
            turned_ref[...] = x_ref[...].T
        move_map(stack_ref, g_ref, dilation)

    def product(g):
        return jnp.dot(source_ref[...], g, preferred_element_type=F32).astype(BF16)

    @pl.when(tap < 9)
    def _():
        start = pl.multiple_of((2 - tap // 3) * dilation * PITCH, 16)
        out_ref[...] = product(stack_ref[2 - tap % 3, pl.ds(start, rows), :])

    if more:

        @pl.when(tap == 9)
        def _():
            out_ref[...] = product(more[0][...])


def conv_weight(image, upstream, dilation, centre=(), is_turned=False):
    rows, wide = upstream.shape
    deep = image.size // rows
    blocks = 9 + len(centre)
    (out,) = call(
        functools.partial(weight_kernel, dilation, is_turned),
        (blocks,),
        [whole(image.shape), whole((rows, wide))] + [whole((rows, wide)) for a in centre],
        [pl.BlockSpec((deep, wide), lambda t: (0, t))],
        [((deep, blocks * wide), BF16)],
        [
            pltpu.VMEM((16, 128) if is_turned else (deep, rows), BF16),
            pltpu.VMEM((3, rows + 2 * dilation * PITCH, wide), BF16),
        ],
        2 * blocks * rows * deep * wide,
        image,
        upstream,
        *centre,
    )
    return out


def trunk_kernel(
    at_ref, g_ref, slope_ref, steep_ref, w_ref, o0, o1, o2, o3, sums_ref, stack_ref, turned_ref, total_ref, line_ref
):
    tap = pl.program_id(0)
    rows = g_ref.shape[0]

    @pl.when(tap == 0)
    def _():
        move_map(stack_ref, g_ref, 1)
        for k in range(9):
            start = (2 - k // 3) * PITCH
            turned_ref[k] = stack_ref[2 - k % 3, start : start + rows, :].T

    part = jnp.dot(w_ref[...], turned_ref[tap], preferred_element_type=F32)

    @pl.when(tap == 0)
    def _():
        total_ref[...] = part

    @pl.when(tap > 0)
    def _():
        total_ref[...] += part

    @pl.when(tap == 8)
    def _():
        for c in range(0, total_ref.shape[0], 512):
            columns = slice(c, c + 512)
            value = total_ref[columns, :].T
            line_ref[...] = value
            sums_ref[0:1, columns] = jnp.sum(
                value * steep_ref[:, columns].astype(F32), axis=0, keepdims=True
            )
            sums_ref[1:2, columns] = jnp.sum(
                value * slope_ref[:, columns].astype(F32), axis=0, keepdims=True
            )
            for k in range(4):
                start = pl.multiple_of(at_ref[k], 16)
                out_ref = (o0, o1, o2, o3)[k]
                out_ref[:, columns] = line_ref[pl.ds(start, rows // 4), :].astype(BF16)


def trunk_back(at, upstream, slope, steep, weights):
    rows, wide = upstream.shape
    deep = weights.shape[0]
    return call(
        trunk_kernel,
        (9,),
        [SCALARS, whole((rows, wide)), whole((rows, deep)), whole((rows, deep))]
        + [pl.BlockSpec((deep, wide), lambda t: (0, t))],
        [whole((rows // 4, deep))] * 4 + [kept((2, deep))],
        [((rows // 4, deep), BF16)] * 4 + [((2, deep), F32)],
        [
            pltpu.VMEM((3, rows + 2 * PITCH, wide), BF16),
            pltpu.VMEM((9, wide, rows), BF16),
            pltpu.VMEM((deep, rows), F32),
            pltpu.VMEM((rows, 512), F32),
        ],
        18 * rows * deep * wide,
        at,
        upstream,
        slope,
        steep,
        weights,
    )
def joined_kernel(
    count_ref, at_ref, own_ref, near_ref, far_ref, pre_ref, base_ref, sums_ref, gain_ref, bias_ref, inside_ref, back_ref,
    w_ref, low_ref, low_sums, low_gain, low_bias,
    d_joined_ref, c0, c1, c2, c3, d_norm_ref, out_sums, d_pre_ref,
):
    count = count_ref[0]
    mean, inverse = moments(sums_ref, count)
    inside = inside_ref[...]
    for c in range(4):
        columns = slice(c * 512, (c + 1) * 512)
        centred = (pre_ref[:, columns].astype(F32) - mean[:, columns]) * inverse[:, columns]
        gain = gain_ref[:, columns]
        joined = gain * centred + bias_ref[:, columns] + base_ref[:, columns].astype(F32)
        d_trunk = (
            own_ref[:, columns].astype(F32)
            + near_ref[:, columns].astype(F32)
            + far_ref[:, columns].astype(F32)
        )
        d_joined = gelu_slope(joined) * d_trunk * inside
        d_joined_ref[:, columns] = d_joined.astype(BF16)
        shift = (back_ref[1:2, columns] + centred * back_ref[0:1, columns]) / count
        d_pre_ref[:, columns] = (
            inside * gain * inverse[:, columns] * (d_joined - shift)
        ).astype(BF16)
    for k, part_ref in enumerate((c0, c1, c2, c3)):
        first = pl.multiple_of(at_ref[k] // (2 * PITCH) * 512, 512)
        part_ref[...] = d_pre_ref[:, pl.ds(first, 512)]
    d_act = times_turned(d_pre_ref[...], w_ref[...])
    mean, inverse = moments(low_sums, count)
    centred = (low_ref[...].astype(F32) - mean) * inverse
    upstream = gelu_slope(low_gain[...] * centred + low_bias[...]) * d_act * inside
    upstream = upstream.astype(BF16)
    d_norm_ref[...] = upstream
    upstream = upstream.astype(F32)
    store_sums(out_sums, upstream * centred, upstream)


def joined_back(count, at, pieces, pre, base, sums, gain, bias, inside, back, weights, low, low_sums, low_gain, low_bias):
    rows, deep = pre.shape
    narrow = low.shape[1]
    operands = (*pieces, pre, base, sums, gain, bias, inside, back)
    lower = (low, low_sums, low_gain, low_bias)
    out_d_joined, *columns, out_d_norm, out_sums = call(
        joined_kernel,
        (1,),
        [SCALARS, SCALARS]
        + [whole(a.shape) for a in pieces]
        + [whole(pre.shape)] * 2
        + [whole(a.shape) for a in operands[5:]]
        + [whole((narrow, deep))]
        + [whole(a.shape) for a in lower],
        [kept((rows, deep))] + [kept((rows, 512))] * 4 + [kept((rows, narrow)), kept((2, narrow))],
        [((rows, deep), BF16)]
        + [((rows, 512), BF16)] * 4
        + [((rows, narrow), BF16), ((2, narrow), F32)],
        [pltpu.VMEM((rows, deep), BF16)],
        2 * rows * deep * narrow,
        count,
        at,
        *operands,
        weights,
        *lower,
    )
    return out_d_joined, columns, out_d_norm, out_sums


def dilated_back_kernel(
    count_ref, at_ref, u0, u1, u2, u3, value_ref, sums_ref, back_ref, gain_ref, inside_ref,
    w_ref, low_ref, low_sums, low_gain, low_bias,
    d_norm_ref, out_sums, part_ref,
    image_ref, stack_ref, turned_ref, total_ref,
):
    tap = pl.program_id(0)
    strip = 2 * PITCH
    rows = value_ref.shape[0]
    count = count_ref[0]

    @pl.when(tap == 0)
    def _():
        clear_image(image_ref)
        mean, inverse = moments(sums_ref, count)
        for k, up in enumerate((u0, u1, u2, u3)):
            start = pl.multiple_of(at_ref[k], 16)
            centred = (value_ref[pl.ds(start, strip), :].astype(F32) - mean) * inverse
            shift = (back_ref[1:2, :] + centred * back_ref[0:1, :]) / count
            scale = inside_ref[pl.ds(start, strip), :] * (gain_ref[...] * inverse)
            lowered = (scale * (up[...].astype(F32) - shift)).astype(BF16)
            image_ref[pl.ds(pl.multiple_of(start + strip, 16), strip), :] = lowered
        window_moved(stack_ref, image_ref, 0, 12)
        mine = pl.multiple_of(at_ref[0] // strip * 128, 128)
        part_ref[...] = image_ref[strip : 5 * strip, pl.ds(mine, 128)]
        for k in range(9):
            start = (2 - k // 3) * strip
            turned_ref[k] = stack_ref[2 - k % 3, start : start + rows, :].T
        total_ref[...] = jnp.zeros_like(total_ref)

    total_ref[...] += jnp.dot(w_ref[...], turned_ref[tap], preferred_element_type=F32)

    @pl.when(tap == 8)
    def _():
        mean, inverse = moments(low_sums, count)
        centred = (low_ref[...].astype(F32) - mean) * inverse
        slope = gelu_slope(low_gain[...] * centred + low_bias[...])
        upstream = (slope * total_ref[...].T * inside_ref[...]).astype(BF16)
        d_norm_ref[...] = upstream
        upstream = upstream.astype(F32)
        store_sums(out_sums, upstream * centred, upstream)


def dilated_back(
    count, at, ups, value, sums, back, gain, inside, weights, first_block, low, low_sums, low_gain, low_bias
):
    rows, wide = value.shape
    strip = 2 * PITCH
    operands = (*ups, value, sums, back, gain, inside)
    lower = (low, low_sums, low_gain, low_bias)
    return call(
        dilated_back_kernel,
        (9,),
        [SCALARS, SCALARS]
        + [whole(a.shape) for a in operands]
        + [pl.BlockSpec((512, wide), lambda t: (0, first_block + t))]
        + [whole(a.shape) for a in lower],
        [kept((rows, 512)), kept((2, 512)), kept((rows, 128))],
        [((rows, 512), BF16), ((2, 512), F32), ((rows, 128), BF16)],
        [
            pltpu.VMEM((rows + 2 * strip, wide), BF16),
            pltpu.VMEM((3, rows + 2 * strip, wide), BF16),
            pltpu.VMEM((9, wide, rows), BF16),
            pltpu.VMEM((512, rows), F32),
        ],
        18 * rows * wide * 512,
        count,
        at,
        *operands,
        weights,
        *lower,
    )


def heads_kernel(at_ref, local_ref, *refs):
    *pieces, got_ref = refs[:5]
    outs = refs[5:]

    def put(k, value):
        first = 0
        for out_ref in outs:
            last = first + out_ref.shape[2]
            out_ref[at_ref[k]] = value[:, first:last].astype(F32)
            first = last

    @pl.when(local_ref[0] == 1)
    def _():
        for k, piece in enumerate(pieces):
            put(k, piece)

    @pl.when(local_ref[0] == 0)
    def _():
        for k in range(4):
            put(k, got_ref.at[k])


def heads_placed(at, local, pieces, got, widths):
    rows, deep = pieces[0].shape
    return call(
        heads_kernel,
        (1,),
        [SCALARS, SCALARS] + [whole((rows, deep))] * 4 + [whole((4, rows, deep))],
        [whole((4, rows, wide)) for wide in widths],
        [((4, rows, wide), F32) for wide in widths],
        [],
        0,
        at,
        local,
        *pieces,
        got,
    )


def sums_of(value):
    return jnp.stack([jnp.sum(value, axis=0), jnp.sum(value * value, axis=0)])


def centred_by(value, sums, count):
    mean = sums[0] / count
    inverse = lax.rsqrt(sums[1] / count - mean * mean + EPS)
    return (value.astype(F32) - mean) * inverse, inverse


def norm_back(upstream, value, sums, gain, inside, back, count):
    centred, inverse = centred_by(value, sums, count)
    return (
        inside * gain * inverse * (upstream.astype(F32) - (back[1] + centred * back[0]) / count)
    ).astype(BF16)


def turned_dot(first, second):
    return lax.dot_general(first, second, (((0,), (0,)), ((), ())), preferred_element_type=F32)


def strips_of(value):
    _, rows, across, deep = value.shape
    padded = jnp.pad(value[0], ((0, 0), (0, PITCH - across), (0, 0)))
    return padded.reshape(rows * PITCH, deep)


def maps_of(value, across):
    rows = value.shape[0] // PITCH
    return value.reshape(1, rows, PITCH, -1)[:, :, :across]


def shares_sent(value, axes):
    count = lax.axis_size(axes)
    return lax.all_to_all(
        value.reshape(count, value.shape[0] // count, value.shape[1]), axes, 0, 0
    )


def parts_summed(parts):
    return jnp.sum(parts.astype(F32), axis=0).astype(BF16)


def shards(
    features,
    image_size,
    reduce_weight,
    dilated_weight,
    expand_weight,
    head_weight,
    message_weight,
    gate_weight,
    bottleneck_gain,
    bottleneck_bias,
    expand_gain,
    expand_bias,
    head_gain,
    head_bias,
    depth_cotangent,
    seg_cotangent,
):
    ylo, core, yhi = (lax.axis_index(a) for a in ("ylo", "core", "yhi"))
    plane = lax.axis_index("x") * 4 + lax.axis_index("z")
    y = yhi * 2 + ylo
    strip = ylo * 2 + core
    width = features.shape[2]
    local = core == yhi

    count = jnp.sum(image_size[:, 0].astype(F32) * image_size[:, 1].astype(F32))
    count_here = count.reshape(1)

    def inside_of(sizes, image, first, rows):
        size = lax.dynamic_index_in_dim(sizes, image, 0, keepdims=False)
        at = jnp.arange(rows * PITCH, dtype=jnp.int32)
        valid = (first + at // PITCH < size[0]) & (at % PITCH < size[1])
        return valid.astype(F32)[:, None]

    length = 2 * PITCH
    head_at = (
        jnp.stack(
            [
                ylo * 2 + core,
                (1 - ylo) * 2 + core,
                ylo * 2 + 1 - core,
                (1 - ylo) * 2 + 1 - core,
            ]
        )
        * length
    ).astype(jnp.int32)
    ring_at = (jnp.stack([y, y ^ 1, y ^ 2, y ^ 3]) * length).astype(jnp.int32)

    group = [(i, i ^ 5) for i in range(8) if (i >> 1) & 1 == i & 1]

    def brought(mine, sent):
        return jnp.where(local, mine, lax.ppermute(sent, GROUP, group))

    def of_head(stacked, head):
        return lax.dynamic_index_in_dim(stacked, head, 0, keepdims=False)

    planes = 16

    deep = features.shape[3]
    same = yhi == core
    inside = inside_of(image_size, plane * 2 + yhi, strip * 2, 2)
    base = strips_of(features) * inside.astype(BF16)
    near, far = beside_y(base)
    channels = expand_weight.shape[0]
    wide_trunk = expand_weight.shape[1] + dilated_weight.shape[1]
    first_weights = jnp.concatenate(
        [expand_weight, dilated_weight, reduce_weight.reshape(channels, -1)], axis=1
    )
    first_part = brought(first_weights, first_weights)
    reduce_part = first_part[:, wide_trunk:].reshape(reduce_weight.shape)
    copies, sizes_first = hold(
        jnp.broadcast_to(reduce_part[None], (planes,) + reduce_part.shape), image_size
    )
    reduce_half = lax.all_to_all(copies, ("x", "z"), 0, 0)
    whole_reduce = jnp.stack(
        in_order(reduce_half, over_core(reduce_half), core), axis=1
    ).reshape(-1, reduce_weight.shape[1])
    whole_trunk = lax.all_gather(first_part[:, :wide_trunk], POOL, axis=0, tiled=True)
    first_tap = expand_weight.shape[1] // 512
    inside_whole = inside_of(sizes_first, plane * 2 + core, 0, 8)

    def spread(own, near, across_low, across_high, far):
        mine = jnp.concatenate([own, near])
        other = jnp.concatenate([across_low, across_high, far])
        return jnp.where(same, mine, other), over_core(jnp.where(same, other, mine))

    near, far, y_first = hold(near, far, y)
    head_part = brought(of_head(head_weight, y_first), of_head(head_weight, y_first ^ 3))
    base_keep, base_got = spread(base, near, *across_y(near, far), far)
    whole_reduce, base_keep, base_got, inside_whole, head_part = hold(
        whole_reduce, base_keep, base_got, inside_whole, head_part
    )
    whole_head = lax.all_gather(head_part, POOL, axis=0, tiled=True)

    pre_one = jnp.concatenate(
        [
            jnp.dot(a, whole_reduce, preferred_element_type=F32).astype(BF16)
            for a in (base_keep, base_got)
        ]
    )
    sums_one = fold(sums_of(pre_one.astype(F32)), CORE, *LINE, *PLANE)
    pre_two, sums_two, act_one_image, pre_one_image = dilated_forward(
        count_here,
        head_at,
        pre_one,
        sums_one,
        bottleneck_gain[:1],
        bottleneck_bias[:1],
        inside_whole,
        whole_trunk,
        first_tap,
    )
    sums_two = fold(sums_two, CORE, *LINE)
    sums_two, y_later, depth_cots, seg_cots = hold(sums_two, y, depth_cotangent, seg_cotangent)
    task_weights = jnp.concatenate([message_weight, gate_weight], axis=2)
    task_part = brought(of_head(task_weights, y_later), of_head(task_weights, y_later ^ 3))
    cots = jnp.concatenate([strips_of(depth_cots), strips_of(seg_cots)], axis=1)
    near, far = beside_y(cots)
    sums_two = fold(sums_two, *PLANE)
    act_two, pre_three, sums_three = expand_forward(
        count_here,
        pre_two,
        sums_two,
        bottleneck_gain[1:],
        bottleneck_bias[1:],
        inside_whole,
        whole_trunk,
    )
    sums_three, task_part = hold(fold(sums_three, CORE, *LINE), task_part)
    whole_task = lax.all_gather(task_part, POOL, axis=0, tiled=True)
    sums_three = fold(sums_three, *PLANE)

    gain_here, bias_here = of_head(head_gain, y)[None], of_head(head_bias, y)[None]
    wide_gain, wide_bias = expand_gain[None], expand_bias[None]
    trunk, slope, steep, base_image, trunk_turned = trunk_forward(
        count_here,
        head_at,
        pre_three,
        base_keep,
        base_got,
        sums_three,
        wide_gain,
        wide_bias,
        inside_whole,
    )
    trunk, near, far = hold(trunk, near, far)
    across_low, across_high = across_y(near, far)
    pre_head, sums_head = head_forward(trunk, inside_whole, whole_head)
    sums_head, near, far, across_low, across_high = hold(
        sums_head, near, far, across_low, across_high
    )
    cots_keep, cots_got = spread(cots, near, across_low, across_high, far)
    sums_head = fold(sums_head, CORE, *LINE, *PLANE)
    task, *streams, d_message, d_logit, d_norm_head, back_here = message_stage(
        count_here,
        head_at,
        ring_at,
        y.astype(jnp.int32).reshape(1),
        pre_head,
        sums_head,
        gain_here,
        bias_here,
        inside_whole,
        whole_task,
        cots_keep,
        cots_got,
    )
    back_head = fold(back_here, CORE, *LINE, *PLANE)
    back_head, streams = hold(back_head, streams)
    d_pre_head = norm_back(
        d_norm_head, pre_head, sums_head, gain_here, inside_whole, back_head, count
    )
    own, near, across, far = streams
    from_near, from_far = half_way(across)
    head_grad = conv_weight(trunk_turned, d_pre_head, 1, is_turned=True)
    head_grad, d_pre_head, from_near, from_far = hold(head_grad, d_pre_head, from_near, from_far)
    head_share = lax.psum_scatter(head_grad, POOL, scatter_dimension=0, tiled=True)
    streams = last_way(own, near, far, from_near, from_far)
    *d_trunk, back_three = trunk_back(ring_at, d_pre_head, slope, steep, whole_head)
    d_trunk, back_three, streams = hold(d_trunk, back_three, streams)
    placed = jnp.where(
        jnp.arange(4)[None, :, None] == y, back_here[:, None], jnp.zeros((1, 1, 1), F32)
    ).reshape(2, -1)
    back_wide = jnp.concatenate([back_three, placed], axis=1)
    own, near, across, far = d_trunk
    from_near, from_far = half_way(across)
    back_wide, from_near, from_far = hold(fold(back_wide, CORE, *LINE), from_near, from_far)
    pieces = last_way(own, near, far, from_near, from_far)
    back_wide = fold(back_wide, *PLANE)
    def strip_of(value):
        return lax.dynamic_slice_in_dim(value, y * length, length, 0)

    pre_two_strip, pre_three_strip, base_strip, inside_strip = (
        strip_of(a) for a in (pre_two, pre_three, base_image, inside_whole)
    )

    def ring_order(value):
        return jnp.concatenate(
            [
                lax.dynamic_slice_in_dim(value, (y ^ flip) * length, length, 0)
                for flip in range(4)
            ]
        )

    act_two_ring = ring_order(act_two)
    task_grad = conv_weight(task, d_message, 1, (d_logit,))
    (
        back_wide,
        pieces,
        pre_two_strip,
        pre_three_strip,
        base_strip,
        inside_strip,
        act_two_ring,
        task_grad,
    ) = hold(
        back_wide,
        pieces,
        pre_two_strip,
        pre_three_strip,
        base_strip,
        inside_strip,
        act_two_ring,
        task_grad,
    )
    task_share = lax.psum_scatter(task_grad, POOL, scatter_dimension=0, tiled=True)
    back_wide = fold(back_wide, *RIDGE)
    back_three, back_heads = back_wide[:, :deep], back_wide[:, deep:]
    d_joined, d_three_parts, d_norm_two, back_two = joined_back(
        count_here,
        ring_at,
        pieces,
        pre_three_strip,
        base_strip,
        sums_three,
        wide_gain,
        wide_bias,
        inside_strip,
        back_three,
        whole_trunk,
        pre_two_strip,
        sums_two,
        bottleneck_gain[1:],
        bottleneck_bias[1:],
    )
    back_two = fold(back_two, CORE, *LINE)
    back_two, d_norm_twos = hold(back_two, around_y(d_norm_two))
    back_two = fold(back_two, *PLANE, *RIDGE)

    d_three_part = jnp.concatenate(for_me(d_three_parts))
    grad_expand = turned_dot(act_two_ring, d_three_part).astype(BF16)
    back_two, grad_expand, d_joined = hold(back_two, grad_expand, d_joined)
    homeward = sent_home(
        jnp.concatenate([d_joined, sum(a.astype(F32) for a in streams).astype(BF16)], axis=1)
    )
    d_norm_one, back_one, d_two_part = dilated_back(
        count_here,
        ring_at,
        d_norm_twos,
        pre_two,
        sums_two,
        back_two,
        bottleneck_gain[1:],
        inside_whole,
        whole_trunk,
        first_tap,
        pre_one_image,
        sums_one,
        bottleneck_gain[:1],
        bottleneck_bias[:1],
    )
    def to_chips(share):
        pieces = [share]
        for flip in (1, 2, 3):
            pairs = []
            for i in range(8):
                low, c, high = i >> 2, (i >> 1) & 1, i & 1
                to = (high * 2 + low) ^ flip
                if to >> 1 == c:
                    pairs.append((i, ((to & 1) << 2) | (c << 1) | (to >> 1)))
            pieces.append(lax.ppermute(share, GROUP, pairs))
        return tuple(pieces)

    heads_at = jnp.stack([y, y ^ 1, y ^ 2, y ^ 3]).astype(jnp.int32)
    local_here = local.astype(jnp.int32).reshape(1)

    def to_cores(pieces, *widths):
        pairs = [(i, i ^ 2) for i in range(8) if (i >> 1) & 1 == i & 1]
        got = lax.ppermute(jnp.stack(pieces), GROUP, pairs)
        return heads_placed(heads_at, local_here, pieces, got, widths)

    back_one = fold(back_one, CORE, *LINE)
    grad_dilated = conv_weight(act_one_image, d_two_part, 2)
    trunk_grad = jnp.concatenate([grad_expand, grad_dilated], axis=1)
    back_one, trunk_grad, homeward, head_share = hold(back_one, trunk_grad, homeward, head_share)
    head_pieces = to_chips(head_share)
    back_one = fold(back_one, *PLANE)
    d_pre_one = norm_back(
        d_norm_one, pre_one_image, sums_one, bottleneck_gain[0], inside_whole, back_one, count
    )
    grad_reduce = turned_dot(
        base_image, lax.dynamic_slice_in_dim(d_pre_one, y * 128, 128, 1)
    ).astype(BF16)
    trunk_grad = jnp.concatenate(
        [trunk_grad, grad_reduce.reshape(trunk_grad.shape[0], -1)], axis=1
    )
    trunk_grad, d_pre_one = hold(trunk_grad, d_pre_one)
    trunk_parts = shares_sent(trunk_grad, POOL)
    wide = message_weight.shape[2]
    (sum_head,) = to_cores(head_pieces, wide)
    d_pre_one = sent_home(strip_of(d_pre_one))
    d_base = homeward[:, :deep].astype(F32) + times_turned(d_pre_one, whole_reduce)
    input_grad = maps_of(d_base * inside, width)
    trunk_parts, sum_head, input_grad, task_share = hold(
        trunk_parts, sum_head, input_grad, task_share
    )
    small_share = jnp.concatenate([task_share, parts_summed(trunk_parts)], axis=1)
    sum_message, sum_gate, all_trunk, all_reduce = to_cores(
        to_chips(small_share), wide, gate_weight.shape[2], trunk_grad.shape[1] - 512, 512
    )
    sum_expand = jnp.moveaxis(all_trunk[:, :, :512], 0, 1).reshape(channels, -1)
    sum_dilated = jnp.moveaxis(
        all_trunk[:, :, 512:].reshape(4, channels, 9, 128), 0, 2
    ).reshape(channels, -1)
    sum_reduce = jnp.moveaxis(all_reduce.reshape(4, -1, 128), 0, 1).reshape(-1, 512)


    streams = maps_of(homeward[:, deep:].astype(F32) * inside, width)
    depth_out, seg_out = jnp.split(streams, 2, axis=3)

    return (
        depth_out,
        seg_out,
        input_grad,
        sum_reduce,
        sum_dilated,
        sum_expand,
        sum_head,
        sum_message,
        sum_gate,
        jnp.stack([back_one[0], back_two[0]]),
        jnp.stack([back_one[1], back_two[1]]),
        back_three[0],
        back_three[1],
        back_heads[0].reshape(4, -1),
        back_heads[1].reshape(4, -1),
    )


def solution(mesh):
    fine = Mesh(mesh.devices.reshape(2, 2, 4, 4, 2), FINE)
    maps = P(IMG, ROWS, None, None)
    placed = (
        maps,
        P(),
        P(IMG, None),
        P(IMG, None),
        P(IMG, None),
        P(None, IMG, None),
        P(None, IMG, None),
        P(None, IMG, None),
        P(),
        P(),
        P(),
        P(),
        P(),
        P(),
        maps,
        maps,
    )
    return jax.shard_map(
        shards,
        mesh=fine,
        in_specs=placed,
        out_specs=(
            maps,
            maps,
            maps,
            P(IMG, None),
            P(IMG, None),
            P(IMG, None),
            P(None, IMG, None),
            P(None, IMG, None),
            P(None, IMG, None),
            P(),
            P(),
            P(),
            P(),
            P(),
            P(),
        ),
        check_vma=False,
    )
```
